256 devices in a mesh: gx: 32 (over y, x, core), gy: 8 (over z).
Axes of the slice: x: 4, y: 4, z: 8, core: 2. Of those that a mesh axis runs over, the one named last changes fastest.
Arguments:
- right_side: float32 [64, 32, 8192], P(None, 'gy', 'gx'), may hold values from -10 to 10
- start_pressure: float32 [64, 32, 8192], P(None, 'gy', 'gx'), may hold values from -1.5 to 1.5
- conductance: float32 [3, 64, 32, 8192], P(None, None, 'gy', 'gx'), may hold values from 0.3 to 3
- inverses: float32 [32, 64, 64, 256], P('gx'), may hold values from -0.05 to 1.6, as said below
Outputs:
- pressure: float32 [64, 32, 8192], P(None, 'gy', 'gx')
- residual: float32 [64, 32, 8192], P(None, 'gy', 'gx')
- direction: float32 [64, 32, 8192], P(None, 'gy', 'gx')
The draws below stay inside these ranges and needn't reach their ends.
Inputs may be any that keep to these rules, and one draw needn't show every extreme that they name: Each block inverses[r, :, :, b] is symmetric with a dominant positive diagonal.
All inputs are finite; a program needn't handle non-finite values.
Results may differ from the reference program's by a relative error of at most 0.00026.
Values sent between devices are 32-bit elements; how exact they have to be, the bound alone decides.
No kernel may reach another device: no remote copies, remote signals or barrier semaphores. Data moves between devices by JAX's collectives and lax.ppermute only.
A program may use at most 128 MiB of HBM per device.

```python
import math
import jax
import jax.numpy as jnp
import numpy as np
from jax import lax

NZ = 64
CX = 256
NX = 8192
NY = 32
RESIDUES = 32


def draw_right_side(key, part):
    key = jax.random.fold_in(key, 11)
    across = jnp.arange(NX, dtype=jnp.float32) / NX
    downward = jnp.arange(NY, dtype=jnp.float32) / NY
    scaling = 0.4 * (1.0 + 2.0 * across)[None, None, :] * (1.0 + downward)[None, :, None]
    noise = jnp.clip(jax.random.normal(key, (NZ, NY, NX), jnp.float32), -4.0, 4.0)
    return (noise * scaling).astype(jnp.float32)


def draw_inverses(key, part):
    key = jax.random.fold_in(key, 23)
    key_diag, key_off = jax.random.split(key)
    diagonal = jax.random.uniform(key_diag, (RESIDUES, NZ, CX), jnp.float32, 1.0, 1.6)
    scatter = jax.random.uniform(key_off, (RESIDUES, NZ, NZ, CX), jnp.float32, -1.0, 1.0) * (0.95 / (NZ - 1))
    symmetric = 0.5 * (scatter + jnp.swapaxes(scatter, 1, 2))
    identity = (jnp.arange(NZ)[:, None] == jnp.arange(NZ)[None, :]).astype(jnp.float32)
    result = symmetric * (1.0 - identity)[None, :, :, None] + identity[None, :, :, None] * diagonal[:, :, None, :]
    return result.astype(jnp.float32)


def block_scale(key, dims, shards, smallest, top_value):
    level, own = 1.0, jax.random.fold_in(key, 6)
    for position, shards_of in shards:
        heights = jnp.exp(jax.random.uniform(jax.random.fold_in(own, position), (shards_of,), jnp.float32, smallest / len(shards), top_value / len(shards)))
        level = level * jnp.repeat(heights, dims[position] // shards_of).reshape([-1 if axis == position else 1 for axis in range(len(dims))])
    return level


def scatter_about(key, dims, scale, bound, pieces=(), kind=jnp.bfloat16):
    values = scale * jax.random.normal(key, dims, jnp.float32)
    if pieces:
        values = values * block_scale(key, dims, pieces, -0.22, 0.18)
    return jnp.clip(values, -bound, bound).astype(kind)


def setup_inputs(seed: int = 0) -> dict:
    streams_of = jax.random.split(jax.random.key(seed), 5)
    return {
        "right_side": draw_right_side(jax.random.fold_in(streams_of[4], 71), 0),
        "start_pressure": scatter_about(streams_of[1], (NZ, NY, NX), 0.1, 1.5, ((1, 8), (2, 32)), jnp.float32),
        "conductance": jnp.clip(jnp.exp(math.log(3.0) - 2.3025851 * jax.random.uniform(streams_of[2], (3, NZ, NY, NX), jnp.float32) ** block_scale(streams_of[2], (3, NZ, NY, NX), ((2, 8), (3, 32)), -0.2, 0.2)), 0.3, 3.0),
        "inverses": draw_inverses(jax.random.fold_in(streams_of[4], 71), 0),
    }


def reversed_order(group_size):
    levels = group_size.bit_length() - 1
    entries = []
    for number in range(group_size):
        reversed_value = 0
        for bit_digit in range(levels):
            reversed_value = reversed_value | (((number >> bit_digit) & 1) << (levels - 1 - bit_digit))
        entries.append(reversed_value)
    return np.array(entries, dtype=np.int32)


def operate(values_in, conductance):
    along_x, along_y, along_z = conductance[0], conductance[1], conductance[2]
    lower_rows = (jnp.arange(NY) != 0).astype(values_in.dtype)[None, :, None]
    upper_rows = (jnp.arange(NY) != NY - 1).astype(values_in.dtype)[None, :, None]
    lower_planes = (jnp.arange(NZ) != 0).astype(values_in.dtype)[:, None, None]
    upper_planes = (jnp.arange(NZ) != NZ - 1).astype(values_in.dtype)[:, None, None]
    behind_x = jnp.roll(values_in, 1, axis=2)
    before_x = jnp.roll(values_in, -1, axis=2)
    behind_y = jnp.roll(values_in, 1, axis=1) * lower_rows
    before_y = jnp.roll(values_in, -1, axis=1) * upper_rows
    behind_z = jnp.roll(values_in, 1, axis=0) * lower_planes
    before_z = jnp.roll(values_in, -1, axis=0) * upper_planes
    result_x = along_x * (values_in - behind_x) + jnp.roll(along_x, -1, axis=2) * (values_in - before_x)
    result_y = along_y * (values_in - behind_y) + jnp.roll(along_y, -1, axis=1) * (values_in - before_y)
    result_z = along_z * (values_in - behind_z) + jnp.roll(along_z, -1, axis=0) * (values_in - before_z)
    return result_x + result_y + result_z


def precondition(values_in, inverses):
    spectrum = jnp.fft.fft(values_in, axis=2)
    ordered = inverses[reversed_order(RESIDUES)]

    def solve(component):
        grouped = component.reshape(NZ, NY, CX, RESIDUES)
        solved = jnp.einsum("awzb,zyba->wyba", ordered, grouped, precision=lax.Precision.HIGHEST)
        return solved.reshape(NZ, NY, NX)

    real_part = solve(jnp.real(spectrum))
    imag_part = solve(jnp.imag(spectrum))
    return jnp.real(jnp.fft.ifft(real_part + 1j * imag_part, axis=2))


def reference(right_side, start_pressure, conductance, inverses):
    residual_start = right_side - operate(start_pressure, conductance)
    precond_start = precondition(residual_start, inverses)
    first_dot = jnp.sum(residual_start * precond_start)
    image_field = operate(precond_start, conductance)
    curvature = jnp.sum(precond_start * image_field)
    step_length = first_dot / curvature
    pressure = start_pressure + step_length * precond_start
    residual = residual_start - step_length * image_field
    precond_next = precondition(residual, inverses)
    second_dot = jnp.sum(residual * precond_next)
    direction = precond_next + (second_dot / first_dot) * precond_start
    return pressure, residual, direction
```

```python
import functools
import math

import jax
import jax.numpy as jnp
import numpy as np
from jax import lax
from jax.experimental import pallas as pl
from jax.experimental.pallas import tpu as pltpu
from jax.sharding import PartitionSpec as P

NZ = 64
ROWS = 4
CELLS = 256
GROUP = 32
COLS = 8
LENGTH = CELLS * GROUP
PLANE = ROWS * NZ
HALF = 128

f32 = jnp.float32
bf16 = jnp.bfloat16


def reverse_bits(number):
    return int(f"{number:05b}"[::-1], 2)


def column_tables():
    residue = np.array([reverse_bits(i) for i in range(GROUP)])
    angle = 2.0 * np.pi * np.outer(residue, np.arange(GROUP)) / GROUP
    same = np.eye(COLS)

    def table(real_row, imag_row):
        pair = np.stack([real_row, imag_row], axis=1)
        full = pair[:, :, None, :, None] * same[None, None, :, None, :]
        return full.reshape(GROUP * 2 * COLS, CELLS).astype(np.float32)

    cosine, sine = np.cos(angle), np.sin(angle)
    return table(cosine, -sine), table(-sine, -cosine)


def wave_table():
    angle = 2.0 * np.pi * np.outer(np.arange(CELLS), np.arange(CELLS)) / CELLS
    cosine, sine = np.cos(angle), np.sin(angle)
    real_rows = np.concatenate([cosine, -sine], axis=1).reshape(GROUP, 1, COLS, 2 * CELLS)
    imag_rows = np.concatenate([sine, cosine], axis=1).reshape(GROUP, 1, COLS, 2 * CELLS)
    full = np.concatenate([real_rows, imag_rows], axis=1).reshape(2 * CELLS, 2 * CELLS)
    full = full.astype(np.float32)
    high = full.astype(jnp.bfloat16)
    low = (full - high.astype(np.float32)).astype(jnp.bfloat16)
    return high, low


def split(values):
    high = values.astype(bf16)
    return high, (values - high.astype(f32)).astype(bf16)


def products(left, right, contract):
    dims = (contract, ((), ()))
    (left_high, left_low), (right_high, right_low) = left, right

    def one(a, b):
        return lax.dot_general(a, b, dims, preferred_element_type=f32)

    return one(left_high, right_high) + (one(left_high, right_low) + one(left_low, right_high))


def lanes_of(shape):
    return lax.broadcasted_iota(jnp.int32, shape, 1)


def roll_half(tile):
    return pltpu.roll(tile, 64, 1)


def low_row_packed(field):
    tile = field[:, :HALF]
    lane = lanes_of((HALF, HALF))
    return jnp.where(lane < 64, tile[:HALF], roll_half(tile[HALF:]))


def high_row_packed(field):
    tile = field[:, HALF:]
    lane = lanes_of((HALF, HALF))
    return jnp.where(lane < 64, roll_half(tile[:HALF]), tile[HALF:])


def behind_rows(field, halo):
    first, second = field[:, :HALF], field[:, HALF:]
    turned, turned_second = roll_half(first), roll_half(second)
    lane = lanes_of(first.shape)
    return jnp.concatenate(
        [jnp.where(lane < 64, halo, turned), jnp.where(lane < 64, turned, turned_second)], axis=1
    )


def before_rows(field, halo):
    first, second = field[:, :HALF], field[:, HALF:]
    turned, turned_second = roll_half(first), roll_half(second)
    lane = lanes_of(first.shape)
    return jnp.concatenate(
        [jnp.where(lane < 64, turned, turned_second), jnp.where(lane < 64, turned_second, halo)], axis=1
    )


def operate(centre, x_pair, y_pair, along, ahead_x, ahead_y):
    along_x, along_y, along_z = along
    plane = lanes_of(centre.shape) % NZ
    first, last = plane == 0, plane == NZ - 1
    ahead_z = jnp.where(last, pltpu.roll(along_z, NZ - 1, 1), pltpu.roll(along_z, PLANE - 1, 1))
    behind_z = jnp.where(first, 0.0, pltpu.roll(centre, 1, 1))
    before_z = jnp.where(last, 0.0, pltpu.roll(centre, PLANE - 1, 1))
    result_x = along_x * (centre - x_pair[0]) + ahead_x * (centre - x_pair[1])
    result_y = along_y * (centre - y_pair[0]) + ahead_y * (centre - y_pair[1])
    result_z = along_z * (centre - behind_z) + ahead_z * (centre - before_z)
    return result_x + result_y + result_z


def turned(ref, lead=()):
    rows = [ref[lead + (slice(None), y, slice(None))] for y in range(ROWS)]
    return jnp.concatenate(rows, axis=0).T


def entry_kernel(place, right_ref, start_ref, cond_ref, left_ref, next_ref, under_ref, over_ref, chunk_ref, residual_ref):
    start = turned(start_ref)
    along = [turned(cond_ref, (axis,)) for axis in range(3)]
    row = lax.broadcasted_iota(jnp.int32, (CELLS, PLANE), 0)
    behind_x = jnp.where(row == 0, left_ref[0:1], pltpu.roll(start, 1, 0))
    before_x = jnp.where(row == CELLS - 1, next_ref[0:1], pltpu.roll(start, CELLS - 1, 0))
    ahead_x = jnp.where(row == CELLS - 1, next_ref[1:2], pltpu.roll(along[0], CELLS - 1, 0))
    under = under_ref[...]
    over = over_ref[...]
    under_t = jnp.concatenate([under, under], axis=0).T
    over_t = jnp.concatenate([over[:NZ], over[:NZ]], axis=0).T
    ahead_t = jnp.concatenate([over[NZ:], over[NZ:]], axis=0).T
    under_t = jnp.where(place[1] == 0, 0.0, under_t)
    over_t = jnp.where(place[1] == place[3] - 1, 0.0, over_t)
    behind_y = behind_rows(start, under_t)
    before_y = before_rows(start, over_t)
    ahead_y = before_rows(along[1], ahead_t)
    image = operate(start, (behind_x, before_x), (behind_y, before_y), along, ahead_x, ahead_y)
    residual = turned(right_ref) - image
    residual_ref[...] = residual
    chunk_ref[:, 0:COLS, :] = residual.reshape(GROUP, COLS, PLANE)
    for axis in range(3):
        low = COLS * (axis + 1)
        chunk_ref[:, low : low + COLS, :] = along[axis].reshape(GROUP, COLS, PLANE)


def table_kernel(cosine_ref, sine_ref, turn_ref, high_ref, low_ref):
    turn = turn_ref[...]
    table = cosine_ref[...] * turn[:, 0:1] + sine_ref[...] * turn[:, 1:2]
    high_ref[...], low_ref[...] = split(table)


def spread_kernel(chunk_ref, high_ref, low_ref, out_ref):
    field = chunk_ref[:, 0:COLS, :].reshape(CELLS, PLANE)
    table = (high_ref[...], low_ref[...])
    out_ref[...] = products(table, split(field), ((1,), (0,))).reshape(GROUP, 2 * COLS, PLANE)


def solve_kernel(which, parts_ref, inverse_ref, high_ref, low_ref, dots_ref, out_ref, sums_ref, wave, solved):
    table = (high_ref[...], low_ref[...])
    parts = parts_ref[...].reshape(2 * CELLS, PLANE).T
    wave[...] = products(split(parts), table, ((1,), (0,)))
    total = jnp.zeros((8, HALF), f32)
    for half in range(2):
        for pair in range(2):
            places = [(2 * pair + y, part * CELLS + half * HALF) for y in range(2) for part in range(2)]

            def step(group, sums):
                tiles = [
                    wave[pl.ds(pl.multiple_of(y * NZ + group * 8, 8), 8), lane : lane + HALF] for y, lane in places
                ]
                for z in range(8):
                    block = inverse_ref[group * 8 + z, :, half * HALF : (half + 1) * HALF]
                    sums = tuple(so_far + block * tile[z : z + 1] for so_far, tile in zip(sums, tiles))
                return sums

            sums = lax.fori_loop(0, NZ // 8, step, tuple(jnp.zeros((NZ, HALF), f32) for _ in places))
            for result, (y, lane) in zip(sums, places):
                solved[y * NZ : (y + 1) * NZ, lane : lane + HALF] = result
                product = result * wave[y * NZ : (y + 1) * NZ, lane : lane + HALF]
                total = total + jnp.sum(product.reshape(NZ // 8, 8, HALF), axis=0)
    row = lax.broadcasted_iota(jnp.int32, (8, HALF), 0)
    sums_ref[...] = dots_ref[...] + jnp.where(row == which, jnp.sum(total, axis=0, keepdims=True) / LENGTH, 0.0)
    out_ref[...] = products(table, split(solved[...]), ((1,), (1,))).reshape(GROUP, 2 * COLS, PLANE)


def gather_field(parts_ref, high_ref, low_ref):
    parts = parts_ref[...].reshape(2 * CELLS, PLANE)
    table = (high_ref[...], low_ref[...])
    return products(table, split(parts), ((0,), (0,))) * (1.0 / LENGTH)


def gather_kernel(parts_ref, high_ref, low_ref, field_ref, edge_low_ref, edge_high_ref, row_low_ref, row_high_ref):
    field = gather_field(parts_ref, high_ref, low_ref)
    field_ref[...] = field
    edges = field.reshape(GROUP, COLS, PLANE)
    edge_low_ref[...] = edges[:, 0, :]
    edge_high_ref[...] = edges[:, COLS - 1, :]
    row_low_ref[...] = low_row_packed(field)
    row_high_ref[...] = high_row_packed(field)


def edge_rows(edge):
    return jnp.broadcast_to(edge[:, None, :], (GROUP, COLS, PLANE)).reshape(CELLS, PLANE)


def image_kernel(
    place,
    field_ref,
    chunk_ref,
    left_ref,
    next_ref,
    under_ref,
    over_ref,
    cond_next_ref,
    cond_over_ref,
    dots_ref,
    high_ref,
    low_ref,
    image_ref,
    parts_ref,
    sums_ref,
):
    field = field_ref[...]
    along = [
        chunk_ref[:, COLS * (axis + 1) : COLS * (axis + 2), :].reshape(CELLS, PLANE) for axis in range(3)
    ]
    column = lax.broadcasted_iota(jnp.int32, (CELLS, PLANE), 0) % COLS
    left, after, cond_after = left_ref[...], next_ref[...], cond_next_ref[...]
    left = jnp.where(place[0] == 0, pltpu.roll(left, 1, 0), left)
    at_end = place[0] == place[2] - 1
    after = jnp.where(at_end, pltpu.roll(after, GROUP - 1, 0), after)
    cond_after = jnp.where(at_end, pltpu.roll(cond_after, GROUP - 1, 0), cond_after)
    behind_x = jnp.where(column == 0, edge_rows(left), pltpu.roll(field, 1, 0))
    before_x = jnp.where(column == COLS - 1, edge_rows(after), pltpu.roll(field, CELLS - 1, 0))
    ahead_x = jnp.where(column == COLS - 1, edge_rows(cond_after), pltpu.roll(along[0], CELLS - 1, 0))
    under, over, cond_over = under_ref[...], over_ref[...], cond_over_ref[...]
    under = jnp.concatenate([under, roll_half(under)], axis=0)
    over = jnp.concatenate([roll_half(over), over], axis=0)
    cond_over = jnp.concatenate([roll_half(cond_over), cond_over], axis=0)
    under = jnp.where(place[1] == 0, 0.0, under)
    over = jnp.where(place[1] == place[3] - 1, 0.0, over)
    behind_y = behind_rows(field, under)
    before_y = before_rows(field, over)
    ahead_y = before_rows(along[1], cond_over)
    image = operate(field, (behind_x, before_x), (behind_y, before_y), along, ahead_x, ahead_y)
    image_ref[...] = image
    table = (high_ref[...], low_ref[...])
    parts_ref[...] = products(table, split(image), ((1,), (0,))).reshape(GROUP, 2 * COLS, PLANE)
    product = field * image
    total = jnp.sum((product[:, :HALF] + product[:, HALF:]), axis=0, keepdims=True)
    row = lax.broadcasted_iota(jnp.int32, (8, HALF), 0)
    sums_ref[...] = dots_ref[...] + jnp.where(row == 1, total, 0.0)


def edges_kernel(chunk_ref, edge_ref, row_ref):
    edge_ref[...] = chunk_ref[:, COLS, :]
    row_ref[...] = low_row_packed(chunk_ref[:, 2 * COLS : 3 * COLS, :].reshape(CELLS, PLANE))


def pack_kernel(parts_ref, high_ref, low_ref, field_ref, image_ref, out_ref):
    out_ref[:, 0:COLS, :] = field_ref[...].reshape(GROUP, COLS, PLANE)
    out_ref[:, COLS : 2 * COLS, :] = image_ref[...].reshape(GROUP, COLS, PLANE)
    latest = gather_field(parts_ref, high_ref, low_ref)
    out_ref[:, 2 * COLS :, :] = latest.reshape(GROUP, COLS, PLANE)


def finish_kernel(packed_ref, start_ref, residual_ref, dots_ref, pressure_out, residual_out, direction_out):
    sums = jnp.sum(dots_ref[...], axis=1, keepdims=True)
    first, curvature, third = sums[0:1], sums[1:2], sums[2:3]
    step = first / curvature
    second = first - 2.0 * step * curvature + step * step * third
    ratio = second / first
    field = packed_ref[:, 0:COLS, :].reshape(CELLS, PLANE)
    image = packed_ref[:, COLS : 2 * COLS, :].reshape(CELLS, PLANE)
    latest = packed_ref[:, 2 * COLS :, :].reshape(CELLS, PLANE)
    change = (step * field).T
    residual = (residual_ref[...] - step * image).T
    direction = ((field - step * latest) + ratio * field).T
    for y in range(ROWS):
        rows = slice(y * NZ, (y + 1) * NZ)
        pressure_out[:, y, :] = start_ref[:, y, :] + change[rows]
        residual_out[:, y, :] = residual[rows]
        direction_out[:, y, :] = direction[rows]


def shape(*dims, dtype=f32):
    return jax.ShapeDtypeStruct(dims, dtype)


def call(kernel, outs, *args, smem=0, scratch=(), cost=0):
    specs = [pl.BlockSpec(memory_space=pltpu.SMEM)] * smem
    specs += [pl.BlockSpec(memory_space=pltpu.VMEM)] * (len(args) - smem)
    many = isinstance(outs, (tuple, list))
    out_spec = pl.BlockSpec(memory_space=pltpu.VMEM)
    return pl.pallas_call(
        kernel,
        out_shape=outs,
        in_specs=specs,
        out_specs=[out_spec] * len(outs) if many else out_spec,
        scratch_shapes=list(scratch),
        compiler_params=pltpu.CompilerParams(vmem_limit_bytes=40 * 1024 * 1024),
        cost_estimate=pl.CostEstimate(flops=cost, bytes_accessed=2**20, transcendentals=0),
    )(*args)


def shift(value, axis, step):
    count = lax.axis_size(axis)
    return lax.ppermute(value, axis, [(i, (i + step) % count) for i in range(count)])


def exchange(parts):
    return lax.all_to_all(parts, "gx", 0, 0, tiled=True)


def all_sum(value):
    for axis in ("gy", "gx"):
        count = lax.axis_size(axis)
        distance = 1
        while distance < count:
            value = value + lax.ppermute(value, axis, [(i, i ^ distance) for i in range(count)])
            distance *= 2
    return value


def shards(right_side, start_pressure, conductance, inverses):
    place = jnp.stack(
        [lax.axis_index("gx"), lax.axis_index("gy"), lax.axis_size("gx"), lax.axis_size("gy")]
    ).astype(jnp.int32)
    field_shape = shape(CELLS, PLANE)
    parts_shape = shape(GROUP, 2 * COLS, PLANE)
    edge_shape, row_shape, dots_shape = shape(GROUP, PLANE), shape(HALF, HALF), shape(8, HALF)

    def column(values):
        return values.T.reshape(1, PLANE)

    along_x, along_y = conductance[0], conductance[1]
    to_left = jnp.concatenate([column(start_pressure[:, :, 0]), column(along_x[:, :, 0])], axis=0)
    to_right = column(start_pressure[:, :, CELLS - 1])
    to_under = jnp.concatenate([start_pressure[:, 0, :], along_y[:, 0, :]], axis=0)
    to_over = start_pressure[:, ROWS - 1, :]
    under = shift(to_over, "gy", 1)
    over = shift(to_under, "gy", -1)
    left = shift(to_right, "gx", 1)
    after = shift(to_left, "gx", -1)

    cosine_table, sine_table = column_tables()
    residues = jnp.asarray([reverse_bits(i) for i in range(GROUP)], jnp.int32)
    columns = lax.axis_index("gx") * COLS + jnp.arange(COLS, dtype=jnp.int32)
    angle = (residues[:, None] * columns[None, :]).astype(f32) * (2.0 * math.pi / LENGTH)
    turn = jnp.stack([jnp.cos(angle), jnp.sin(angle)], axis=-1)
    turn = jnp.broadcast_to(turn[:, None], (GROUP, 2, COLS, 2)).reshape(2 * CELLS, 2)
    table = call(
        table_kernel,
        [shape(2 * CELLS, CELLS, dtype=bf16)] * 2,
        jnp.asarray(cosine_table),
        jnp.asarray(sine_table),
        turn,
    )
    waves = [jnp.asarray(part) for part in wave_table()]
    inverse = inverses.reshape(inverses.shape[1:])

    def solve(which, parts, dots):
        return call(
            functools.partial(solve_kernel, which),
            [parts_shape, dots_shape],
            parts,
            inverse,
            *waves,
            dots,
            scratch=[pltpu.VMEM((PLANE, 2 * CELLS), f32)] * 2,
            cost=2 * 10**9,
        )

    chunk, residual = call(
        entry_kernel,
        [shape(GROUP, 4 * COLS, PLANE), field_shape],
        place,
        right_side,
        start_pressure,
        conductance,
        left,
        after,
        under,
        over,
        smem=1,
    )
    chunk = exchange(chunk)
    parts = exchange(call(spread_kernel, parts_shape, chunk, *table))
    cond_edge, cond_row = call(edges_kernel, [edge_shape, row_shape], chunk)
    cond_after = shift(cond_edge, "gx", -1)
    cond_over = shift(cond_row, "gy", -1)
    parts, dots = solve(0, parts, jnp.zeros((8, HALF), f32))
    parts = exchange(parts)
    field, edge_low, edge_high, row_low, row_high = call(
        gather_kernel, [field_shape, edge_shape, edge_shape, row_shape, row_shape], parts, *table
    )
    under = shift(row_high, "gy", 1)
    over = shift(row_low, "gy", -1)
    left = shift(edge_high, "gx", 1)
    after = shift(edge_low, "gx", -1)
    image, parts, dots = call(
        image_kernel,
        [field_shape, parts_shape, dots_shape],
        place,
        field,
        chunk,
        left,
        after,
        under,
        over,
        cond_after,
        cond_over,
        dots,
        *table,
        smem=1,
    )
    parts, dots = solve(2, exchange(parts), dots)
    dots = all_sum(dots)
    parts = exchange(parts)
    packed = exchange(call(pack_kernel, shape(GROUP, 3 * COLS, PLANE), parts, *table, field, image))
    cells = shape(NZ, ROWS, CELLS)
    return tuple(call(finish_kernel, [cells] * 3, packed, start_pressure, residual, dots))


def solution(mesh):
    placed = (
        P(None, "gy", "gx"),
        P(None, "gy", "gx"),
        P(None, None, "gy", "gx"),
        P("gx", None, None, None),
    )
    return jax.shard_map(
        shards,
        mesh=mesh,
        in_specs=placed,
        out_specs=(P(None, "gy", "gx"), P(None, "gy", "gx"), P(None, "gy", "gx")),
        check_vma=False,
    )
```

```python
import functools
import math

import jax
import jax.numpy as jnp
import numpy as np
from jax import lax
from jax.experimental import pallas as pl
from jax.experimental.pallas import tpu as pltpu
from jax.sharding import PartitionSpec as P

NZ = 64
ROWS = 4
CELLS = 256
GROUP = 32
COLS = 8
LENGTH = CELLS * GROUP
PLANE = ROWS * NZ
HALF = 128

f32 = jnp.float32
bf16 = jnp.bfloat16


def reverse_bits(number):
    return int(f"{number:05b}"[::-1], 2)


def column_tables():
    residue = np.array([reverse_bits(i) for i in range(GROUP)])
    angle = 2.0 * np.pi * np.outer(residue, np.arange(GROUP)) / GROUP
    same = np.eye(COLS)

    def table(real_row, imag_row):
        pair = np.stack([real_row, imag_row], axis=1)
        full = pair[:, :, None, :, None] * same[None, None, :, None, :]
        return full.reshape(GROUP * 2 * COLS, CELLS).astype(np.float32)

    cosine, sine = np.cos(angle), np.sin(angle)
    return table(cosine, -sine), table(-sine, -cosine)


def edge_tables():
    residue = np.array([reverse_bits(i) for i in range(GROUP)])
    angle = 2.0 * np.pi * np.outer(residue, np.arange(GROUP)) / GROUP
    same = np.eye(4).reshape(2, 2, 2, 2)

    def table(real_row, imag_row):
        pair = np.stack([real_row, imag_row], axis=1)
        full = pair[:, None, None, :, None, None, :] * same[None, :, :, None, :, :, None]
        return full.reshape(GROUP * 8, 4 * GROUP).astype(np.float32)

    cosine, sine = np.cos(angle), np.sin(angle)
    return table(cosine, -sine), table(-sine, -cosine)


def wave_table():
    angle = 2.0 * np.pi * np.outer(np.arange(CELLS), np.arange(CELLS)) / CELLS
    cosine, sine = np.cos(angle), np.sin(angle)
    real_rows = np.concatenate([cosine, -sine], axis=1).reshape(GROUP, 1, COLS, 2 * CELLS)
    imag_rows = np.concatenate([sine, cosine], axis=1).reshape(GROUP, 1, COLS, 2 * CELLS)
    full = np.concatenate([real_rows, imag_rows], axis=1).reshape(2 * CELLS, 2 * CELLS)
    full = full.astype(np.float32)
    high = full.astype(jnp.bfloat16)
    low = (full - high.astype(np.float32)).astype(jnp.bfloat16)
    return high, low


def split(values):
    high = values.astype(bf16)
    return high, (values - high.astype(f32)).astype(bf16)


def products(left, right, contract):
    dims = (contract, ((), ()))
    (left_high, left_low), (right_high, right_low) = left, right

    def one(a, b):
        return lax.dot_general(a, b, dims, preferred_element_type=f32)

    return one(left_high, right_high) + (one(left_high, right_low) + one(left_low, right_high))


def lanes_of(shape):
    return lax.broadcasted_iota(jnp.int32, shape, 1)


def roll_half(tile):
    return pltpu.roll(tile, 64, 1)


def low_row_packed(field):
    tile = field[:, :HALF]
    lane = lanes_of((HALF, HALF))
    return jnp.where(lane < 64, tile[:HALF], roll_half(tile[HALF:]))


def high_row_packed(field):
    tile = field[:, HALF:]
    lane = lanes_of((HALF, HALF))
    return jnp.where(lane < 64, roll_half(tile[:HALF]), tile[HALF:])


def behind_rows(field, halo):
    first, second = field[:, :HALF], field[:, HALF:]
    turned, turned_second = roll_half(first), roll_half(second)
    lane = lanes_of(first.shape)
    return jnp.concatenate(
        [jnp.where(lane < 64, halo, turned), jnp.where(lane < 64, turned, turned_second)], axis=1
    )


def before_rows(field, halo):
    first, second = field[:, :HALF], field[:, HALF:]
    turned, turned_second = roll_half(first), roll_half(second)
    lane = lanes_of(first.shape)
    return jnp.concatenate(
        [jnp.where(lane < 64, turned, turned_second), jnp.where(lane < 64, turned_second, halo)], axis=1
    )


def operate(centre, x_pair, y_pair, along, ahead_x, ahead_y):
    along_x, along_y, along_z = along
    plane = lanes_of(centre.shape) % NZ
    first, last = plane == 0, plane == NZ - 1
    ahead_z = jnp.where(last, pltpu.roll(along_z, NZ - 1, 1), pltpu.roll(along_z, PLANE - 1, 1))
    behind_z = jnp.where(first, 0.0, pltpu.roll(centre, 1, 1))
    before_z = jnp.where(last, 0.0, pltpu.roll(centre, PLANE - 1, 1))
    result_x = along_x * (centre - x_pair[0]) + ahead_x * (centre - x_pair[1])
    result_y = along_y * (centre - y_pair[0]) + ahead_y * (centre - y_pair[1])
    result_z = along_z * (centre - behind_z) + ahead_z * (centre - before_z)
    return result_x + result_y + result_z


def turned(ref, lead=()):
    rows = [ref[lead + (slice(None), y, slice(None))] for y in range(ROWS)]
    return jnp.concatenate(rows, axis=0).T


def y_neighbours(place, field, along_y, under, over, cond_over):
    under = jnp.concatenate([under, roll_half(under)], axis=0)
    over = jnp.concatenate([roll_half(over), over], axis=0)
    cond_over = jnp.concatenate([roll_half(cond_over), cond_over], axis=0)
    under = jnp.where(place[1] == 0, 0.0, under)
    over = jnp.where(place[1] == place[3] - 1, 0.0, over)
    pair = (behind_rows(field, under), before_rows(field, over))
    return pair, before_rows(along_y, cond_over)


def entry_kernel(
    start_hbm,
    cond_hbm,
    right_hbm,
    field_ref,
    along_ref,
    right_out,
    left_ref,
    right_ref,
    under_ref,
    over_ref,
    start_ref,
    cond_ref,
    rhs_ref,
    semaphores,
):
    copies = [pltpu.make_async_copy(start_hbm, start_ref, semaphores.at[0])]
    copies += [pltpu.make_async_copy(cond_hbm.at[i], cond_ref.at[i], semaphores.at[1 + i]) for i in range(3)]
    copies += [pltpu.make_async_copy(right_hbm, rhs_ref, semaphores.at[4])]
    for copy in copies:
        copy.start()
    copies[0].wait()
    field = turned(start_ref)
    field_ref[...] = field
    left_ref[0:1] = field[0:1]
    right_ref[0:1] = field[CELLS - 1 :]
    under_ref[:HALF] = low_row_packed(field)
    over_ref[...] = high_row_packed(field)
    for axis in range(3):
        copies[1 + axis].wait()
        along = turned(cond_ref, (axis,))
        if axis == 0:
            left_ref[1:2] = along[0:1]
        if axis == 1:
            under_ref[HALF:] = low_row_packed(along)
        along_ref[:, COLS * axis : COLS * (axis + 1), :] = along.reshape(GROUP, COLS, PLANE)
    copies[4].wait()
    right_out[...] = turned(rhs_ref)


def residual_kernel(place, rhs_ref, field_ref, chunk_ref, left_ref, next_ref, under_ref, over_ref, out_ref, residual_ref):
    field = field_ref[...]
    along = coefficients(chunk_ref)
    row = lax.broadcasted_iota(jnp.int32, (CELLS, PLANE), 0)
    behind_x = jnp.where(row == 0, left_ref[0:1], pltpu.roll(field, 1, 0))
    before_x = jnp.where(row == CELLS - 1, next_ref[0:1], pltpu.roll(field, CELLS - 1, 0))
    ahead_x = jnp.where(row == CELLS - 1, next_ref[1:2], pltpu.roll(along[0], CELLS - 1, 0))
    y_pair, ahead_y = y_neighbours(
        place, field, along[1], under_ref[...], over_ref[:HALF], over_ref[HALF:]
    )
    image = operate(field, (behind_x, before_x), y_pair, along, ahead_x, ahead_y)
    residual = rhs_ref[...] - image
    residual_ref[...] = residual
    out_ref[:, 0 : 3 * COLS, :] = chunk_ref[...]
    out_ref[:, 3 * COLS :, :] = residual.reshape(GROUP, COLS, PLANE)


def coefficients(chunk_ref):
    return [chunk_ref[:, COLS * axis : COLS * (axis + 1), :].reshape(CELLS, PLANE) for axis in range(3)]


def table_kernel(cosine_ref, sine_ref, turn_ref, high_ref, low_ref):
    turn = turn_ref[...]
    table = cosine_ref[...] * turn[:, 0:1] + sine_ref[...] * turn[:, 1:2]
    high_ref[...], low_ref[...] = split(table)


def spread_kernel(field_ref, high_ref, low_ref, out_ref):
    field = field_ref[:, 3 * COLS :, :].reshape(CELLS, PLANE)
    table = (high_ref[...], low_ref[...])
    out_ref[...] = products(table, split(field), ((1,), (0,))).reshape(GROUP, 2 * COLS, PLANE)


def solve_kernel(which, parts_ref, inverse_ref, high_ref, low_ref, dots_ref, out_ref, sums_ref, wave, solved, back, held, semaphores):
    copies = []
    for half in range(2):
        lanes = pl.ds(half * HALF, HALF)
        source = inverse_ref.at[:, :, lanes]
        copies.append(pltpu.make_async_copy(source, held.at[half], semaphores.at[half]))
        copies[half].start()
    table = (high_ref[...], low_ref[...])
    parts = parts_ref[...].reshape(2 * CELLS, PLANE).T
    wave[...] = products(split(parts), table, ((1,), (0,)))
    total = jnp.zeros((8, HALF), f32)
    for half in range(2):
        copies[half].wait()
        for pair in range(2):
            places = [(2 * pair + y, part * CELLS + half * HALF) for y in range(2) for part in range(2)]

            def step(group, sums):
                tiles = [
                    wave[pl.ds(pl.multiple_of(y * NZ + group * 8, 8), 8), lane : lane + HALF] for y, lane in places
                ]
                for z in range(8):
                    block = held[half, group * 8 + z]
                    sums = tuple(so_far + block * tile[z : z + 1] for so_far, tile in zip(sums, tiles))
                return sums

            sums = lax.fori_loop(0, NZ // 8, step, tuple(jnp.zeros((NZ, HALF), f32) for _ in places))
            for result, (y, lane) in zip(sums, places):
                solved[y * NZ : (y + 1) * NZ, lane : lane + HALF] = result
                product = result * wave[y * NZ : (y + 1) * NZ, lane : lane + HALF]
                total = total + jnp.sum(product.reshape(NZ // 8, 8, HALF), axis=0)
    row = lax.broadcasted_iota(jnp.int32, (8, HALF), 0)
    sums_ref[...] = dots_ref[...] + jnp.where(row == which, jnp.sum(total, axis=0, keepdims=True) / LENGTH, 0.0)
    parts = products(table, split(solved[...]), ((1,), (1,))).reshape(GROUP, 2 * COLS, PLANE)
    for half in range(2):
        out_ref[:, 16 * half : 16 * (half + 1), :] = parts[:, :, half * HALF : (half + 1) * HALF]
    if which == 0:
        back[...] = parts
        for side, (column, step) in enumerate(((COLS - 1, 1), (0, GROUP - 1))):
            for part in range(2):
                rows = pltpu.roll(back[:, part * COLS + column, :], step, 0)
                for half in range(2):
                    out_ref[:, 32 + 4 * half + 2 * side + part, :] = rows[:, half * HALF : (half + 1) * HALF]
    else:
        out_ref[:, 32:40, :] = jnp.broadcast_to(sums_ref[...][None], (GROUP, 8, HALF))


def gather_field(parts_ref, high_ref, low_ref):
    parts = jnp.concatenate(
        [parts_ref[:, 16 * half : 16 * (half + 1), :].reshape(2 * CELLS, HALF) for half in range(2)], axis=1
    )
    table = (high_ref[...], low_ref[...])
    return products(table, split(parts), ((0,), (0,))) * (1.0 / LENGTH)


def gather_kernel(
    parts_ref, high_ref, low_ref, edge_high_ref, edge_low_ref, field_ref, left_ref, next_ref, row_low_ref, row_high_ref
):
    field = gather_field(parts_ref, high_ref, low_ref)
    field_ref[...] = field
    row_low_ref[...] = low_row_packed(field)
    row_high_ref[...] = high_row_packed(field)
    beside = parts_ref[:, 32:40, :].reshape(CELLS, HALF)
    edges = products((edge_high_ref[...], edge_low_ref[...]), split(beside), ((0,), (0,))) * (1.0 / LENGTH)
    left_ref[...] = jnp.concatenate([edges[0:32], edges[64:96]], axis=1)
    next_ref[...] = jnp.concatenate([edges[32:64], edges[96:128]], axis=1)


def edge_rows(edge):
    return jnp.broadcast_to(edge[:, None, :], (GROUP, COLS, PLANE)).reshape(CELLS, PLANE)


def image_kernel(
    place,
    field_ref,
    chunk_ref,
    left_ref,
    next_ref,
    under_ref,
    over_ref,
    cond_next_ref,
    cond_over_ref,
    dots_ref,
    high_ref,
    low_ref,
    image_ref,
    parts_ref,
    sums_ref,
):
    field = field_ref[...]
    along = coefficients(chunk_ref)
    column = lax.broadcasted_iota(jnp.int32, (CELLS, PLANE), 0) % COLS
    cond_after = cond_next_ref[...]
    at_end = place[0] == place[2] - 1
    cond_after = jnp.where(at_end, pltpu.roll(cond_after, GROUP - 1, 0), cond_after)
    behind_x = jnp.where(column == 0, edge_rows(left_ref[...]), pltpu.roll(field, 1, 0))
    before_x = jnp.where(column == COLS - 1, edge_rows(next_ref[...]), pltpu.roll(field, CELLS - 1, 0))
    ahead_x = jnp.where(column == COLS - 1, edge_rows(cond_after), pltpu.roll(along[0], CELLS - 1, 0))
    y_pair, ahead_y = y_neighbours(place, field, along[1], under_ref[...], over_ref[...], cond_over_ref[...])
    image = operate(field, (behind_x, before_x), y_pair, along, ahead_x, ahead_y)
    image_ref[...] = image
    table = (high_ref[...], low_ref[...])
    parts_ref[...] = products(table, split(image), ((1,), (0,))).reshape(GROUP, 2 * COLS, PLANE)
    product = field * image
    total = jnp.sum((product[:, :HALF] + product[:, HALF:]), axis=0, keepdims=True)
    row = lax.broadcasted_iota(jnp.int32, (8, HALF), 0)
    sums_ref[...] = dots_ref[...] + jnp.where(row == 1, total, 0.0)


def edges_kernel(chunk_ref, edge_ref, row_ref):
    edge_ref[...] = chunk_ref[:, 0, :]
    row_ref[...] = low_row_packed(chunk_ref[:, COLS : 2 * COLS, :].reshape(CELLS, PLANE))


def pack_kernel(parts_ref, high_ref, low_ref, field_ref, image_ref, out_ref, sums_ref):
    out_ref[:, 0:COLS, :] = field_ref[...].reshape(GROUP, COLS, PLANE)
    out_ref[:, COLS : 2 * COLS, :] = image_ref[...].reshape(GROUP, COLS, PLANE)
    latest = gather_field(parts_ref, high_ref, low_ref)
    out_ref[:, 2 * COLS :, :] = latest.reshape(GROUP, COLS, PLANE)
    sums_ref[...] = jnp.sum(parts_ref[:, 32:40, :], axis=0)


def finish_kernel(packed_ref, start_ref, residual_ref, dots_ref, pressure_out, residual_out, direction_out):
    sums = jnp.sum(dots_ref[...], axis=1, keepdims=True)
    first, curvature, third = sums[0:1], sums[1:2], sums[2:3]
    step = first / curvature
    second = first - 2.0 * step * curvature + step * step * third
    ratio = second / first
    field = packed_ref[:, 0:COLS, :].reshape(CELLS, PLANE)
    image = packed_ref[:, COLS : 2 * COLS, :].reshape(CELLS, PLANE)
    latest = packed_ref[:, 2 * COLS :, :].reshape(CELLS, PLANE)
    change = (step * field).T
    residual = (residual_ref[...] - step * image).T
    direction = ((field - step * latest) + ratio * field).T
    for y in range(ROWS):
        rows = slice(y * NZ, (y + 1) * NZ)
        pressure_out[:, y, :] = start_ref[:, y, :] + change[rows]
        residual_out[:, y, :] = residual[rows]
        direction_out[:, y, :] = direction[rows]


def shape(*dims, dtype=f32):
    return jax.ShapeDtypeStruct(dims, dtype)


def call(kernel, outs, *args, smem=0, hbm=(), scratch=(), cost=0):
    specs = [pl.BlockSpec(memory_space=pltpu.SMEM if i < smem else pltpu.VMEM) for i in range(len(args))]
    args = list(args)
    for i in hbm:
        specs[i] = pl.BlockSpec(memory_space=pltpu.HBM)
        args[i] = pltpu.with_memory_space_constraint(args[i], pltpu.HBM)
    many = isinstance(outs, (tuple, list))
    out_spec = pl.BlockSpec(memory_space=pltpu.VMEM)
    return pl.pallas_call(
        kernel,
        out_shape=outs,
        in_specs=specs,
        out_specs=[out_spec] * len(outs) if many else out_spec,
        scratch_shapes=list(scratch),
        compiler_params=pltpu.CompilerParams(vmem_limit_bytes=16 * 1024 * 1024),
        cost_estimate=pl.CostEstimate(flops=cost, bytes_accessed=2**20, transcendentals=0),
    )(*args)


def shift(value, axis, step):
    count = lax.axis_size(axis)
    return lax.ppermute(value, axis, [(i, (i + step) % count) for i in range(count)])


def exchange(parts):
    return lax.all_to_all(parts, "gx", 0, 0, tiled=True)


def sum_over(value, axis):
    count = lax.axis_size(axis)
    distance = 1
    while distance < count:
        value = value + lax.ppermute(value, axis, [(i, i ^ distance) for i in range(count)])
        distance *= 2
    return value


def turns(columns, repeats):
    residues = jnp.asarray([reverse_bits(i) for i in range(GROUP)], jnp.int32)
    angle = (residues[:, None] * columns[None, :] % LENGTH).astype(f32) * (2.0 * math.pi / LENGTH)
    turn = jnp.stack([jnp.cos(angle), jnp.sin(angle)], axis=-1)
    return jnp.broadcast_to(turn[:, None], (GROUP, repeats) + turn.shape[1:]).reshape(-1, 2)


def shards(right_side, start_pressure, conductance, inverses):
    place = jnp.stack(
        [lax.axis_index("gx"), lax.axis_index("gy"), lax.axis_size("gx"), lax.axis_size("gy")]
    ).astype(jnp.int32)
    field_shape = shape(CELLS, PLANE)
    parts_shape = shape(GROUP, 2 * COLS, PLANE)
    wide_shape = shape(GROUP, 5 * COLS, HALF)
    edge_shape, row_shape, dots_shape = shape(GROUP, PLANE), shape(HALF, HALF), shape(8, HALF)

    cells_shape = shape(NZ, ROWS, CELLS)
    start, along, turned_right, to_left, to_right, to_under, to_over = call(
        entry_kernel,
        [
            field_shape,
            shape(GROUP, 3 * COLS, PLANE),
            field_shape,
            shape(8, PLANE),
            shape(8, PLANE),
            shape(2 * HALF, HALF),
            row_shape,
        ],
        start_pressure,
        conductance,
        right_side,
        hbm=(0, 1, 2),
        scratch=[
            pltpu.VMEM((NZ, ROWS, CELLS), f32),
            pltpu.VMEM((3, NZ, ROWS, CELLS), f32),
            pltpu.VMEM((NZ, ROWS, CELLS), f32),
            pltpu.SemaphoreType.DMA((5,)),
        ],
    )
    under = shift(to_over, "gy", 1)
    over = shift(to_under, "gy", -1)
    left = shift(to_right, "gx", 1)
    after = shift(to_left, "gx", -1)
    chunk, residual = call(
        residual_kernel,
        [shape(GROUP, 4 * COLS, PLANE), field_shape],
        place,
        turned_right,
        start,
        along,
        left,
        after,
        under,
        over,
        smem=1,
    )
    chunk = exchange(chunk)

    first = lax.axis_index("gx") * COLS
    columns = first + jnp.arange(COLS, dtype=jnp.int32)
    table = call(
        table_kernel,
        [shape(2 * CELLS, CELLS, dtype=bf16)] * 2,
        *[jnp.asarray(part) for part in column_tables()],
        turns(columns, 2),
    )
    beside = jnp.stack([first - 1, first - 1, first + COLS, first + COLS]).astype(jnp.int32) % LENGTH
    edge_table = call(
        table_kernel,
        [shape(CELLS, HALF, dtype=bf16)] * 2,
        *[jnp.asarray(part) for part in edge_tables()],
        turns(beside, 2),
    )
    waves = [jnp.asarray(part) for part in wave_table()]
    inverse = inverses.reshape(inverses.shape[1:])

    def solve(which, parts, dots):
        return call(
            functools.partial(solve_kernel, which),
            [wide_shape, dots_shape],
            parts,
            inverse,
            *waves,
            dots,
            hbm=(1,),
            scratch=[
                pltpu.VMEM((PLANE, 2 * CELLS), f32),
                pltpu.VMEM((PLANE, 2 * CELLS), f32),
                pltpu.VMEM((GROUP, 2 * COLS, PLANE), f32),
                pltpu.VMEM((2, NZ, NZ, HALF), f32),
                pltpu.SemaphoreType.DMA((2,)),
            ],
            cost=2 * 10**9,
        )

    parts = exchange(call(spread_kernel, parts_shape, chunk, *table))
    cond_edge, cond_row = call(edges_kernel, [edge_shape, row_shape], chunk)
    cond_after = shift(cond_edge, "gx", -1)
    cond_over = shift(cond_row, "gy", -1)
    parts, cond_after, cond_over = lax.optimization_barrier((parts, cond_after, cond_over))
    parts, dots = solve(0, parts, jnp.zeros((8, HALF), f32))
    field, left, after, row_low, row_high = call(
        gather_kernel,
        [field_shape, edge_shape, edge_shape, row_shape, row_shape],
        exchange(parts),
        *table,
        *edge_table,
    )
    under = shift(row_high, "gy", 1)
    over = shift(row_low, "gy", -1)
    image, parts, dots = call(
        image_kernel,
        [field_shape, parts_shape, dots_shape],
        place,
        field,
        chunk,
        left,
        after,
        under,
        over,
        cond_after,
        cond_over,
        dots,
        *table,
        smem=1,
    )
    parts, _ = solve(2, exchange(parts), dots)
    packed, dots = call(
        pack_kernel, [shape(GROUP, 3 * COLS, PLANE), dots_shape], exchange(parts), *table, field, image
    )
    dots = sum_over(dots, "gy")
    return tuple(call(finish_kernel, [cells_shape] * 3, exchange(packed), start_pressure, residual, dots))


def solution(mesh):
    placed = (
        P(None, "gy", "gx"),
        P(None, "gy", "gx"),
        P(None, None, "gy", "gx"),
        P("gx", None, None, None),
    )
    return jax.shard_map(
        shards,
        mesh=mesh,
        in_specs=placed,
        out_specs=(P(None, "gy", "gx"), P(None, "gy", "gx"), P(None, "gy", "gx")),
        check_vma=False,
    )
```

```python
import functools

import jax
import jax.numpy as jnp
import numpy as np
from jax import lax
from jax.experimental import pallas as pl
from jax.experimental.pallas import tpu as pltpu
from jax.sharding import PartitionSpec as P

NZ = 64
ROWS = 4
CELLS = 256
GROUP = 32
COLS = 8
LENGTH = CELLS * GROUP
PLANE = ROWS * NZ
HALF = 128

f32 = jnp.float32
bf16 = jnp.bfloat16


def reverse_bits(number):
    return int(f"{number:05b}"[::-1], 2)


def column_table():
    residue = np.array([reverse_bits(i) for i in range(GROUP)])
    angle = 2.0 * np.pi * np.outer(residue, np.arange(GROUP)) / GROUP
    same = np.eye(COLS)

    def table(real_row, imag_row):
        pair = np.stack([real_row, imag_row], axis=1)
        full = pair[:, :, None, :, None] * same[None, None, :, None, :]
        return full.reshape(GROUP * 2 * COLS, CELLS).astype(np.float32)

    return table(np.cos(angle), -np.sin(angle))


def edge_table():
    residue = np.array([reverse_bits(i) for i in range(GROUP)])
    angle = 2.0 * np.pi * np.outer(residue, np.arange(GROUP)) / GROUP
    same = np.eye(4).reshape(2, 2, 2, 2)

    def table(real_row, imag_row):
        pair = np.stack([real_row, imag_row], axis=1)
        full = pair[:, None, None, :, None, None, :] * same[None, :, :, None, :, :, None]
        return full.reshape(GROUP * 8, 4 * GROUP).astype(np.float32)

    return table(np.cos(angle), -np.sin(angle))


def turn_table():
    residue = np.array([reverse_bits(i) for i in range(GROUP)])
    first = COLS * np.arange(GROUP)[:, None]
    own = np.tile(np.arange(COLS), 2)[None, :] + first
    beside = np.tile(np.array([-1, -1, COLS, COLS]), 2)[None, :] + first

    def angles(columns):
        turns = residue[None, :, None] * columns[:, None, :] % LENGTH
        return (2.0 * np.pi / LENGTH) * turns.reshape(GROUP, -1)

    full = np.zeros((GROUP, 8, 2 * CELLS), np.float32)
    for i, angle in enumerate((angles(own), angles(beside))):
        full[:, 2 * i, : angle.shape[1]] = np.cos(angle)
        full[:, 2 * i + 1, : angle.shape[1]] = np.sin(angle)
    return full


def wave_table():
    angle = 2.0 * np.pi * np.outer(np.arange(CELLS), np.arange(CELLS)) / CELLS
    cosine, sine = np.cos(angle), np.sin(angle)
    real_rows = np.concatenate([cosine, -sine], axis=1).reshape(GROUP, 1, COLS, 2 * CELLS)
    imag_rows = np.concatenate([sine, cosine], axis=1).reshape(GROUP, 1, COLS, 2 * CELLS)
    full = np.concatenate([real_rows, imag_rows], axis=1).reshape(2 * CELLS, 2 * CELLS)
    full = full.astype(np.float32)
    high = full.astype(jnp.bfloat16)
    low = (full - high.astype(np.float32)).astype(jnp.bfloat16)
    return high, low


def split(values):
    high = values.astype(bf16)
    return high, (values - high.astype(f32)).astype(bf16)


def products(left, right, contract):
    dims = (contract, ((), ()))
    (left_high, left_low), (right_high, right_low) = left, right

    def one(a, b):
        return lax.dot_general(a, b, dims, preferred_element_type=f32)

    return one(left_high, right_high) + (one(left_high, right_low) + one(left_low, right_high))


def lanes_of(shape):
    return lax.broadcasted_iota(jnp.int32, shape, 1)


def roll_half(tile):
    return pltpu.roll(tile, 64, 1)


def low_row_packed(field):
    tile = field[:, :HALF]
    lane = lanes_of((HALF, HALF))
    return jnp.where(lane < 64, tile[:HALF], roll_half(tile[HALF:]))


def high_row_packed(field):
    tile = field[:, HALF:]
    lane = lanes_of((HALF, HALF))
    return jnp.where(lane < 64, roll_half(tile[:HALF]), tile[HALF:])


def behind_rows(field, halo):
    first, second = field[:, :HALF], field[:, HALF:]
    turned, turned_second = roll_half(first), roll_half(second)
    lane = lanes_of(first.shape)
    return jnp.concatenate(
        [jnp.where(lane < 64, halo, turned), jnp.where(lane < 64, turned, turned_second)], axis=1
    )


def before_rows(field, halo):
    first, second = field[:, :HALF], field[:, HALF:]
    turned, turned_second = roll_half(first), roll_half(second)
    lane = lanes_of(first.shape)
    return jnp.concatenate(
        [jnp.where(lane < 64, turned, turned_second), jnp.where(lane < 64, turned_second, halo)], axis=1
    )


def operate(centre, x_pair, y_pair, along, ahead_x, ahead_y):
    along_x, along_y, along_z = along
    plane = lanes_of(centre.shape) % NZ
    first, last = plane == 0, plane == NZ - 1
    ahead_z = jnp.where(last, pltpu.roll(along_z, NZ - 1, 1), pltpu.roll(along_z, PLANE - 1, 1))
    behind_z = jnp.where(first, 0.0, pltpu.roll(centre, 1, 1))
    before_z = jnp.where(last, 0.0, pltpu.roll(centre, PLANE - 1, 1))
    result_x = along_x * (centre - x_pair[0]) + ahead_x * (centre - x_pair[1])
    result_y = along_y * (centre - y_pair[0]) + ahead_y * (centre - y_pair[1])
    result_z = along_z * (centre - behind_z) + ahead_z * (centre - before_z)
    return result_x + result_y + result_z


def turned(ref, lead=()):
    rows = [ref[lead + (slice(None), y, slice(None))] for y in range(ROWS)]
    return jnp.concatenate(rows, axis=0).T


def y_neighbours(place, field, along_y, under, over, cond_over):
    under = jnp.concatenate([under, roll_half(under)], axis=0)
    over = jnp.concatenate([roll_half(over), over], axis=0)
    cond_over = jnp.concatenate([roll_half(cond_over), cond_over], axis=0)
    under = jnp.where(place[1] == 0, 0.0, under)
    over = jnp.where(place[1] == place[3] - 1, 0.0, over)
    pair = (behind_rows(field, under), before_rows(field, over))
    return pair, before_rows(along_y, cond_over)


def entry_kernel(
    start_hbm,
    cond_hbm,
    field_ref,
    along_ref,
    left_ref,
    right_ref,
    under_ref,
    over_ref,
    start_ref,
    cond_ref,
    semaphores,
):
    copies = [pltpu.make_async_copy(start_hbm, start_ref, semaphores.at[0])]
    copies += [pltpu.make_async_copy(cond_hbm.at[i], cond_ref.at[i], semaphores.at[1 + i]) for i in range(2)]
    for copy in copies:
        copy.start()
    copies[0].wait()
    field = turned(start_ref)
    field_ref[...] = field
    left_ref[0:1] = field[0:1]
    right_ref[0:1] = field[CELLS - 1 :]
    under_ref[:HALF] = low_row_packed(field)
    over_ref[...] = high_row_packed(field)
    for axis in range(2):
        copies[1 + axis].wait()
        along = turned(cond_ref, (axis,))
        if axis == 0:
            left_ref[1:2] = along[0:1]
        else:
            under_ref[HALF:] = low_row_packed(along)
        along_ref[:, COLS * axis : COLS * (axis + 1), :] = along.reshape(GROUP, COLS, PLANE)


def side_kernel(place, order_ref, cond_hbm, right_hbm, turns_hbm, column_hbm, edge_hbm, *refs):
    along_out, right_out, high_ref, low_ref, edge_high_ref, edge_low_ref = refs[:6]
    cond_ref, rhs_ref, turns_ref, column_ref, edge_ref, semaphores = refs[6:]
    sources = (cond_hbm.at[2], right_hbm, turns_hbm.at[place[0]], column_hbm, edge_hbm)
    targets = (cond_ref, rhs_ref, turns_ref, column_ref, edge_ref)
    copies = [pltpu.make_async_copy(*pair, semaphores.at[i]) for i, pair in enumerate(zip(sources, targets))]
    for copy in copies:
        copy.start()
    copies[0].wait()
    along_out[...] = turned(cond_ref).reshape(GROUP, COLS, PLANE)
    copies[1].wait()
    right_out[...] = turned(rhs_ref)
    copies[2].wait()
    turns = turns_ref[...].T
    copies[3].wait()
    table = column_ref[...]
    blocks = table.reshape(GROUP, 2 * COLS, CELLS)
    other = jnp.concatenate([blocks[:, COLS:], -blocks[:, :COLS]], axis=1).reshape(2 * CELLS, CELLS)
    high_ref[...], low_ref[...] = split(table * turns[:, 0:1] + other * turns[:, 1:2])
    copies[4].wait()
    table = edge_ref[...]
    part = lax.broadcasted_iota(jnp.int32, (CELLS, HALF), 0) % 2
    other = jnp.where(part == 0, pltpu.roll(table, CELLS - 1, 0), -pltpu.roll(table, 1, 0))
    edge_high_ref[...], edge_low_ref[...] = split(table * turns[:CELLS, 2:3] + other * turns[:CELLS, 3:4])


def residual_kernel(
    place, rhs_ref, field_ref, along_ref, along_z_ref, left_ref, next_ref, under_ref, over_ref, out_ref, residual_ref
):
    field = field_ref[...]
    along = [along_ref[:, COLS * axis : COLS * (axis + 1), :].reshape(CELLS, PLANE) for axis in range(2)]
    along += [along_z_ref[...].reshape(CELLS, PLANE)]
    row = lax.broadcasted_iota(jnp.int32, (CELLS, PLANE), 0)
    behind_x = jnp.where(row == 0, left_ref[0:1], pltpu.roll(field, 1, 0))
    before_x = jnp.where(row == CELLS - 1, next_ref[0:1], pltpu.roll(field, CELLS - 1, 0))
    ahead_x = jnp.where(row == CELLS - 1, next_ref[1:2], pltpu.roll(along[0], CELLS - 1, 0))
    y_pair, ahead_y = y_neighbours(
        place, field, along[1], under_ref[...], over_ref[:HALF], over_ref[HALF:]
    )
    image = operate(field, (behind_x, before_x), y_pair, along, ahead_x, ahead_y)
    residual = rhs_ref[...] - image
    residual_ref[...] = residual
    out_ref[:, 0 : 2 * COLS, :] = along_ref[...]
    out_ref[:, 2 * COLS : 3 * COLS, :] = along_z_ref[...]
    out_ref[:, 3 * COLS :, :] = residual.reshape(GROUP, COLS, PLANE)


def coefficients(chunk_ref):
    return [chunk_ref[:, COLS * axis : COLS * (axis + 1), :].reshape(CELLS, PLANE) for axis in range(3)]


def spread_kernel(field_ref, high_ref, low_ref, out_ref):
    field = field_ref[:, 3 * COLS :, :].reshape(CELLS, PLANE)
    table = (high_ref[...], low_ref[...])
    out_ref[...] = products(table, split(field), ((1,), (0,))).reshape(GROUP, 2 * COLS, PLANE)


def solve_kernel(which, parts_ref, inverse_ref, high_ref, low_ref, dots_ref, out_ref, sums_ref, wave, solved, back, held, semaphores):
    copies = []
    for half in range(2):
        for i in range(2):
            planes, lanes = pl.ds(i * NZ // 2, NZ // 2), pl.ds(half * HALF, HALF)
            target = held.at[half, planes]
            copies.append(pltpu.make_async_copy(inverse_ref.at[planes, :, lanes], target, semaphores.at[2 * half + i]))
            copies[-1].start()
    table = (high_ref[...], low_ref[...])
    parts = parts_ref[...].reshape(2 * CELLS, PLANE).T
    wave[...] = products(split(parts), table, ((1,), (0,)))
    total = jnp.zeros((8, HALF), f32)
    for half in range(2):
        for pair in range(2):
            places = [(2 * pair + y, part * CELLS + half * HALF) for y in range(2) for part in range(2)]

            def step(group, sums):
                tiles = [
                    wave[pl.ds(pl.multiple_of(y * NZ + group * 8, 8), 8), lane : lane + HALF] for y, lane in places
                ]
                for z in range(8):
                    block = held[half, group * 8 + z]
                    sums = tuple(so_far + block * tile[z : z + 1] for so_far, tile in zip(sums, tiles))
                return sums

            sums = tuple(jnp.zeros((NZ, HALF), f32) for _ in places)
            for i in range(2):
                if pair == 0:
                    copies[2 * half + i].wait()
                sums = lax.fori_loop(i * NZ // 16, (i + 1) * NZ // 16, step, sums)
            for result, (y, lane) in zip(sums, places):
                solved[y * NZ : (y + 1) * NZ, lane : lane + HALF] = result
                product = result * wave[y * NZ : (y + 1) * NZ, lane : lane + HALF]
                total = total + jnp.sum(product.reshape(NZ // 8, 8, HALF), axis=0)
    row = lax.broadcasted_iota(jnp.int32, (8, HALF), 0)
    sums_ref[...] = dots_ref[...] + jnp.where(row == which, jnp.sum(total, axis=0, keepdims=True) / LENGTH, 0.0)
    parts = products(table, split(solved[...]), ((1,), (1,))).reshape(GROUP, 2 * COLS, PLANE)
    for half in range(2):
        out_ref[:, 16 * half : 16 * (half + 1), :] = parts[:, :, half * HALF : (half + 1) * HALF]
    if which == 0:
        back[...] = parts
        for side, (column, step) in enumerate(((COLS - 1, 1), (0, GROUP - 1))):
            for part in range(2):
                rows = pltpu.roll(back[:, part * COLS + column, :], step, 0)
                for half in range(2):
                    out_ref[:, 32 + 4 * half + 2 * side + part, :] = rows[:, half * HALF : (half + 1) * HALF]
    else:
        out_ref[:, 32:40, :] = jnp.broadcast_to(sums_ref[...][None], (GROUP, 8, HALF))


def gather_field(parts_ref, high_ref, low_ref):
    parts = jnp.concatenate(
        [parts_ref[:, 16 * half : 16 * (half + 1), :].reshape(2 * CELLS, HALF) for half in range(2)], axis=1
    )
    table = (high_ref[...], low_ref[...])
    return products(table, split(parts), ((0,), (0,))) * (1.0 / LENGTH)


def gather_kernel(
    parts_ref, high_ref, low_ref, edge_high_ref, edge_low_ref, field_ref, left_ref, next_ref, row_low_ref, row_high_ref
):
    field = gather_field(parts_ref, high_ref, low_ref)
    field_ref[...] = field
    row_low_ref[...] = low_row_packed(field)
    row_high_ref[...] = high_row_packed(field)
    beside = parts_ref[:, 32:40, :].reshape(CELLS, HALF)
    edges = products((edge_high_ref[...], edge_low_ref[...]), split(beside), ((0,), (0,))) * (1.0 / LENGTH)
    left_ref[...] = jnp.concatenate([edges[0:32], edges[64:96]], axis=1)
    next_ref[...] = jnp.concatenate([edges[32:64], edges[96:128]], axis=1)


def edge_rows(edge):
    return jnp.broadcast_to(edge[:, None, :], (GROUP, COLS, PLANE)).reshape(CELLS, PLANE)


def image_kernel(
    place,
    field_ref,
    chunk_ref,
    left_ref,
    next_ref,
    under_ref,
    over_ref,
    cond_next_ref,
    cond_over_ref,
    dots_ref,
    high_ref,
    low_ref,
    image_ref,
    parts_ref,
    sums_ref,
):
    field = field_ref[...]
    along = coefficients(chunk_ref)
    column = lax.broadcasted_iota(jnp.int32, (CELLS, PLANE), 0) % COLS
    cond_after = cond_next_ref[...]
    at_end = place[0] == place[2] - 1
    cond_after = jnp.where(at_end, pltpu.roll(cond_after, GROUP - 1, 0), cond_after)
    behind_x = jnp.where(column == 0, edge_rows(left_ref[...]), pltpu.roll(field, 1, 0))
    before_x = jnp.where(column == COLS - 1, edge_rows(next_ref[...]), pltpu.roll(field, CELLS - 1, 0))
    ahead_x = jnp.where(column == COLS - 1, edge_rows(cond_after), pltpu.roll(along[0], CELLS - 1, 0))
    y_pair, ahead_y = y_neighbours(place, field, along[1], under_ref[...], over_ref[...], cond_over_ref[...])
    image = operate(field, (behind_x, before_x), y_pair, along, ahead_x, ahead_y)
    image_ref[...] = image
    table = (high_ref[...], low_ref[...])
    parts_ref[...] = products(table, split(image), ((1,), (0,))).reshape(GROUP, 2 * COLS, PLANE)
    product = field * image
    total = jnp.sum((product[:, :HALF] + product[:, HALF:]), axis=0, keepdims=True)
    row = lax.broadcasted_iota(jnp.int32, (8, HALF), 0)
    sums_ref[...] = dots_ref[...] + jnp.where(row == 1, total, 0.0)


def edges_kernel(chunk_ref, edge_ref, row_ref):
    edge_ref[...] = chunk_ref[:, 0, :]
    row_ref[...] = low_row_packed(chunk_ref[:, COLS : 2 * COLS, :].reshape(CELLS, PLANE))


def pack_kernel(parts_ref, high_ref, low_ref, field_ref, image_ref, out_ref, sums_ref):
    out_ref[:, 0:COLS, :] = field_ref[...].reshape(GROUP, COLS, PLANE)
    out_ref[:, COLS : 2 * COLS, :] = image_ref[...].reshape(GROUP, COLS, PLANE)
    latest = gather_field(parts_ref, high_ref, low_ref)
    out_ref[:, 2 * COLS :, :] = latest.reshape(GROUP, COLS, PLANE)
    sums_ref[...] = jnp.sum(parts_ref[:, 32:40, :], axis=0)


def finish_kernel(packed_ref, start_ref, residual_ref, dots_ref, pressure_out, residual_out, direction_out):
    sums = jnp.sum(dots_ref[...], axis=1, keepdims=True)
    first, curvature, third = sums[0:1], sums[1:2], sums[2:3]
    step = first / curvature
    second = first - 2.0 * step * curvature + step * step * third
    ratio = second / first
    field = packed_ref[:, 0:COLS, :].reshape(CELLS, PLANE)
    image = packed_ref[:, COLS : 2 * COLS, :].reshape(CELLS, PLANE)
    latest = packed_ref[:, 2 * COLS :, :].reshape(CELLS, PLANE)
    change = (step * field).T
    residual = (residual_ref[...] - step * image).T
    direction = ((field - step * latest) + ratio * field).T
    for y in range(ROWS):
        rows = slice(y * NZ, (y + 1) * NZ)
        pressure_out[:, y, :] = start_ref[:, y, :] + change[rows]
        residual_out[:, y, :] = residual[rows]
        direction_out[:, y, :] = direction[rows]


def shape(*dims, dtype=f32):
    return jax.ShapeDtypeStruct(dims, dtype)


def call(kernel, outs, *args, smem=0, hbm=(), scratch=(), cost=0):
    specs = [pl.BlockSpec(memory_space=pltpu.SMEM if i < smem else pltpu.VMEM) for i in range(len(args))]
    args = list(args)
    for i in hbm:
        specs[i] = pl.BlockSpec(memory_space=pltpu.HBM)
        args[i] = pltpu.with_memory_space_constraint(args[i], pltpu.HBM)
    many = isinstance(outs, (tuple, list))
    out_spec = pl.BlockSpec(memory_space=pltpu.VMEM)
    return pl.pallas_call(
        kernel,
        out_shape=outs,
        in_specs=specs,
        out_specs=[out_spec] * len(outs) if many else out_spec,
        scratch_shapes=list(scratch),
        compiler_params=pltpu.CompilerParams(vmem_limit_bytes=16 * 1024 * 1024),
        cost_estimate=pl.CostEstimate(flops=cost, bytes_accessed=2**20, transcendentals=0),
    )(*args)


def shift(value, axis, step):
    count = lax.axis_size(axis)
    return lax.ppermute(value, axis, [(i, (i + step) % count) for i in range(count)])


def exchange(parts):
    return lax.all_to_all(parts, "gx", 0, 0, tiled=True)


def sum_over(value, axis):
    count = lax.axis_size(axis)
    distance = 1
    while distance < count:
        value = value + lax.ppermute(value, axis, [(i, i ^ distance) for i in range(count)])
        distance *= 2
    return value


def shards(right_side, start_pressure, conductance, inverses):
    place = jnp.stack(
        [lax.axis_index("gx"), lax.axis_index("gy"), lax.axis_size("gx"), lax.axis_size("gy")]
    ).astype(jnp.int32)
    field_shape = shape(CELLS, PLANE)
    parts_shape = shape(GROUP, 2 * COLS, PLANE)
    wide_shape = shape(GROUP, 5 * COLS, HALF)
    edge_shape, row_shape, dots_shape = shape(GROUP, PLANE), shape(HALF, HALF), shape(8, HALF)

    cells_shape = shape(NZ, ROWS, CELLS)
    start, along, to_left, to_right, to_under, to_over = call(
        entry_kernel,
        [
            field_shape,
            shape(GROUP, 2 * COLS, PLANE),
            shape(8, PLANE),
            shape(8, PLANE),
            shape(2 * HALF, HALF),
            row_shape,
        ],
        start_pressure,
        conductance,
        hbm=(0, 1),
        scratch=[
            pltpu.VMEM((NZ, ROWS, CELLS), f32),
            pltpu.VMEM((2, NZ, ROWS, CELLS), f32),
            pltpu.SemaphoreType.DMA((3,)),
        ],
    )
    under = shift(to_over, "gy", 1)
    over = shift(to_under, "gy", -1)
    left = shift(to_right, "gx", 1)
    after = shift(to_left, "gx", -1)
    along_z, turned_right, *tables = call(
        side_kernel,
        [shape(GROUP, COLS, PLANE), field_shape]
        + [shape(2 * CELLS, CELLS, dtype=bf16)] * 2
        + [shape(CELLS, HALF, dtype=bf16)] * 2,
        place,
        to_left,
        conductance,
        right_side,
        jnp.asarray(turn_table()),
        jnp.asarray(column_table()),
        jnp.asarray(edge_table()),
        smem=1,
        hbm=(2, 3, 4, 5, 6),
        scratch=[
            pltpu.VMEM((NZ, ROWS, CELLS), f32),
            pltpu.VMEM((NZ, ROWS, CELLS), f32),
            pltpu.VMEM((8, 2 * CELLS), f32),
            pltpu.VMEM((2 * CELLS, CELLS), f32),
            pltpu.VMEM((CELLS, HALF), f32),
            pltpu.SemaphoreType.DMA((5,)),
        ],
    )
    under, over, left, after, along_z, turned_right, tables = lax.optimization_barrier(
        (under, over, left, after, along_z, turned_right, tables)
    )
    table, beside_table = tables[:2], tables[2:]
    chunk, residual = call(
        residual_kernel,
        [shape(GROUP, 4 * COLS, PLANE), field_shape],
        place,
        turned_right,
        start,
        along,
        along_z,
        left,
        after,
        under,
        over,
        smem=1,
    )
    chunk = exchange(chunk)
    waves = [jnp.asarray(part) for part in wave_table()]
    inverse = inverses.reshape(inverses.shape[1:])

    def solve(which, parts, dots):
        return call(
            functools.partial(solve_kernel, which),
            [wide_shape, dots_shape],
            parts,
            inverse,
            *waves,
            dots,
            hbm=(1,),
            scratch=[
                pltpu.VMEM((PLANE, 2 * CELLS), f32),
                pltpu.VMEM((PLANE, 2 * CELLS), f32),
                pltpu.VMEM((GROUP, 2 * COLS, PLANE), f32),
                pltpu.VMEM((2, NZ, NZ, HALF), f32),
                pltpu.SemaphoreType.DMA((4,)),
            ],
            cost=2 * 10**9,
        )

    parts = exchange(call(spread_kernel, parts_shape, chunk, *table))
    cond_edge, cond_row = call(edges_kernel, [edge_shape, row_shape], chunk)
    cond_after = shift(cond_edge, "gx", -1)
    cond_over = shift(cond_row, "gy", -1)
    parts, dots = solve(0, parts, jnp.zeros((8, HALF), f32))
    parts, cond_after, cond_over = lax.optimization_barrier((exchange(parts), cond_after, cond_over))
    field, left, after, row_low, row_high = call(
        gather_kernel,
        [field_shape, edge_shape, edge_shape, row_shape, row_shape],
        parts,
        *table,
        *beside_table,
    )
    under = shift(row_high, "gy", 1)
    over = shift(row_low, "gy", -1)
    image, parts, dots = call(
        image_kernel,
        [field_shape, parts_shape, dots_shape],
        place,
        field,
        chunk,
        left,
        after,
        under,
        over,
        cond_after,
        cond_over,
        dots,
        *table,
        smem=1,
    )
    parts, _ = solve(2, exchange(parts), dots)
    packed, dots = call(
        pack_kernel, [shape(GROUP, 3 * COLS, PLANE), dots_shape], exchange(parts), *table, field, image
    )
    dots = sum_over(dots, "gy")
    return tuple(call(finish_kernel, [cells_shape] * 3, exchange(packed), start_pressure, residual, dots))


def solution(mesh):
    placed = (
        P(None, "gy", "gx"),
        P(None, "gy", "gx"),
        P(None, None, "gy", "gx"),
        P("gx", None, None, None),
    )
    return jax.shard_map(
        shards,
        mesh=mesh,
        in_specs=placed,
        out_specs=(P(None, "gy", "gx"), P(None, "gy", "gx"), P(None, "gy", "gx")),
        check_vma=False,
    )
```

```python
import functools

import jax
import jax.numpy as jnp
import numpy as np
from jax import lax
from jax.experimental import pallas as pl
from jax.experimental.pallas import tpu as pltpu
from jax.sharding import PartitionSpec as P

NZ = 64
ROWS = 4
CELLS = 256
GROUP = 32
COLS = 8
LENGTH = CELLS * GROUP
PLANE = ROWS * NZ
HALF = 128

f32 = jnp.float32
bf16 = jnp.bfloat16


def reverse_bits(number):
    return int(f"{number:05b}"[::-1], 2)


def column_table():
    residue = np.array([reverse_bits(i) for i in range(GROUP)])
    angle = 2.0 * np.pi * np.outer(residue, np.arange(GROUP)) / GROUP
    same = np.eye(COLS)

    def table(real_row, imag_row):
        pair = np.stack([real_row, imag_row], axis=1)
        full = pair[:, :, None, :, None] * same[None, None, :, None, :]
        return full.reshape(GROUP * 2 * COLS, CELLS).astype(np.float32)

    return table(np.cos(angle), -np.sin(angle))


def edge_table():
    residue = np.array([reverse_bits(i) for i in range(GROUP)])
    angle = 2.0 * np.pi * np.outer(residue, np.arange(GROUP)) / GROUP
    same = np.eye(4).reshape(2, 2, 2, 2)

    def table(real_row, imag_row):
        pair = np.stack([real_row, imag_row], axis=1)
        full = pair[:, None, None, :, None, None, :] * same[None, :, :, None, :, :, None]
        return full.reshape(GROUP * 8, 4 * GROUP).astype(np.float32)

    return table(np.cos(angle), -np.sin(angle))


def turn_table():
    residue = np.array([reverse_bits(i) for i in range(GROUP)])
    first = COLS * np.arange(GROUP)[:, None]
    own = np.tile(np.arange(COLS), 2)[None, :] + first
    beside = np.tile(np.array([-1, -1, COLS, COLS]), 2)[None, :] + first

    def angles(columns):
        turns = residue[None, :, None] * columns[:, None, :] % LENGTH
        return (2.0 * np.pi / LENGTH) * turns.reshape(GROUP, -1)

    full = np.zeros((GROUP, 8, 2 * CELLS), np.float32)
    for i, angle in enumerate((angles(own), angles(beside))):
        full[:, 2 * i, : angle.shape[1]] = np.cos(angle)
        full[:, 2 * i + 1, : angle.shape[1]] = np.sin(angle)
    return full


def wave_table():
    angle = 2.0 * np.pi * np.outer(np.arange(CELLS), np.arange(CELLS)) / CELLS
    cosine, sine = np.cos(angle), np.sin(angle)
    real_rows = np.concatenate([cosine, -sine], axis=1).reshape(GROUP, 1, COLS, 2 * CELLS)
    imag_rows = np.concatenate([sine, cosine], axis=1).reshape(GROUP, 1, COLS, 2 * CELLS)
    full = np.concatenate([real_rows, imag_rows], axis=1).reshape(2 * CELLS, 2 * CELLS)
    full = full.astype(np.float32)
    high = full.astype(jnp.bfloat16)
    low = (full - high.astype(np.float32)).astype(jnp.bfloat16)
    return high, low


def split(values):
    high = values.astype(bf16)
    return high, (values - high.astype(f32)).astype(bf16)


def products(left, right, contract):
    dims = (contract, ((), ()))
    (left_high, left_low), (right_high, right_low) = left, right

    def one(a, b):
        return lax.dot_general(a, b, dims, preferred_element_type=f32)

    return one(left_high, right_high) + (one(left_high, right_low) + one(left_low, right_high))


def lanes_of(shape):
    return lax.broadcasted_iota(jnp.int32, shape, 1)


def roll_half(tile):
    return pltpu.roll(tile, 64, 1)


def low_row_packed(field):
    tile = field[:, :HALF]
    lane = lanes_of((HALF, HALF))
    return jnp.where(lane < 64, tile[:HALF], roll_half(tile[HALF:]))


def high_row_packed(field):
    tile = field[:, HALF:]
    lane = lanes_of((HALF, HALF))
    return jnp.where(lane < 64, roll_half(tile[:HALF]), tile[HALF:])


def behind_rows(field, halo):
    first, second = field[:, :HALF], field[:, HALF:]
    turned, turned_second = roll_half(first), roll_half(second)
    lane = lanes_of(first.shape)
    return jnp.concatenate(
        [jnp.where(lane < 64, halo, turned), jnp.where(lane < 64, turned, turned_second)], axis=1
    )


def before_rows(field, halo):
    first, second = field[:, :HALF], field[:, HALF:]
    turned, turned_second = roll_half(first), roll_half(second)
    lane = lanes_of(first.shape)
    return jnp.concatenate(
        [jnp.where(lane < 64, turned, turned_second), jnp.where(lane < 64, turned_second, halo)], axis=1
    )


def operate(centre, x_pair, y_pair, along, ahead_x, ahead_y):
    along_x, along_y, along_z = along
    plane = lanes_of(centre.shape) % NZ
    first, last = plane == 0, plane == NZ - 1
    ahead_z = jnp.where(last, pltpu.roll(along_z, NZ - 1, 1), pltpu.roll(along_z, PLANE - 1, 1))
    behind_z = jnp.where(first, 0.0, pltpu.roll(centre, 1, 1))
    before_z = jnp.where(last, 0.0, pltpu.roll(centre, PLANE - 1, 1))
    result_x = along_x * (centre - x_pair[0]) + ahead_x * (centre - x_pair[1])
    result_y = along_y * (centre - y_pair[0]) + ahead_y * (centre - y_pair[1])
    result_z = along_z * (centre - behind_z) + ahead_z * (centre - before_z)
    return result_x + result_y + result_z


def turned(ref, lead=()):
    rows = [ref[lead + (slice(None), y, slice(None))] for y in range(ROWS)]
    return jnp.concatenate(rows, axis=0).T


def y_neighbours(place, field, along_y, under, over, cond_over):
    under = jnp.concatenate([under, roll_half(under)], axis=0)
    over = jnp.concatenate([roll_half(over), over], axis=0)
    cond_over = jnp.concatenate([roll_half(cond_over), cond_over], axis=0)
    under = jnp.where(place[1:2, :HALF] == 0, 0.0, under)
    over = jnp.where(place[1:2, :HALF] == place[3:4, :HALF], 0.0, over)
    pair = (behind_rows(field, under), before_rows(field, over))
    return pair, before_rows(along_y, cond_over)


def from_below(place, axis, first, second):
    return jnp.where(place[axis : axis + 1, : first.shape[1]] % 2 == 1, first, second)


def entry_kernel(
    place,
    start_hbm,
    cond_hbm,
    field_ref,
    along_ref,
    x_first_ref,
    x_second_ref,
    y_first_ref,
    y_second_ref,
    start_ref,
    cond_ref,
    semaphores,
):
    copies = [pltpu.make_async_copy(start_hbm, start_ref, semaphores.at[0])]
    copies += [pltpu.make_async_copy(cond_hbm.at[i], cond_ref.at[i], semaphores.at[1 + i]) for i in range(2)]
    for copy in copies:
        copy.start()
    copies[0].wait()
    field = turned(start_ref)
    field_ref[...] = field
    high, low = high_row_packed(field), low_row_packed(field)
    for axis in range(2):
        copies[1 + axis].wait()
        along = turned(cond_ref, (axis,))
        if axis == 0:
            left = jnp.concatenate([field[0:1], along[0:1]], axis=0)
            right = jnp.concatenate([field[CELLS - 1 :], along[0:1]], axis=0)
            x_first_ref[0:2] = from_below(place, 0, left, right)
            x_second_ref[0:2] = from_below(place, 0, right, left)
        else:
            along_low = low_row_packed(along)
            y_first_ref[:HALF] = from_below(place, 1, low, high)
            y_second_ref[:HALF] = from_below(place, 1, high, low)
            y_first_ref[HALF:] = along_low
            y_second_ref[HALF:] = along_low
        along_ref[:, COLS * axis : COLS * (axis + 1), :] = along.reshape(GROUP, COLS, PLANE)


def side_kernel(place, order_ref, cond_hbm, right_hbm, turns_hbm, column_hbm, edge_hbm, *refs):
    along_out, right_out, high_ref, low_ref, edge_high_ref, edge_low_ref = refs[:6]
    cond_ref, rhs_ref, turns_ref, column_ref, edge_ref, semaphores = refs[6:]
    sources = (cond_hbm.at[2], right_hbm, turns_hbm.at[place[0]], column_hbm, edge_hbm)
    targets = (cond_ref, rhs_ref, turns_ref, column_ref, edge_ref)
    copies = [pltpu.make_async_copy(*pair, semaphores.at[i]) for i, pair in enumerate(zip(sources, targets))]
    for copy in copies:
        copy.start()
    copies[0].wait()
    along_out[...] = turned(cond_ref).reshape(GROUP, COLS, PLANE)
    copies[1].wait()
    right_out[...] = turned(rhs_ref)
    copies[2].wait()
    turns = turns_ref[...].T
    copies[3].wait()
    table = column_ref[...]
    blocks = table.reshape(GROUP, 2 * COLS, CELLS)
    other = jnp.concatenate([blocks[:, COLS:], -blocks[:, :COLS]], axis=1).reshape(2 * CELLS, CELLS)
    high_ref[...], low_ref[...] = split(table * turns[:, 0:1] + other * turns[:, 1:2])
    copies[4].wait()
    table = edge_ref[...]
    part = lax.broadcasted_iota(jnp.int32, (CELLS, HALF), 0) % 2
    other = jnp.where(part == 0, pltpu.roll(table, CELLS - 1, 0), -pltpu.roll(table, 1, 0))
    edge_high_ref[...], edge_low_ref[...] = split(table * turns[:CELLS, 2:3] + other * turns[:CELLS, 3:4])


def residual_kernel(
    place, rhs_ref, field_ref, along_ref, along_z_ref, x_first_ref, x_second_ref, y_first_ref, y_second_ref, *outs
):
    out_ref, residual_ref = outs
    x_swaps, y_swaps = (x_first_ref[...], x_second_ref[...]), (y_first_ref[...], y_second_ref[...])
    left, after = from_below(place, 0, *x_swaps), from_below(place, 0, *x_swaps[::-1])
    under, over = from_below(place, 1, *y_swaps), from_below(place, 1, *y_swaps[::-1])
    field = field_ref[...]
    along = [along_ref[:, COLS * axis : COLS * (axis + 1), :].reshape(CELLS, PLANE) for axis in range(2)]
    along += [along_z_ref[...].reshape(CELLS, PLANE)]
    row = lax.broadcasted_iota(jnp.int32, (CELLS, PLANE), 0)
    behind_x = jnp.where(row == 0, left[0:1], pltpu.roll(field, 1, 0))
    before_x = jnp.where(row == CELLS - 1, after[0:1], pltpu.roll(field, CELLS - 1, 0))
    ahead_x = jnp.where(row == CELLS - 1, after[1:2], pltpu.roll(along[0], CELLS - 1, 0))
    y_pair, ahead_y = y_neighbours(
        place, field, along[1], under[:HALF], over[:HALF], over[HALF:]
    )
    image = operate(field, (behind_x, before_x), y_pair, along, ahead_x, ahead_y)
    residual = rhs_ref[...] - image
    residual_ref[...] = residual
    out_ref[:, 0 : 2 * COLS, :] = along_ref[...]
    out_ref[:, 2 * COLS : 3 * COLS, :] = along_z_ref[...]
    out_ref[:, 3 * COLS :, :] = residual.reshape(GROUP, COLS, PLANE)


def coefficients(chunk_ref):
    return [chunk_ref[:, COLS * axis : COLS * (axis + 1), :].reshape(CELLS, PLANE) for axis in range(3)]


def spread_kernel(field_ref, high_ref, low_ref, out_ref):
    field = field_ref[:, 3 * COLS :, :].reshape(CELLS, PLANE)
    table = (high_ref[...], low_ref[...])
    out_ref[...] = products(table, split(field), ((1,), (0,))).reshape(GROUP, 2 * COLS, PLANE)


def first_solve_kernel(
    parts_ref, inverse_ref, high_ref, low_ref, dots_ref, out_ref, sums_ref, wave, solved, back, held, semaphores
):
    copies = []
    for half in range(2):
        for i in range(2):
            planes, lanes = pl.ds(i * NZ // 2, NZ // 2), pl.ds(half * HALF, HALF)
            target = held.at[half, planes]
            copies.append(pltpu.make_async_copy(inverse_ref.at[planes, :, lanes], target, semaphores.at[2 * half + i]))
            copies[-1].start()
    def inverse_block(z, half):
        return held[half, z]

    solve(0, copies, inverse_block, parts_ref, high_ref, low_ref, dots_ref, out_ref, sums_ref, wave, solved, back)


def second_solve_kernel(parts_ref, inverse_ref, high_ref, low_ref, dots_ref, out_ref, wave, solved, sums_ref):
    def inverse_block(z, half):
        return inverse_ref[z, :, half * HALF : (half + 1) * HALF]

    solve(2, (), inverse_block, parts_ref, high_ref, low_ref, dots_ref, out_ref, sums_ref, wave, solved, None)


def solve(
    which, copies, inverse_block, parts_ref, high_ref, low_ref, dots_ref, out_ref, sums_ref, wave, solved, back
):
    table = (high_ref[...], low_ref[...])
    parts = parts_ref[...].reshape(2 * CELLS, PLANE).T
    wave[...] = products(split(parts), table, ((1,), (0,)))
    total = jnp.zeros((8, HALF), f32)
    for half in range(2):
        for pair in range(2):
            places = [(2 * pair + y, part * CELLS + half * HALF) for y in range(2) for part in range(2)]

            def step(group, sums):
                tiles = [
                    wave[pl.ds(pl.multiple_of(y * NZ + group * 8, 8), 8), lane : lane + HALF] for y, lane in places
                ]
                for z in range(8):
                    block = inverse_block(group * 8 + z, half)
                    sums = tuple(so_far + block * tile[z : z + 1] for so_far, tile in zip(sums, tiles))
                return sums

            sums = tuple(jnp.zeros((NZ, HALF), f32) for _ in places)
            for i in range(2):
                if copies and pair == 0:
                    copies[2 * half + i].wait()
                sums = lax.fori_loop(i * NZ // 16, (i + 1) * NZ // 16, step, sums)
            for result, (y, lane) in zip(sums, places):
                solved[y * NZ : (y + 1) * NZ, lane : lane + HALF] = result
                product = result * wave[y * NZ : (y + 1) * NZ, lane : lane + HALF]
                total = total + jnp.sum(product.reshape(NZ // 8, 8, HALF), axis=0)
    row = lax.broadcasted_iota(jnp.int32, (8, HALF), 0)
    total = jnp.sum(total, axis=0, keepdims=True) / LENGTH
    sums_ref[...] = dots_ref[...] + jnp.where(row == which, total, 0.0)
    parts = products(table, split(solved[...]), ((1,), (1,))).reshape(GROUP, 2 * COLS, PLANE)
    for half in range(2):
        out_ref[:, 16 * half : 16 * (half + 1), :] = parts[:, :, half * HALF : (half + 1) * HALF]
    if which == 0:
        back[...] = parts
        for side, (column, step) in enumerate(((COLS - 1, 1), (0, GROUP - 1))):
            for part in range(2):
                rows = pltpu.roll(back[:, part * COLS + column, :], step, 0)
                for half in range(2):
                    out_ref[:, 32 + 4 * half + 2 * side + part, :] = rows[:, half * HALF : (half + 1) * HALF]
    else:
        out_ref[:, 32:40, :] = jnp.broadcast_to(sums_ref[...][None], (GROUP, 8, HALF))


def gather_field(parts_ref, high_ref, low_ref):
    parts = jnp.concatenate(
        [parts_ref[:, 16 * half : 16 * (half + 1), :].reshape(2 * CELLS, HALF) for half in range(2)], axis=1
    )
    table = (high_ref[...], low_ref[...])
    return products(table, split(parts), ((0,), (0,))) * (1.0 / LENGTH)


def gather_kernel(
    parts_ref, high_ref, low_ref, edge_high_ref, edge_low_ref, field_ref, left_ref, next_ref, row_low_ref, row_high_ref
):
    field = gather_field(parts_ref, high_ref, low_ref)
    field_ref[...] = field
    row_low_ref[...] = low_row_packed(field)
    row_high_ref[...] = high_row_packed(field)
    beside = parts_ref[:, 32:40, :].reshape(CELLS, HALF)
    edges = products((edge_high_ref[...], edge_low_ref[...]), split(beside), ((0,), (0,))) * (1.0 / LENGTH)
    left_ref[...] = jnp.concatenate([edges[0:32], edges[64:96]], axis=1)
    next_ref[...] = jnp.concatenate([edges[32:64], edges[96:128]], axis=1)


def edge_rows(edge):
    return jnp.broadcast_to(edge[:, None, :], (GROUP, COLS, PLANE)).reshape(CELLS, PLANE)


def image_kernel(
    place,
    field_ref,
    chunk_ref,
    left_ref,
    next_ref,
    under_ref,
    over_ref,
    cond_next_ref,
    cond_over_ref,
    dots_ref,
    high_ref,
    low_ref,
    image_ref,
    parts_ref,
    sums_ref,
):
    field = field_ref[...]
    along = coefficients(chunk_ref)
    column = lax.broadcasted_iota(jnp.int32, (CELLS, PLANE), 0) % COLS
    cond_after = cond_next_ref[...]
    at_end = place[0:1] == place[2:3]
    cond_after = jnp.where(at_end, pltpu.roll(cond_after, GROUP - 1, 0), cond_after)
    behind_x = jnp.where(column == 0, edge_rows(left_ref[...]), pltpu.roll(field, 1, 0))
    before_x = jnp.where(column == COLS - 1, edge_rows(next_ref[...]), pltpu.roll(field, CELLS - 1, 0))
    ahead_x = jnp.where(column == COLS - 1, edge_rows(cond_after), pltpu.roll(along[0], CELLS - 1, 0))
    y_pair, ahead_y = y_neighbours(place, field, along[1], under_ref[...], over_ref[...], cond_over_ref[...])
    image = operate(field, (behind_x, before_x), y_pair, along, ahead_x, ahead_y)
    image_ref[...] = image
    table = (high_ref[...], low_ref[...])
    parts_ref[...] = products(table, split(image), ((1,), (0,))).reshape(GROUP, 2 * COLS, PLANE)
    product = field * image
    total = jnp.sum((product[:, :HALF] + product[:, HALF:]), axis=0, keepdims=True)
    row = lax.broadcasted_iota(jnp.int32, (8, HALF), 0)
    sums_ref[...] = dots_ref[...] + jnp.where(row == 1, total, 0.0)


def edges_kernel(chunk_ref, edge_ref, row_ref):
    edge_ref[...] = chunk_ref[:, 0, :]
    row_ref[...] = low_row_packed(chunk_ref[:, COLS : 2 * COLS, :].reshape(CELLS, PLANE))


def pack_kernel(parts_ref, high_ref, low_ref, field_ref, image_ref, out_ref, sums_ref):
    out_ref[:, 0:COLS, :] = field_ref[...].reshape(GROUP, COLS, PLANE)
    out_ref[:, COLS : 2 * COLS, :] = image_ref[...].reshape(GROUP, COLS, PLANE)
    latest = gather_field(parts_ref, high_ref, low_ref)
    out_ref[:, 2 * COLS :, :] = latest.reshape(GROUP, COLS, PLANE)
    sums_ref[...] = jnp.sum(parts_ref[:, 32:40, :], axis=0)


def finish_kernel(packed_ref, start_ref, residual_ref, dots_ref, pressure_out, residual_out, direction_out):
    sums = jnp.sum(dots_ref[...], axis=1, keepdims=True)
    first, curvature, third = sums[0:1], sums[1:2], sums[2:3]
    step = first / curvature
    second = first - 2.0 * step * curvature + step * step * third
    ratio = second / first
    field = packed_ref[:, 0:COLS, :].reshape(CELLS, PLANE)
    image = packed_ref[:, COLS : 2 * COLS, :].reshape(CELLS, PLANE)
    latest = packed_ref[:, 2 * COLS :, :].reshape(CELLS, PLANE)
    change = (step * field).T
    residual = (residual_ref[...] - step * image).T
    direction = ((field - step * latest) + ratio * field).T
    for y in range(ROWS):
        rows = slice(y * NZ, (y + 1) * NZ)
        pressure_out[:, y, :] = start_ref[:, y, :] + change[rows]
        residual_out[:, y, :] = residual[rows]
        direction_out[:, y, :] = direction[rows]


def shape(*dims, dtype=f32):
    return jax.ShapeDtypeStruct(dims, dtype)


def call(kernel, outs, *args, smem=0, hbm=(), scratch=(), cost=0):
    specs = [pl.BlockSpec(memory_space=pltpu.SMEM if i < smem else pltpu.VMEM) for i in range(len(args))]
    args = list(args)
    for i in hbm:
        specs[i] = pl.BlockSpec(memory_space=pltpu.HBM)
        args[i] = pltpu.with_memory_space_constraint(args[i], pltpu.HBM)
    many = isinstance(outs, (tuple, list))
    out_spec = pl.BlockSpec(memory_space=pltpu.VMEM)
    return pl.pallas_call(
        kernel,
        out_shape=outs,
        in_specs=specs,
        out_specs=[out_spec] * len(outs) if many else out_spec,
        scratch_shapes=list(scratch),
        compiler_params=pltpu.CompilerParams(vmem_limit_bytes=16 * 1024 * 1024),
        cost_estimate=pl.CostEstimate(flops=cost, bytes_accessed=2**20, transcendentals=0),
    )(*args)


def shift(value, axis, step):
    count = lax.axis_size(axis)
    return lax.ppermute(value, axis, [(i, (i + step) % count) for i in range(count)])


def swap(first, second, axis):
    count = lax.axis_size(axis)
    first = lax.ppermute(first, axis, [(i, i ^ 1) for i in range(count)])
    second = lax.ppermute(second, axis, [(i, (i + 2 * (i % 2) - 1) % count) for i in range(count)])
    return [first, second]


def exchange(parts):
    return lax.all_to_all(parts, "gx", 0, 0, tiled=True)


def sum_rows(value):
    count = lax.axis_size("gy")
    for mask in (1, 2, 6):
        value = value + lax.ppermute(value, "gy", [(i, i ^ mask) for i in range(count)])
    return value


def shards(right_side, start_pressure, conductance, inverses):
    sizes = [lax.axis_size(axis) for axis in ("gx", "gy")]
    place = jnp.stack([lax.axis_index("gx"), lax.axis_index("gy"), *[size - 1 for size in sizes]]).astype(jnp.int32)
    spread_place = jnp.broadcast_to(jnp.tile(place, 2)[:, None], (8, PLANE))
    field_shape = shape(CELLS, PLANE)
    parts_shape = shape(GROUP, 2 * COLS, PLANE)
    wide_shape = shape(GROUP, 5 * COLS, HALF)
    edge_shape, row_shape, dots_shape = shape(GROUP, PLANE), shape(HALF, HALF), shape(8, HALF)

    cells_shape = shape(NZ, ROWS, CELLS)
    start, along, *swaps = call(
        entry_kernel,
        [
            field_shape,
            shape(GROUP, 2 * COLS, PLANE),
            shape(8, PLANE),
            shape(8, PLANE),
            shape(2 * HALF, HALF),
            shape(2 * HALF, HALF),
        ],
        spread_place,
        start_pressure,
        conductance,
        hbm=(1, 2),
        scratch=[
            pltpu.VMEM((NZ, ROWS, CELLS), f32),
            pltpu.VMEM((2, NZ, ROWS, CELLS), f32),
            pltpu.SemaphoreType.DMA((3,)),
        ],
    )
    halos = swap(swaps[0], swaps[1], "gx") + swap(swaps[2], swaps[3], "gy")
    along_z, turned_right, *tables = call(
        side_kernel,
        [shape(GROUP, COLS, PLANE), field_shape]
        + [shape(2 * CELLS, CELLS, dtype=bf16)] * 2
        + [shape(CELLS, HALF, dtype=bf16)] * 2,
        place,
        swaps[0],
        conductance,
        right_side,
        jnp.asarray(turn_table()),
        jnp.asarray(column_table()),
        jnp.asarray(edge_table()),
        smem=1,
        hbm=(2, 3, 4, 5, 6),
        scratch=[
            pltpu.VMEM((NZ, ROWS, CELLS), f32),
            pltpu.VMEM((NZ, ROWS, CELLS), f32),
            pltpu.VMEM((8, 2 * CELLS), f32),
            pltpu.VMEM((2 * CELLS, CELLS), f32),
            pltpu.VMEM((CELLS, HALF), f32),
            pltpu.SemaphoreType.DMA((5,)),
        ],
    )
    halos, along_z, turned_right, tables = lax.optimization_barrier((halos, along_z, turned_right, tables))
    table, beside_table = tables[:2], tables[2:]
    chunk, residual = call(
        residual_kernel,
        [shape(GROUP, 4 * COLS, PLANE), field_shape],
        spread_place,
        turned_right,
        start,
        along,
        along_z,
        *halos,
    )
    chunk = exchange(chunk)
    waves = [jnp.asarray(part) for part in wave_table()]
    inverse = inverses.reshape(inverses.shape[1:])

    parts = exchange(call(spread_kernel, parts_shape, chunk, *table))
    cond_edge, cond_row = call(edges_kernel, [edge_shape, row_shape], chunk)
    cond_after = shift(cond_edge, "gx", -1)
    cond_over = shift(cond_row, "gy", -1)
    wave_shape = pltpu.VMEM((PLANE, 2 * CELLS), f32)
    parts, dots = call(
        first_solve_kernel,
        [wide_shape, dots_shape],
        parts,
        inverse,
        *waves,
        jnp.zeros((8, HALF), f32),
        hbm=(1,),
        scratch=[
            wave_shape,
            wave_shape,
            pltpu.VMEM((GROUP, 2 * COLS, PLANE), f32),
            pltpu.VMEM((2, NZ, NZ, HALF), f32),
            pltpu.SemaphoreType.DMA((4,)),
        ],
        cost=2 * 10**9,
    )
    parts, cond_after, cond_over = lax.optimization_barrier((exchange(parts), cond_after, cond_over))
    field, left, after, row_low, row_high = call(
        gather_kernel,
        [field_shape, edge_shape, edge_shape, row_shape, row_shape],
        parts,
        *table,
        *beside_table,
    )
    under = shift(row_high, "gy", 1)
    over = shift(row_low, "gy", -1)
    image, parts, dots = call(
        image_kernel,
        [field_shape, parts_shape, dots_shape],
        spread_place,
        field,
        chunk,
        left,
        after,
        under,
        over,
        cond_after,
        cond_over,
        dots,
        *table,
    )
    parts = call(
        second_solve_kernel,
        wide_shape,
        exchange(parts),
        inverse,
        *waves,
        dots,
        scratch=[wave_shape, wave_shape, pltpu.VMEM((8, HALF), f32)],
        cost=2 * 10**9,
    )
    packed, dots = call(
        pack_kernel, [shape(GROUP, 3 * COLS, PLANE), dots_shape], exchange(parts), *table, field, image
    )
    dots = sum_rows(dots)
    return tuple(call(finish_kernel, [cells_shape] * 3, exchange(packed), start_pressure, residual, dots))


def solution(mesh):
    placed = (
        P(None, "gy", "gx"),
        P(None, "gy", "gx"),
        P(None, None, "gy", "gx"),
        P("gx", None, None, None),
    )
    return jax.shard_map(
        shards,
        mesh=mesh,
        in_specs=placed,
        out_specs=(P(None, "gy", "gx"), P(None, "gy", "gx"), P(None, "gy", "gx")),
        check_vma=False,
    )
```

```python
import functools

import jax
import jax.numpy as jnp
import numpy as np
from jax import lax
from jax.experimental import pallas as pl
from jax.experimental.pallas import tpu as pltpu
from jax.sharding import PartitionSpec as P

NZ = 64
ROWS = 4
CELLS = 256
GROUP = 32
COLS = 8
LENGTH = CELLS * GROUP
PLANE = ROWS * NZ
HALF = 128

f32 = jnp.float32
bf16 = jnp.bfloat16


def reverse_bits(number):
    return int(f"{number:05b}"[::-1], 2)


def column_table():
    residue = np.array([reverse_bits(i) for i in range(GROUP)])
    angle = 2.0 * np.pi * np.outer(residue, np.arange(GROUP)) / GROUP
    same = np.eye(COLS)

    def table(real_row, imag_row):
        pair = np.stack([real_row, imag_row], axis=1)
        full = pair[:, :, None, :, None] * same[None, None, :, None, :]
        return full.reshape(GROUP * 2 * COLS, CELLS).astype(np.float32)

    return table(np.cos(angle), -np.sin(angle))


def edge_table():
    residue = np.array([reverse_bits(i) for i in range(GROUP)])
    angle = 2.0 * np.pi * np.outer(residue, np.arange(GROUP)) / GROUP
    same = np.eye(4).reshape(2, 2, 2, 2)

    def table(real_row, imag_row):
        pair = np.stack([real_row, imag_row], axis=1)
        full = pair[:, None, None, :, None, None, :] * same[None, :, :, None, :, :, None]
        return full.reshape(GROUP * 8, 4 * GROUP).astype(np.float32)

    return table(np.cos(angle), -np.sin(angle))


def turn_table():
    residue = np.array([reverse_bits(i) for i in range(GROUP)])
    first = COLS * np.arange(GROUP)[:, None]
    own = np.tile(np.arange(COLS), 2)[None, :] + first
    beside = np.tile(np.array([-1, -1, COLS, COLS]), 2)[None, :] + first

    def angles(columns):
        turns = residue[None, :, None] * columns[:, None, :] % LENGTH
        return (2.0 * np.pi / LENGTH) * turns.reshape(GROUP, -1)

    full = np.zeros((GROUP, 8, 2 * CELLS), np.float32)
    for i, angle in enumerate((angles(own), angles(beside))):
        full[:, 2 * i, : angle.shape[1]] = np.cos(angle)
        full[:, 2 * i + 1, : angle.shape[1]] = np.sin(angle)
    return full


def wave_table():
    angle = 2.0 * np.pi * np.outer(np.arange(CELLS), np.arange(CELLS)) / CELLS
    cosine, sine = np.cos(angle), np.sin(angle)
    real_rows = np.concatenate([cosine, -sine], axis=1).reshape(GROUP, 1, COLS, 2 * CELLS)
    imag_rows = np.concatenate([sine, cosine], axis=1).reshape(GROUP, 1, COLS, 2 * CELLS)
    full = np.concatenate([real_rows, imag_rows], axis=1).reshape(2 * CELLS, 2 * CELLS)
    full = full.astype(np.float32)
    high = full.astype(jnp.bfloat16)
    low = (full - high.astype(np.float32)).astype(jnp.bfloat16)
    return high, low


def split(values):
    high = values.astype(bf16)
    return high, (values - high.astype(f32)).astype(bf16)


def products(left, right, contract):
    dims = (contract, ((), ()))
    (left_high, left_low), (right_high, right_low) = left, right

    def one(a, b):
        return lax.dot_general(a, b, dims, preferred_element_type=f32)

    return one(left_high, right_high) + (one(left_high, right_low) + one(left_low, right_high))


def lanes_of(shape):
    return lax.broadcasted_iota(jnp.int32, shape, 1)


def roll_half(tile):
    return pltpu.roll(tile, 64, 1)


def low_row_packed(field):
    tile = field[:, :HALF]
    lane = lanes_of((HALF, HALF))
    return jnp.where(lane < 64, tile[:HALF], roll_half(tile[HALF:]))


def high_row_packed(field):
    tile = field[:, HALF:]
    lane = lanes_of((HALF, HALF))
    return jnp.where(lane < 64, roll_half(tile[:HALF]), tile[HALF:])


def behind_rows(field, halo):
    first, second = field[:, :HALF], field[:, HALF:]
    turned, turned_second = roll_half(first), roll_half(second)
    lane = lanes_of(first.shape)
    return jnp.concatenate(
        [jnp.where(lane < 64, halo, turned), jnp.where(lane < 64, turned, turned_second)], axis=1
    )


def before_rows(field, halo):
    first, second = field[:, :HALF], field[:, HALF:]
    turned, turned_second = roll_half(first), roll_half(second)
    lane = lanes_of(first.shape)
    return jnp.concatenate(
        [jnp.where(lane < 64, turned, turned_second), jnp.where(lane < 64, turned_second, halo)], axis=1
    )


def operate(centre, x_pair, y_pair, along, ahead_x, ahead_y):
    along_x, along_y, along_z = along
    plane = lanes_of(centre.shape) % NZ
    first, last = plane == 0, plane == NZ - 1
    ahead_z = jnp.where(last, pltpu.roll(along_z, NZ - 1, 1), pltpu.roll(along_z, PLANE - 1, 1))
    behind_z = jnp.where(first, 0.0, pltpu.roll(centre, 1, 1))
    before_z = jnp.where(last, 0.0, pltpu.roll(centre, PLANE - 1, 1))
    result_x = along_x * (centre - x_pair[0]) + ahead_x * (centre - x_pair[1])
    result_y = along_y * (centre - y_pair[0]) + ahead_y * (centre - y_pair[1])
    result_z = along_z * (centre - behind_z) + ahead_z * (centre - before_z)
    return result_x + result_y + result_z


def turned(ref, lead=()):
    rows = [ref[lead + (slice(None), y, slice(None))] for y in range(ROWS)]
    return jnp.concatenate(rows, axis=0).T


def y_neighbours(field, along_y, under, over, cond_over):
    under = jnp.concatenate([under, roll_half(under)], axis=0)
    over = jnp.concatenate([roll_half(over), over], axis=0)
    cond_over = jnp.concatenate([roll_half(cond_over), cond_over], axis=0)
    row = lax.axis_index("gy")
    under = jnp.where(row == 0, 0.0, under)
    over = jnp.where(row == lax.axis_size("gy") - 1, 0.0, over)
    pair = (behind_rows(field, under), before_rows(field, over))
    return pair, before_rows(along_y, cond_over)


def from_below(axis, first, second):
    return jnp.where(lax.axis_index(axis) % 2 == 1, first, second)


def entry_kernel(
    start_hbm,
    cond_hbm,
    field_ref,
    along_ref,
    x_first_ref,
    x_second_ref,
    y_first_ref,
    y_second_ref,
    start_ref,
    cond_ref,
    semaphores,
):
    copies = [pltpu.make_async_copy(start_hbm, start_ref, semaphores.at[0])]
    copies += [pltpu.make_async_copy(cond_hbm.at[i], cond_ref.at[i], semaphores.at[1 + i]) for i in range(2)]
    for copy in copies:
        copy.start()
    copies[0].wait()
    field = turned(start_ref)
    field_ref[...] = field
    high, low = high_row_packed(field), low_row_packed(field)
    for axis in range(2):
        copies[1 + axis].wait()
        along = turned(cond_ref, (axis,))
        if axis == 0:
            left = jnp.concatenate([field[0:1], along[0:1]], axis=0)
            right = jnp.concatenate([field[CELLS - 1 :], along[0:1]], axis=0)
            x_first_ref[0:2] = from_below("gx", left, right)
            x_second_ref[0:2] = from_below("gx", right, left)
        else:
            along_low = low_row_packed(along)
            y_first_ref[:HALF] = from_below("gy", low, high)
            y_second_ref[:HALF] = from_below("gy", high, low)
            y_first_ref[HALF:] = along_low
            y_second_ref[HALF:] = along_low
        along_ref[:, COLS * axis : COLS * (axis + 1), :] = along.reshape(GROUP, COLS, PLANE)


def side_kernel(order_ref, cond_hbm, right_hbm, turns_hbm, column_hbm, edge_hbm, *refs):
    along_out, right_out, high_ref, low_ref, edge_high_ref, edge_low_ref = refs[:6]
    cond_ref, rhs_ref, turns_ref, column_ref, edge_ref, semaphores = refs[6:]
    sources = (cond_hbm.at[2], right_hbm, turns_hbm.at[lax.axis_index("gx")], column_hbm, edge_hbm)
    targets = (cond_ref, rhs_ref, turns_ref, column_ref, edge_ref)
    copies = [pltpu.make_async_copy(*pair, semaphores.at[i]) for i, pair in enumerate(zip(sources, targets))]
    for copy in copies:
        copy.start()
    copies[0].wait()
    along_out[...] = turned(cond_ref).reshape(GROUP, COLS, PLANE)
    copies[1].wait()
    right_out[...] = turned(rhs_ref)
    copies[2].wait()
    turns = turns_ref[...].T
    copies[3].wait()
    table = column_ref[...]
    blocks = table.reshape(GROUP, 2 * COLS, CELLS)
    other = jnp.concatenate([blocks[:, COLS:], -blocks[:, :COLS]], axis=1).reshape(2 * CELLS, CELLS)
    high_ref[...], low_ref[...] = split(table * turns[:, 0:1] + other * turns[:, 1:2])
    copies[4].wait()
    table = edge_ref[...]
    part = lax.broadcasted_iota(jnp.int32, (CELLS, HALF), 0) % 2
    other = jnp.where(part == 0, pltpu.roll(table, CELLS - 1, 0), -pltpu.roll(table, 1, 0))
    edge_high_ref[...], edge_low_ref[...] = split(table * turns[:CELLS, 2:3] + other * turns[:CELLS, 3:4])


def residual_kernel(
    rhs_ref, field_ref, along_ref, along_z_ref, x_first_ref, x_second_ref, y_first_ref, y_second_ref, *outs
):
    out_ref, residual_ref = outs
    x_swaps, y_swaps = (x_first_ref[...], x_second_ref[...]), (y_first_ref[...], y_second_ref[...])
    left, after = from_below("gx", *x_swaps), from_below("gx", *x_swaps[::-1])
    under, over = from_below("gy", *y_swaps), from_below("gy", *y_swaps[::-1])
    field = field_ref[...]
    along = [along_ref[:, COLS * axis : COLS * (axis + 1), :].reshape(CELLS, PLANE) for axis in range(2)]
    along += [along_z_ref[...].reshape(CELLS, PLANE)]
    row = lax.broadcasted_iota(jnp.int32, (CELLS, PLANE), 0)
    behind_x = jnp.where(row == 0, left[0:1], pltpu.roll(field, 1, 0))
    before_x = jnp.where(row == CELLS - 1, after[0:1], pltpu.roll(field, CELLS - 1, 0))
    ahead_x = jnp.where(row == CELLS - 1, after[1:2], pltpu.roll(along[0], CELLS - 1, 0))
    y_pair, ahead_y = y_neighbours(
        field, along[1], under[:HALF], over[:HALF], over[HALF:]
    )
    image = operate(field, (behind_x, before_x), y_pair, along, ahead_x, ahead_y)
    residual = rhs_ref[...] - image
    residual_ref[...] = residual
    out_ref[:, 0 : 2 * COLS, :] = along_ref[...]
    out_ref[:, 2 * COLS : 3 * COLS, :] = along_z_ref[...]
    out_ref[:, 3 * COLS :, :] = residual.reshape(GROUP, COLS, PLANE)


def coefficients(chunk_ref):
    return [chunk_ref[:, COLS * axis : COLS * (axis + 1), :].reshape(CELLS, PLANE) for axis in range(3)]


def spread_kernel(field_ref, high_ref, low_ref, out_ref):
    field = field_ref[:, 3 * COLS :, :].reshape(CELLS, PLANE)
    table = (high_ref[...], low_ref[...])
    out_ref[...] = products(table, split(field), ((1,), (0,))).reshape(GROUP, 2 * COLS, PLANE)


def first_solve_kernel(parts_ref, inverse_ref, high_ref, low_ref, out_ref, sums_ref, wave, solved, back):
    solve(0, parts_ref, inverse_ref, high_ref, low_ref, None, out_ref, sums_ref, wave, solved, back)


def second_solve_kernel(parts_ref, inverse_ref, high_ref, low_ref, dots_ref, out_ref, wave, solved, sums_ref):
    solve(2, parts_ref, inverse_ref, high_ref, low_ref, dots_ref, out_ref, sums_ref, wave, solved, None)


def solve(which, parts_ref, inverse_ref, high_ref, low_ref, dots_ref, out_ref, sums_ref, wave, solved, back):
    table = (high_ref[...], low_ref[...])
    parts = parts_ref[...].reshape(2 * CELLS, PLANE).T
    wave[...] = products(split(parts), table, ((1,), (0,)))
    total = jnp.zeros((8, HALF), f32)
    for half in range(2):
        for pair in range(2):
            places = [(2 * pair + y, part * CELLS + half * HALF) for y in range(2) for part in range(2)]

            def step(group, sums):
                tiles = [
                    wave[pl.ds(pl.multiple_of(y * NZ + group * 8, 8), 8), lane : lane + HALF] for y, lane in places
                ]
                for z in range(8):
                    block = inverse_ref[group * 8 + z, :, half * HALF : (half + 1) * HALF]
                    sums = tuple(so_far + block * tile[z : z + 1] for so_far, tile in zip(sums, tiles))
                return sums

            sums = tuple(jnp.zeros((NZ, HALF), f32) for _ in places)
            sums = lax.fori_loop(0, NZ // 8, step, sums)
            for result, (y, lane) in zip(sums, places):
                solved[y * NZ : (y + 1) * NZ, lane : lane + HALF] = result
                product = result * wave[y * NZ : (y + 1) * NZ, lane : lane + HALF]
                total = total + jnp.sum(product.reshape(NZ // 8, 8, HALF), axis=0)
    row = lax.broadcasted_iota(jnp.int32, (8, HALF), 0)
    total = jnp.sum(total, axis=0, keepdims=True) / LENGTH
    others = 0.0 if dots_ref is None else dots_ref[...]
    sums_ref[...] = jnp.where(row == which, total, others)
    parts = products(table, split(solved[...]), ((1,), (1,))).reshape(GROUP, 2 * COLS, PLANE)
    for half in range(2):
        out_ref[:, 16 * half : 16 * (half + 1), :] = parts[:, :, half * HALF : (half + 1) * HALF]
    if which == 0:
        back[...] = parts
        for side, (column, step) in enumerate(((COLS - 1, 1), (0, GROUP - 1))):
            for part in range(2):
                rows = pltpu.roll(back[:, part * COLS + column, :], step, 0)
                for half in range(2):
                    out_ref[:, 32 + 4 * half + 2 * side + part, :] = rows[:, half * HALF : (half + 1) * HALF]
    else:
        out_ref[:, 32:40, :] = jnp.broadcast_to(sums_ref[...][None], (GROUP, 8, HALF))


def gather_field(parts_ref, high_ref, low_ref):
    parts = jnp.concatenate(
        [parts_ref[:, 16 * half : 16 * (half + 1), :].reshape(2 * CELLS, HALF) for half in range(2)], axis=1
    )
    table = (high_ref[...], low_ref[...])
    return products(table, split(parts), ((0,), (0,))) * (1.0 / LENGTH)


def gather_kernel(
    parts_ref, high_ref, low_ref, edge_high_ref, edge_low_ref, field_ref, left_ref, next_ref, row_low_ref, row_high_ref
):
    field = gather_field(parts_ref, high_ref, low_ref)
    field_ref[...] = field
    row_low_ref[...] = low_row_packed(field)
    row_high_ref[...] = high_row_packed(field)
    beside = parts_ref[:, 32:40, :].reshape(CELLS, HALF)
    edges = products((edge_high_ref[...], edge_low_ref[...]), split(beside), ((0,), (0,))) * (1.0 / LENGTH)
    left_ref[...] = jnp.concatenate([edges[0:32], edges[64:96]], axis=1)
    next_ref[...] = jnp.concatenate([edges[32:64], edges[96:128]], axis=1)


def edge_rows(edge):
    return jnp.broadcast_to(edge[:, None, :], (GROUP, COLS, PLANE)).reshape(CELLS, PLANE)


def image_kernel(
    field_ref,
    chunk_ref,
    left_ref,
    next_ref,
    under_ref,
    over_ref,
    cond_next_ref,
    cond_over_ref,
    dots_ref,
    high_ref,
    low_ref,
    image_ref,
    parts_ref,
    sums_ref,
):
    field = field_ref[...]
    along = coefficients(chunk_ref)
    column = lax.broadcasted_iota(jnp.int32, (CELLS, PLANE), 0) % COLS
    cond_after = cond_next_ref[...]
    at_end = lax.axis_index("gx") == lax.axis_size("gx") - 1
    cond_after = jnp.where(at_end, pltpu.roll(cond_after, GROUP - 1, 0), cond_after)
    behind_x = jnp.where(column == 0, edge_rows(left_ref[...]), pltpu.roll(field, 1, 0))
    before_x = jnp.where(column == COLS - 1, edge_rows(next_ref[...]), pltpu.roll(field, CELLS - 1, 0))
    ahead_x = jnp.where(column == COLS - 1, edge_rows(cond_after), pltpu.roll(along[0], CELLS - 1, 0))
    y_pair, ahead_y = y_neighbours(field, along[1], under_ref[...], over_ref[...], cond_over_ref[...])
    image = operate(field, (behind_x, before_x), y_pair, along, ahead_x, ahead_y)
    image_ref[...] = image
    table = (high_ref[...], low_ref[...])
    parts_ref[...] = products(table, split(image), ((1,), (0,))).reshape(GROUP, 2 * COLS, PLANE)
    product = field * image
    total = jnp.sum((product[:, :HALF] + product[:, HALF:]), axis=0, keepdims=True)
    row = lax.broadcasted_iota(jnp.int32, (8, HALF), 0)
    sums_ref[...] = dots_ref[...] + jnp.where(row == 1, total, 0.0)


def edges_kernel(chunk_ref, edge_ref, row_ref):
    edge_ref[...] = chunk_ref[:, 0, :]
    row_ref[...] = low_row_packed(chunk_ref[:, COLS : 2 * COLS, :].reshape(CELLS, PLANE))


def pack_kernel(parts_ref, high_ref, low_ref, field_ref, image_ref, out_ref, sums_ref):
    out_ref[:, 0:COLS, :] = field_ref[...].reshape(GROUP, COLS, PLANE)
    out_ref[:, COLS : 2 * COLS, :] = image_ref[...].reshape(GROUP, COLS, PLANE)
    latest = gather_field(parts_ref, high_ref, low_ref)
    out_ref[:, 2 * COLS :, :] = latest.reshape(GROUP, COLS, PLANE)
    sums_ref[...] = jnp.sum(parts_ref[:, 32:40, :], axis=0)


def finish_kernel(packed_ref, start_ref, residual_ref, dots_ref, pressure_out, residual_out, direction_out):
    sums = jnp.sum(dots_ref[...], axis=1, keepdims=True)
    first, curvature, third = sums[0:1], sums[1:2], sums[2:3]
    step = first / curvature
    second = first - 2.0 * step * curvature + step * step * third
    ratio = second / first
    field = packed_ref[:, 0:COLS, :].reshape(CELLS, PLANE)
    image = packed_ref[:, COLS : 2 * COLS, :].reshape(CELLS, PLANE)
    latest = packed_ref[:, 2 * COLS :, :].reshape(CELLS, PLANE)
    change = (step * field).T
    residual = (residual_ref[...] - step * image).T
    direction = ((field - step * latest) + ratio * field).T
    for y in range(ROWS):
        rows = slice(y * NZ, (y + 1) * NZ)
        pressure_out[:, y, :] = start_ref[:, y, :] + change[rows]
        residual_out[:, y, :] = residual[rows]
        direction_out[:, y, :] = direction[rows]


def shape(*dims, dtype=f32):
    return jax.ShapeDtypeStruct(dims, dtype)


def call(kernel, outs, *args, hbm=(), scratch=(), cost=0):
    specs = [pl.BlockSpec(memory_space=pltpu.VMEM) for _ in args]
    args = list(args)
    for i in hbm:
        specs[i] = pl.BlockSpec(memory_space=pltpu.HBM)
        args[i] = pltpu.with_memory_space_constraint(args[i], pltpu.HBM)
    many = isinstance(outs, (tuple, list))
    out_spec = pl.BlockSpec(memory_space=pltpu.VMEM)
    return pl.pallas_call(
        kernel,
        out_shape=outs,
        in_specs=specs,
        out_specs=[out_spec] * len(outs) if many else out_spec,
        scratch_shapes=list(scratch),
        compiler_params=pltpu.CompilerParams(vmem_limit_bytes=16 * 1024 * 1024),
        cost_estimate=pl.CostEstimate(flops=cost, bytes_accessed=2**20, transcendentals=0),
    )(*args)


def shift(value, axis, step):
    count = lax.axis_size(axis)
    return lax.ppermute(value, axis, [(i, (i + step) % count) for i in range(count)])


def swap(first, second, axis):
    count = lax.axis_size(axis)
    first = lax.ppermute(first, axis, [(i, i ^ 1) for i in range(count)])
    second = lax.ppermute(second, axis, [(i, (i + 2 * (i % 2) - 1) % count) for i in range(count)])
    return [first, second]


def exchange(parts):
    return lax.all_to_all(parts, "gx", 0, 0, tiled=True)


def sum_rows(value):
    count = lax.axis_size("gy")
    for mask in (1, 2, 6):
        value = value + lax.ppermute(value, "gy", [(i, i ^ mask) for i in range(count)])
    return value


def shards(right_side, start_pressure, conductance, inverses):
    field_shape = shape(CELLS, PLANE)
    parts_shape = shape(GROUP, 2 * COLS, PLANE)
    wide_shape = shape(GROUP, 5 * COLS, HALF)
    edge_shape, row_shape, dots_shape = shape(GROUP, PLANE), shape(HALF, HALF), shape(8, HALF)

    cells_shape = shape(NZ, ROWS, CELLS)
    start, along, *swaps = call(
        entry_kernel,
        [
            field_shape,
            shape(GROUP, 2 * COLS, PLANE),
            shape(8, PLANE),
            shape(8, PLANE),
            shape(2 * HALF, HALF),
            shape(2 * HALF, HALF),
        ],
        start_pressure,
        conductance,
        hbm=(0, 1),
        scratch=[
            pltpu.VMEM((NZ, ROWS, CELLS), f32),
            pltpu.VMEM((2, NZ, ROWS, CELLS), f32),
            pltpu.SemaphoreType.DMA((3,)),
        ],
    )
    halos = swap(swaps[0], swaps[1], "gx") + swap(swaps[2], swaps[3], "gy")
    along_z, turned_right, *tables = call(
        side_kernel,
        [shape(GROUP, COLS, PLANE), field_shape]
        + [shape(2 * CELLS, CELLS, dtype=bf16)] * 2
        + [shape(CELLS, HALF, dtype=bf16)] * 2,
        swaps[0],
        conductance,
        right_side,
        jnp.asarray(turn_table()),
        jnp.asarray(column_table()),
        jnp.asarray(edge_table()),
        hbm=(1, 2, 3, 4, 5),
        scratch=[
            pltpu.VMEM((NZ, ROWS, CELLS), f32),
            pltpu.VMEM((NZ, ROWS, CELLS), f32),
            pltpu.VMEM((8, 2 * CELLS), f32),
            pltpu.VMEM((2 * CELLS, CELLS), f32),
            pltpu.VMEM((CELLS, HALF), f32),
            pltpu.SemaphoreType.DMA((5,)),
        ],
    )
    halos, along_z, turned_right, tables = lax.optimization_barrier((halos, along_z, turned_right, tables))
    table, beside_table = tables[:2], tables[2:]
    chunk, residual = call(
        residual_kernel,
        [shape(GROUP, 4 * COLS, PLANE), field_shape],
        turned_right,
        start,
        along,
        along_z,
        *halos,
    )
    chunk = exchange(chunk)
    waves = [jnp.asarray(part) for part in wave_table()]
    inverse = inverses.reshape(inverses.shape[1:])

    parts = exchange(call(spread_kernel, parts_shape, chunk, *table))
    cond_edge, cond_row = call(edges_kernel, [edge_shape, row_shape], chunk)
    cond_after = shift(cond_edge, "gx", -1)
    cond_over = shift(cond_row, "gy", -1)
    wave_shape = pltpu.VMEM((PLANE, 2 * CELLS), f32)
    parts, dots = call(
        first_solve_kernel,
        [wide_shape, dots_shape],
        parts,
        inverse,
        *waves,
        scratch=[wave_shape, wave_shape, pltpu.VMEM((GROUP, 2 * COLS, PLANE), f32)],
        cost=2 * 10**9,
    )
    parts, cond_after, cond_over = lax.optimization_barrier((exchange(parts), cond_after, cond_over))
    field, left, after, row_low, row_high = call(
        gather_kernel,
        [field_shape, edge_shape, edge_shape, row_shape, row_shape],
        parts,
        *table,
        *beside_table,
    )
    under = shift(row_high, "gy", 1)
    over = shift(row_low, "gy", -1)
    image, parts, dots = call(
        image_kernel,
        [field_shape, parts_shape, dots_shape],
        field,
        chunk,
        left,
        after,
        under,
        over,
        cond_after,
        cond_over,
        dots,
        *table,
    )
    parts = call(
        second_solve_kernel,
        wide_shape,
        exchange(parts),
        inverse,
        *waves,
        dots,
        scratch=[wave_shape, wave_shape, pltpu.VMEM((8, HALF), f32)],
        cost=2 * 10**9,
    )
    packed, dots = call(
        pack_kernel, [shape(GROUP, 3 * COLS, PLANE), dots_shape], exchange(parts), *table, field, image
    )
    dots = sum_rows(dots)
    return tuple(call(finish_kernel, [cells_shape] * 3, exchange(packed), start_pressure, residual, dots))


def solution(mesh):
    placed = (
        P(None, "gy", "gx"),
        P(None, "gy", "gx"),
        P(None, None, "gy", "gx"),
        P("gx", None, None, None),
    )
    return jax.shard_map(
        shards,
        mesh=mesh,
        in_specs=placed,
        out_specs=(P(None, "gy", "gx"), P(None, "gy", "gx"), P(None, "gy", "gx")),
        check_vma=False,
    )
```

```python
import functools

import jax
import jax.numpy as jnp
import numpy as np
from jax import lax
from jax.experimental import pallas as pl
from jax.experimental.pallas import tpu as pltpu
from jax.sharding import PartitionSpec as P

NZ = 64
ROWS = 4
CELLS = 256
GROUP = 32
COLS = 8
LENGTH = CELLS * GROUP
PLANE = ROWS * NZ
HALF = 128

f32 = jnp.float32
bf16 = jnp.bfloat16


def reverse_bits(number):
    return int(f"{number:05b}"[::-1], 2)


def column_table():
    residue = np.array([reverse_bits(i) for i in range(GROUP)])
    angle = 2.0 * np.pi * np.outer(residue, np.arange(GROUP)) / GROUP
    same = np.eye(COLS)

    def table(real_row, imag_row):
        pair = np.stack([real_row, imag_row], axis=1)
        full = pair[:, :, None, :, None] * same[None, None, :, None, :]
        return full.reshape(GROUP * 2 * COLS, CELLS).astype(np.float32)

    return table(np.cos(angle), -np.sin(angle))


def edge_table():
    residue = np.array([reverse_bits(i) for i in range(GROUP)])
    angle = 2.0 * np.pi * np.outer(residue, np.arange(GROUP)) / GROUP
    same = np.eye(4).reshape(2, 2, 2, 2)

    def table(real_row, imag_row):
        pair = np.stack([real_row, imag_row], axis=1)
        full = pair[:, None, None, :, None, None, :] * same[None, :, :, None, :, :, None]
        return full.reshape(GROUP * 8, 4 * GROUP).astype(np.float32)

    return table(np.cos(angle), -np.sin(angle))


def turn_table():
    residue = np.array([reverse_bits(i) for i in range(GROUP)])
    first = COLS * np.arange(GROUP)[:, None]
    own = np.tile(np.arange(COLS), 2)[None, :] + first
    beside = np.tile(np.array([-1, -1, COLS, COLS]), 2)[None, :] + first

    def angles(columns):
        turns = residue[None, :, None] * columns[:, None, :] % LENGTH
        return (2.0 * np.pi / LENGTH) * turns.reshape(GROUP, -1)

    full = np.zeros((GROUP, 8, 2 * CELLS), np.float32)
    for i, angle in enumerate((angles(own), angles(beside))):
        full[:, 2 * i, : angle.shape[1]] = np.cos(angle)
        full[:, 2 * i + 1, : angle.shape[1]] = np.sin(angle)
    return full


def wave_table():
    angle = 2.0 * np.pi * np.outer(np.arange(CELLS), np.arange(CELLS)) / CELLS
    cosine, sine = np.cos(angle), np.sin(angle)
    real_rows = np.concatenate([cosine, -sine], axis=1).reshape(GROUP, 1, COLS, 2 * CELLS)
    imag_rows = np.concatenate([sine, cosine], axis=1).reshape(GROUP, 1, COLS, 2 * CELLS)
    full = np.concatenate([real_rows, imag_rows], axis=1).reshape(2 * CELLS, 2 * CELLS)
    full = full.astype(np.float32)
    high = full.astype(jnp.bfloat16)
    low = (full - high.astype(np.float32)).astype(jnp.bfloat16)
    return high, low


def split(values):
    high = values.astype(bf16)
    return high, (values - high.astype(f32)).astype(bf16)


def products(left, right, contract):
    dims = (contract, ((), ()))
    (left_high, left_low), (right_high, right_low) = left, right

    def one(a, b):
        return lax.dot_general(a, b, dims, preferred_element_type=f32)

    return one(left_high, right_high) + (one(left_high, right_low) + one(left_low, right_high))


def lanes_of(shape):
    return lax.broadcasted_iota(jnp.int32, shape, 1)


def roll_half(tile):
    return pltpu.roll(tile, 64, 1)


def low_row_packed(field):
    tile = field[:, :HALF]
    lane = lanes_of((HALF, HALF))
    return jnp.where(lane < 64, tile[:HALF], roll_half(tile[HALF:]))


def high_row_packed(field):
    tile = field[:, HALF:]
    lane = lanes_of((HALF, HALF))
    return jnp.where(lane < 64, roll_half(tile[:HALF]), tile[HALF:])


def behind_rows(field, halo):
    first, second = field[:, :HALF], field[:, HALF:]
    turned, turned_second = roll_half(first), roll_half(second)
    lane = lanes_of(first.shape)
    return jnp.concatenate(
        [jnp.where(lane < 64, halo, turned), jnp.where(lane < 64, turned, turned_second)], axis=1
    )


def before_rows(field, halo):
    first, second = field[:, :HALF], field[:, HALF:]
    turned, turned_second = roll_half(first), roll_half(second)
    lane = lanes_of(first.shape)
    return jnp.concatenate(
        [jnp.where(lane < 64, turned, turned_second), jnp.where(lane < 64, turned_second, halo)], axis=1
    )


def operate(centre, x_pair, y_pair, along, ahead_x, ahead_y):
    along_x, along_y, along_z = along
    plane = lanes_of(centre.shape) % NZ
    first, last = plane == 0, plane == NZ - 1
    ahead_z = jnp.where(last, pltpu.roll(along_z, NZ - 1, 1), pltpu.roll(along_z, PLANE - 1, 1))
    behind_z = jnp.where(first, 0.0, pltpu.roll(centre, 1, 1))
    before_z = jnp.where(last, 0.0, pltpu.roll(centre, PLANE - 1, 1))
    result_x = along_x * (centre - x_pair[0]) + ahead_x * (centre - x_pair[1])
    result_y = along_y * (centre - y_pair[0]) + ahead_y * (centre - y_pair[1])
    result_z = along_z * (centre - behind_z) + ahead_z * (centre - before_z)
    return result_x + result_y + result_z


def turned(ref, lead=()):
    rows = [ref[lead + (slice(None), y, slice(None))] for y in range(ROWS)]
    return jnp.concatenate(rows, axis=0).T


def y_neighbours(field, along_y, under, over, cond_over):
    under = jnp.concatenate([under, roll_half(under)], axis=0)
    over = jnp.concatenate([roll_half(over), over], axis=0)
    cond_over = jnp.concatenate([roll_half(cond_over), cond_over], axis=0)
    row = lax.axis_index("gy")
    under = jnp.where(row == 0, 0.0, under)
    over = jnp.where(row == lax.axis_size("gy") - 1, 0.0, over)
    pair = (behind_rows(field, under), before_rows(field, over))
    return pair, before_rows(along_y, cond_over)


def from_below(axis, first, second):
    return jnp.where(lax.axis_index(axis) % 2 == 1, first, second)


def entry_kernel(
    start_hbm,
    cond_hbm,
    field_ref,
    along_ref,
    x_first_ref,
    x_second_ref,
    y_first_ref,
    y_second_ref,
    start_ref,
    cond_ref,
    semaphores,
):
    copies = [pltpu.make_async_copy(start_hbm, start_ref, semaphores.at[0])]
    copies += [pltpu.make_async_copy(cond_hbm.at[i], cond_ref.at[i], semaphores.at[1 + i]) for i in range(2)]
    for copy in copies:
        copy.start()
    copies[0].wait()
    field = turned(start_ref)
    field_ref[...] = field
    high, low = high_row_packed(field), low_row_packed(field)
    for axis in range(2):
        copies[1 + axis].wait()
        along = turned(cond_ref, (axis,))
        if axis == 0:
            left = jnp.concatenate([field[0:1], along[0:1]], axis=0)
            right = jnp.concatenate([field[CELLS - 1 :], along[0:1]], axis=0)
            x_first_ref[0:2] = from_below("gx", left, right)
            x_second_ref[0:2] = from_below("gx", right, left)
        else:
            along_low = low_row_packed(along)
            y_first_ref[:HALF] = from_below("gy", low, high)
            y_second_ref[:HALF] = from_below("gy", high, low)
            y_first_ref[HALF:] = along_low
            y_second_ref[HALF:] = along_low
        along_ref[:, COLS * axis : COLS * (axis + 1), :] = along.reshape(GROUP, COLS, PLANE)


def side_kernel(order_ref, cond_hbm, right_hbm, turns_hbm, column_hbm, *refs):
    along_out, right_out, high_ref, low_ref, cond_ref, rhs_ref, turns_ref, column_ref, semaphores = refs
    sources = (cond_hbm.at[2], right_hbm, turns_hbm.at[lax.axis_index("gx")], column_hbm)
    targets = (cond_ref, rhs_ref, turns_ref, column_ref)
    copies = [pltpu.make_async_copy(*pair, semaphores.at[i]) for i, pair in enumerate(zip(sources, targets))]
    for copy in copies:
        copy.start()
    copies[0].wait()
    along_out[...] = turned(cond_ref).reshape(GROUP, COLS, PLANE)
    copies[1].wait()
    right_out[...] = turned(rhs_ref)
    copies[2].wait()
    turns = turns_ref[...].T
    copies[3].wait()
    table = column_ref[...]
    blocks = table.reshape(GROUP, 2 * COLS, CELLS)
    other = jnp.concatenate([blocks[:, COLS:], -blocks[:, :COLS]], axis=1).reshape(2 * CELLS, CELLS)
    high_ref[...], low_ref[...] = split(table * turns[:, 0:1] + other * turns[:, 1:2])


def residual_kernel(
    rhs_ref, field_ref, along_ref, along_z_ref, x_first_ref, x_second_ref, y_first_ref, y_second_ref, *outs
):
    out_ref, residual_ref = outs
    x_swaps, y_swaps = (x_first_ref[...], x_second_ref[...]), (y_first_ref[...], y_second_ref[...])
    left, after = from_below("gx", *x_swaps), from_below("gx", *x_swaps[::-1])
    under, over = from_below("gy", *y_swaps), from_below("gy", *y_swaps[::-1])
    field = field_ref[...]
    along = [along_ref[:, COLS * axis : COLS * (axis + 1), :].reshape(CELLS, PLANE) for axis in range(2)]
    along += [along_z_ref[...].reshape(CELLS, PLANE)]
    row = lax.broadcasted_iota(jnp.int32, (CELLS, PLANE), 0)
    behind_x = jnp.where(row == 0, left[0:1], pltpu.roll(field, 1, 0))
    before_x = jnp.where(row == CELLS - 1, after[0:1], pltpu.roll(field, CELLS - 1, 0))
    ahead_x = jnp.where(row == CELLS - 1, after[1:2], pltpu.roll(along[0], CELLS - 1, 0))
    y_pair, ahead_y = y_neighbours(
        field, along[1], under[:HALF], over[:HALF], over[HALF:]
    )
    image = operate(field, (behind_x, before_x), y_pair, along, ahead_x, ahead_y)
    residual = rhs_ref[...] - image
    residual_ref[...] = residual
    out_ref[:, 0 : 2 * COLS, :] = along_ref[...]
    out_ref[:, 2 * COLS : 3 * COLS, :] = along_z_ref[...]
    out_ref[:, 3 * COLS :, :] = residual.reshape(GROUP, COLS, PLANE)


def coefficients(chunk_ref):
    return [chunk_ref[:, COLS * axis : COLS * (axis + 1), :].reshape(CELLS, PLANE) for axis in range(3)]


def spread_kernel(field_ref, high_ref, low_ref, out_ref):
    field = field_ref[:, 3 * COLS :, :].reshape(CELLS, PLANE)
    table = (high_ref[...], low_ref[...])
    out_ref[...] = products(table, split(field), ((1,), (0,))).reshape(GROUP, 2 * COLS, PLANE)


def first_solve_kernel(parts_ref, inverse_ref, high_ref, low_ref, out_ref, sums_ref, wave, solved, back):
    solve(0, parts_ref, inverse_ref, high_ref, low_ref, None, out_ref, sums_ref, wave, solved, back)


def second_solve_kernel(parts_ref, inverse_ref, high_ref, low_ref, dots_ref, out_ref, wave, solved, sums_ref):
    solve(2, parts_ref, inverse_ref, high_ref, low_ref, dots_ref, out_ref, sums_ref, wave, solved, None)


def solve(which, parts_ref, inverse_ref, high_ref, low_ref, dots_ref, out_ref, sums_ref, wave, solved, back):
    table = (high_ref[...], low_ref[...])
    parts = parts_ref[...].reshape(2 * CELLS, PLANE).T
    wave[...] = products(split(parts), table, ((1,), (0,)))
    total = jnp.zeros((8, HALF), f32)
    for half in range(2):
        for pair in range(2):
            places = [(2 * pair + y, part * CELLS + half * HALF) for y in range(2) for part in range(2)]

            def step(group, sums):
                tiles = [
                    wave[pl.ds(pl.multiple_of(y * NZ + group * 8, 8), 8), lane : lane + HALF] for y, lane in places
                ]
                for z in range(8):
                    block = inverse_ref[group * 8 + z, :, half * HALF : (half + 1) * HALF]
                    sums = tuple(so_far + block * tile[z : z + 1] for so_far, tile in zip(sums, tiles))
                return sums

            sums = tuple(jnp.zeros((NZ, HALF), f32) for _ in places)
            sums = lax.fori_loop(0, NZ // 8, step, sums)
            for result, (y, lane) in zip(sums, places):
                solved[y * NZ : (y + 1) * NZ, lane : lane + HALF] = result
                product = result * wave[y * NZ : (y + 1) * NZ, lane : lane + HALF]
                total = total + jnp.sum(product.reshape(NZ // 8, 8, HALF), axis=0)
    row = lax.broadcasted_iota(jnp.int32, (8, HALF), 0)
    total = jnp.sum(total, axis=0, keepdims=True) / LENGTH
    others = 0.0 if dots_ref is None else dots_ref[...]
    sums_ref[...] = jnp.where(row == which, total, others)
    parts = products(table, split(solved[...]), ((1,), (1,))).reshape(GROUP, 2 * COLS, PLANE)
    for half in range(2):
        out_ref[:, 16 * half : 16 * (half + 1), :] = parts[:, :, half * HALF : (half + 1) * HALF]
    if which == 0:
        back[...] = parts
        for side, (column, step) in enumerate(((COLS - 1, 1), (0, GROUP - 1))):
            for part in range(2):
                rows = pltpu.roll(back[:, part * COLS + column, :], step, 0)
                for half in range(2):
                    out_ref[:, 32 + 4 * half + 2 * side + part, :] = rows[:, half * HALF : (half + 1) * HALF]
    else:
        out_ref[:, 32:40, :] = jnp.broadcast_to(sums_ref[...][None], (GROUP, 8, HALF))


def gather_field(parts_ref, high_ref, low_ref):
    parts = jnp.concatenate(
        [parts_ref[:, 16 * half : 16 * (half + 1), :].reshape(2 * CELLS, HALF) for half in range(2)], axis=1
    )
    table = (high_ref[...], low_ref[...])
    return products(table, split(parts), ((0,), (0,))) * (1.0 / LENGTH)


def gather_kernel(
    parts_ref, high_ref, low_ref, edge_high_ref, edge_low_ref, field_ref, left_ref, next_ref, row_low_ref, row_high_ref
):
    field = gather_field(parts_ref, high_ref, low_ref)
    field_ref[...] = field
    row_low_ref[...] = low_row_packed(field)
    row_high_ref[...] = high_row_packed(field)
    beside = parts_ref[:, 32:40, :].reshape(CELLS, HALF)
    edges = products((edge_high_ref[...], edge_low_ref[...]), split(beside), ((0,), (0,))) * (1.0 / LENGTH)
    left_ref[...] = jnp.concatenate([edges[0:32], edges[64:96]], axis=1)
    next_ref[...] = jnp.concatenate([edges[32:64], edges[96:128]], axis=1)


def edge_rows(edge):
    return jnp.broadcast_to(edge[:, None, :], (GROUP, COLS, PLANE)).reshape(CELLS, PLANE)


def table_kernel(order_ref, high_hbm, low_hbm, high_ref, low_ref, semaphores):
    pairs = ((high_hbm, high_ref), (low_hbm, low_ref))
    copies = [pltpu.make_async_copy(source, target, semaphores.at[i]) for i, (source, target) in enumerate(pairs)]
    for copy in copies:
        copy.start()
    for copy in copies:
        copy.wait()


def image_kernel(
    field_ref,
    chunk_ref,
    left_ref,
    next_ref,
    under_ref,
    over_ref,
    cond_next_ref,
    cond_over_ref,
    dots_ref,
    high_ref,
    low_ref,
    image_ref,
    parts_ref,
    sums_ref,
):
    field = field_ref[...]
    along = coefficients(chunk_ref)
    column = lax.broadcasted_iota(jnp.int32, (CELLS, PLANE), 0) % COLS
    cond_after = cond_next_ref[...]
    at_end = lax.axis_index("gx") == lax.axis_size("gx") - 1
    cond_after = jnp.where(at_end, pltpu.roll(cond_after, GROUP - 1, 0), cond_after)
    behind_x = jnp.where(column == 0, edge_rows(left_ref[...]), pltpu.roll(field, 1, 0))
    before_x = jnp.where(column == COLS - 1, edge_rows(next_ref[...]), pltpu.roll(field, CELLS - 1, 0))
    ahead_x = jnp.where(column == COLS - 1, edge_rows(cond_after), pltpu.roll(along[0], CELLS - 1, 0))
    y_pair, ahead_y = y_neighbours(field, along[1], under_ref[...], over_ref[...], cond_over_ref[...])
    image = operate(field, (behind_x, before_x), y_pair, along, ahead_x, ahead_y)
    image_ref[...] = image
    table = (high_ref[...], low_ref[...])
    parts_ref[...] = products(table, split(image), ((1,), (0,))).reshape(GROUP, 2 * COLS, PLANE)
    product = field * image
    total = jnp.sum((product[:, :HALF] + product[:, HALF:]), axis=0, keepdims=True)
    row = lax.broadcasted_iota(jnp.int32, (8, HALF), 0)
    sums_ref[...] = dots_ref[...] + jnp.where(row == 1, total, 0.0)


def edges_kernel(
    chunk_ref, turns_hbm, table_hbm, edge_ref, row_ref, high_ref, low_ref, turns_ref, table_ref, semaphores
):
    pairs = ((turns_hbm.at[lax.axis_index("gx")], turns_ref), (table_hbm, table_ref))
    copies = [pltpu.make_async_copy(source, target, semaphores.at[i]) for i, (source, target) in enumerate(pairs)]
    for copy in copies:
        copy.start()
    edge_ref[...] = chunk_ref[:, 0, :]
    row_ref[...] = low_row_packed(chunk_ref[:, COLS : 2 * COLS, :].reshape(CELLS, PLANE))
    for copy in copies:
        copy.wait()
    turns = turns_ref[...].T
    table = table_ref[...]
    part = lax.broadcasted_iota(jnp.int32, (CELLS, HALF), 0) % 2
    other = jnp.where(part == 0, pltpu.roll(table, CELLS - 1, 0), -pltpu.roll(table, 1, 0))
    high_ref[...], low_ref[...] = split(table * turns[:CELLS, 2:3] + other * turns[:CELLS, 3:4])


def pack_kernel(parts_ref, high_ref, low_ref, field_ref, image_ref, out_ref, sums_ref):
    out_ref[:, 0:COLS, :] = field_ref[...].reshape(GROUP, COLS, PLANE)
    out_ref[:, COLS : 2 * COLS, :] = image_ref[...].reshape(GROUP, COLS, PLANE)
    latest = gather_field(parts_ref, high_ref, low_ref)
    out_ref[:, 2 * COLS :, :] = latest.reshape(GROUP, COLS, PLANE)
    sums_ref[...] = jnp.sum(parts_ref[:, 32:40, :], axis=0)


def finish_kernel(packed_ref, start_ref, residual_ref, dots_ref, pressure_out, residual_out, direction_out):
    sums = jnp.sum(dots_ref[...], axis=1, keepdims=True)
    first, curvature, third = sums[0:1], sums[1:2], sums[2:3]
    step = first / curvature
    second = first - 2.0 * step * curvature + step * step * third
    ratio = second / first
    field = packed_ref[:, 0:COLS, :].reshape(CELLS, PLANE)
    image = packed_ref[:, COLS : 2 * COLS, :].reshape(CELLS, PLANE)
    latest = packed_ref[:, 2 * COLS :, :].reshape(CELLS, PLANE)
    change = (step * field).T
    residual = (residual_ref[...] - step * image).T
    direction = ((field - step * latest) + ratio * field).T
    for y in range(ROWS):
        rows = slice(y * NZ, (y + 1) * NZ)
        pressure_out[:, y, :] = start_ref[:, y, :] + change[rows]
        residual_out[:, y, :] = residual[rows]
        direction_out[:, y, :] = direction[rows]


def shape(*dims, dtype=f32):
    return jax.ShapeDtypeStruct(dims, dtype)


def call(kernel, outs, *args, hbm=(), scratch=(), cost=0):
    specs = [pl.BlockSpec(memory_space=pltpu.VMEM) for _ in args]
    args = list(args)
    for i in hbm:
        specs[i] = pl.BlockSpec(memory_space=pltpu.HBM)
        args[i] = pltpu.with_memory_space_constraint(args[i], pltpu.HBM)
    many = isinstance(outs, (tuple, list))
    out_spec = pl.BlockSpec(memory_space=pltpu.VMEM)
    return pl.pallas_call(
        kernel,
        out_shape=outs,
        in_specs=specs,
        out_specs=[out_spec] * len(outs) if many else out_spec,
        scratch_shapes=list(scratch),
        compiler_params=pltpu.CompilerParams(vmem_limit_bytes=16 * 1024 * 1024),
        cost_estimate=pl.CostEstimate(flops=cost, bytes_accessed=2**20, transcendentals=0),
    )(*args)


def shift(value, axis, step):
    count = lax.axis_size(axis)
    return lax.ppermute(value, axis, [(i, (i + step) % count) for i in range(count)])


def swap(first, second, axis):
    count = lax.axis_size(axis)
    first = lax.ppermute(first, axis, [(i, i ^ 1) for i in range(count)])
    second = lax.ppermute(second, axis, [(i, (i + 2 * (i % 2) - 1) % count) for i in range(count)])
    return [first, second]


def exchange(parts):
    return lax.all_to_all(parts, "gx", 0, 0, tiled=True)


def sum_rows(value):
    count = lax.axis_size("gy")
    for mask in (1, 2, 6):
        value = value + lax.ppermute(value, "gy", [(i, i ^ mask) for i in range(count)])
    return value


def shards(right_side, start_pressure, conductance, inverses):
    field_shape = shape(CELLS, PLANE)
    parts_shape = shape(GROUP, 2 * COLS, PLANE)
    wide_shape = shape(GROUP, 5 * COLS, HALF)
    edge_shape, row_shape, dots_shape = shape(GROUP, PLANE), shape(HALF, HALF), shape(8, HALF)

    cells_shape = shape(NZ, ROWS, CELLS)
    start, along, *swaps = call(
        entry_kernel,
        [
            field_shape,
            shape(GROUP, 2 * COLS, PLANE),
            shape(8, PLANE),
            shape(8, PLANE),
            shape(2 * HALF, HALF),
            shape(2 * HALF, HALF),
        ],
        start_pressure,
        conductance,
        hbm=(0, 1),
        scratch=[
            pltpu.VMEM((NZ, ROWS, CELLS), f32),
            pltpu.VMEM((2, NZ, ROWS, CELLS), f32),
            pltpu.SemaphoreType.DMA((3,)),
        ],
    )
    halos = swap(swaps[0], swaps[1], "gx") + swap(swaps[2], swaps[3], "gy")
    turn_angles = jnp.asarray(turn_table())
    along_z, turned_right, *table = call(
        side_kernel,
        [shape(GROUP, COLS, PLANE), field_shape] + [shape(2 * CELLS, CELLS, dtype=bf16)] * 2,
        swaps[0],
        conductance,
        right_side,
        turn_angles,
        jnp.asarray(column_table()),
        hbm=(1, 2, 3, 4),
        scratch=[
            pltpu.VMEM((NZ, ROWS, CELLS), f32),
            pltpu.VMEM((NZ, ROWS, CELLS), f32),
            pltpu.VMEM((8, 2 * CELLS), f32),
            pltpu.VMEM((2 * CELLS, CELLS), f32),
            pltpu.SemaphoreType.DMA((4,)),
        ],
    )
    halos, along_z, turned_right, table = lax.optimization_barrier((halos, along_z, turned_right, table))
    chunk, residual = call(
        residual_kernel,
        [shape(GROUP, 4 * COLS, PLANE), field_shape],
        turned_right,
        start,
        along,
        along_z,
        *halos,
    )
    chunk = exchange(chunk)
    waves = [jnp.asarray(part) for part in wave_table()]
    inverse = inverses.reshape(inverses.shape[1:])

    parts = exchange(call(spread_kernel, parts_shape, chunk, *table))
    cond_edge, cond_row, *beside_table = call(
        edges_kernel,
        [edge_shape, row_shape] + [shape(CELLS, HALF, dtype=bf16)] * 2,
        chunk,
        turn_angles,
        jnp.asarray(edge_table()),
        hbm=(1, 2),
        scratch=[
            pltpu.VMEM((8, 2 * CELLS), f32),
            pltpu.VMEM((CELLS, HALF), f32),
            pltpu.SemaphoreType.DMA((2,)),
        ],
    )
    cond_after = shift(cond_edge, "gx", -1)
    cond_over = shift(cond_row, "gy", -1)
    wave_shape = pltpu.VMEM((PLANE, 2 * CELLS), f32)
    parts, dots = call(
        first_solve_kernel,
        [wide_shape, dots_shape],
        parts,
        inverse,
        *waves,
        scratch=[wave_shape, wave_shape, pltpu.VMEM((GROUP, 2 * COLS, PLANE), f32)],
        cost=2 * 10**9,
    )
    parts, cond_after, cond_over = lax.optimization_barrier((exchange(parts), cond_after, cond_over))
    field, left, after, row_low, row_high = call(
        gather_kernel,
        [field_shape, edge_shape, edge_shape, row_shape, row_shape],
        parts,
        *table,
        *beside_table,
    )
    under = shift(row_high, "gy", 1)
    over = shift(row_low, "gy", -1)
    tables = call(
        table_kernel,
        [shape(2 * CELLS, 2 * CELLS, dtype=bf16)] * 2,
        row_low,
        *waves,
        hbm=(1, 2),
        scratch=[pltpu.SemaphoreType.DMA((2,))],
    )
    under, over, tables = lax.optimization_barrier((under, over, tables))
    image, parts, dots = call(
        image_kernel,
        [field_shape, parts_shape, dots_shape],
        field,
        chunk,
        left,
        after,
        under,
        over,
        cond_after,
        cond_over,
        dots,
        *table,
    )
    parts = call(
        second_solve_kernel,
        wide_shape,
        exchange(parts),
        inverse,
        *tables,
        dots,
        scratch=[wave_shape, wave_shape, pltpu.VMEM((8, HALF), f32)],
        cost=2 * 10**9,
    )
    packed, dots = call(
        pack_kernel, [shape(GROUP, 3 * COLS, PLANE), dots_shape], exchange(parts), *table, field, image
    )
    dots = sum_rows(dots)
    return tuple(call(finish_kernel, [cells_shape] * 3, exchange(packed), start_pressure, residual, dots))


def solution(mesh):
    placed = (
        P(None, "gy", "gx"),
        P(None, "gy", "gx"),
        P(None, None, "gy", "gx"),
        P("gx", None, None, None),
    )
    return jax.shard_map(
        shards,
        mesh=mesh,
        in_specs=placed,
        out_specs=(P(None, "gy", "gx"), P(None, "gy", "gx"), P(None, "gy", "gx")),
        check_vma=False,
    )
```

```python
import functools

import jax
import jax.numpy as jnp
import numpy as np
from jax import lax
from jax.experimental import pallas as pl
from jax.experimental.pallas import tpu as pltpu
from jax.sharding import PartitionSpec as P

NZ = 64
ROWS = 4
CELLS = 256
GROUP = 32
COLS = 8
LENGTH = CELLS * GROUP
PLANE = ROWS * NZ
HALF = 128

f32 = jnp.float32
bf16 = jnp.bfloat16


def reverse_bits(number):
    return int(f"{number:05b}"[::-1], 2)


def column_table():
    residue = np.array([reverse_bits(i) for i in range(GROUP)])
    angle = 2.0 * np.pi * np.outer(residue, np.arange(GROUP)) / GROUP
    same = np.eye(COLS)

    def table(real_row, imag_row):
        pair = np.stack([real_row, imag_row], axis=1)
        full = pair[:, :, None, :, None] * same[None, None, :, None, :]
        return full.reshape(GROUP * 2 * COLS, CELLS).astype(np.float32)

    return table(np.cos(angle), -np.sin(angle))


def edge_table():
    residue = np.array([reverse_bits(i) for i in range(GROUP)])
    angle = 2.0 * np.pi * np.outer(residue, np.arange(GROUP)) / GROUP
    same = np.eye(4).reshape(2, 2, 2, 2)

    def table(real_row, imag_row):
        pair = np.stack([real_row, imag_row], axis=1)
        full = pair[:, None, None, :, None, None, :] * same[None, :, :, None, :, :, None]
        return full.reshape(GROUP * 8, 4 * GROUP).astype(np.float32)

    return table(np.cos(angle), -np.sin(angle))


def turn_table():
    residue = np.array([reverse_bits(i) for i in range(GROUP)])
    first = COLS * np.arange(GROUP)[:, None]
    own = np.tile(np.arange(COLS), 2)[None, :] + first
    beside = np.tile(np.array([-1, -1, COLS, COLS]), 2)[None, :] + first

    def angles(columns):
        turns = residue[None, :, None] * columns[:, None, :] % LENGTH
        return (2.0 * np.pi / LENGTH) * turns.reshape(GROUP, -1)

    full = np.zeros((GROUP, 8, 2 * CELLS), np.float32)
    for i, angle in enumerate((angles(own), angles(beside))):
        full[:, 2 * i, : angle.shape[1]] = np.cos(angle)
        full[:, 2 * i + 1, : angle.shape[1]] = np.sin(angle)
    return full


def wave_table():
    angle = 2.0 * np.pi * np.outer(np.arange(CELLS), np.arange(CELLS)) / CELLS
    cosine, sine = np.cos(angle), np.sin(angle)
    real_rows = np.concatenate([cosine, -sine], axis=1).reshape(GROUP, 1, COLS, 2 * CELLS)
    imag_rows = np.concatenate([sine, cosine], axis=1).reshape(GROUP, 1, COLS, 2 * CELLS)
    full = np.concatenate([real_rows, imag_rows], axis=1).reshape(2 * CELLS, 2 * CELLS)
    full = full.astype(np.float32)
    high = full.astype(jnp.bfloat16)
    low = (full - high.astype(np.float32)).astype(jnp.bfloat16)
    return high, low


def split(values):
    high = values.astype(bf16)
    return high, (values - high.astype(f32)).astype(bf16)


def products(left, right, contract):
    dims = (contract, ((), ()))
    (left_high, left_low), (right_high, right_low) = left, right

    def one(a, b):
        return lax.dot_general(a, b, dims, preferred_element_type=f32)

    return one(left_high, right_high) + (one(left_high, right_low) + one(left_low, right_high))


def lanes_of(shape):
    return lax.broadcasted_iota(jnp.int32, shape, 1)


def roll_half(tile):
    return pltpu.roll(tile, 64, 1)


def low_row_packed(field):
    tile = field[:, :HALF]
    lane = lanes_of((HALF, HALF))
    return jnp.where(lane < 64, tile[:HALF], roll_half(tile[HALF:]))


def high_row_packed(field):
    tile = field[:, HALF:]
    lane = lanes_of((HALF, HALF))
    return jnp.where(lane < 64, roll_half(tile[:HALF]), tile[HALF:])


def behind_rows(field, halo):
    first, second = field[:, :HALF], field[:, HALF:]
    turned, turned_second = roll_half(first), roll_half(second)
    lane = lanes_of(first.shape)
    return jnp.concatenate(
        [jnp.where(lane < 64, halo, turned), jnp.where(lane < 64, turned, turned_second)], axis=1
    )


def before_rows(field, halo):
    first, second = field[:, :HALF], field[:, HALF:]
    turned, turned_second = roll_half(first), roll_half(second)
    lane = lanes_of(first.shape)
    return jnp.concatenate(
        [jnp.where(lane < 64, turned, turned_second), jnp.where(lane < 64, turned_second, halo)], axis=1
    )


def operate(centre, x_pair, y_pair, along, ahead_x, ahead_y):
    along_x, along_y, along_z = along
    plane = lanes_of(centre.shape) % NZ
    first, last = plane == 0, plane == NZ - 1
    ahead_z = jnp.where(last, pltpu.roll(along_z, NZ - 1, 1), pltpu.roll(along_z, PLANE - 1, 1))
    behind_z = jnp.where(first, 0.0, pltpu.roll(centre, 1, 1))
    before_z = jnp.where(last, 0.0, pltpu.roll(centre, PLANE - 1, 1))
    result_x = along_x * (centre - x_pair[0]) + ahead_x * (centre - x_pair[1])
    result_y = along_y * (centre - y_pair[0]) + ahead_y * (centre - y_pair[1])
    result_z = along_z * (centre - behind_z) + ahead_z * (centre - before_z)
    return result_x + result_y + result_z


def turned(ref, lead=()):
    rows = [ref[lead + (slice(None), y, slice(None))] for y in range(ROWS)]
    return jnp.concatenate(rows, axis=0).T


def y_neighbours(field, along_y, under, over, cond_over):
    under = jnp.concatenate([under, roll_half(under)], axis=0)
    over = jnp.concatenate([roll_half(over), over], axis=0)
    cond_over = jnp.concatenate([roll_half(cond_over), cond_over], axis=0)
    row = lax.axis_index("gy")
    under = jnp.where(row == 0, 0.0, under)
    over = jnp.where(row == lax.axis_size("gy") - 1, 0.0, over)
    pair = (behind_rows(field, under), before_rows(field, over))
    return pair, before_rows(along_y, cond_over)


def from_below(axis, first, second):
    return jnp.where(lax.axis_index(axis) % 2 == 1, first, second)


def entry_kernel(
    start_hbm,
    cond_hbm,
    field_ref,
    x_first_ref,
    x_second_ref,
    y_first_ref,
    y_second_ref,
    start_ref,
    cond_ref,
    semaphores,
):
    copies = [pltpu.make_async_copy(start_hbm, start_ref, semaphores.at[0])]
    copies += [pltpu.make_async_copy(cond_hbm.at[i], cond_ref.at[i], semaphores.at[1 + i]) for i in range(2)]
    for copy in copies:
        copy.start()
    copies[0].wait()
    field = turned(start_ref)
    field_ref[...] = field
    high, low = high_row_packed(field), low_row_packed(field)
    copies[1].wait()
    column = jnp.concatenate([cond_ref[0, :, y, :HALF] for y in range(ROWS)], axis=0).T[0:1]
    left = jnp.concatenate([field[0:1], column], axis=0)
    right = jnp.concatenate([field[CELLS - 1 :], column], axis=0)
    x_first_ref[0:2] = from_below("gx", left, right)
    x_second_ref[0:2] = from_below("gx", right, left)
    copies[2].wait()
    along_low = jnp.concatenate([cond_ref[1, :, 0, :HALF], cond_ref[1, :, 0, HALF:]], axis=0).T
    y_first_ref[:HALF] = from_below("gy", low, high)
    y_second_ref[:HALF] = from_below("gy", high, low)
    y_first_ref[HALF:] = along_low
    y_second_ref[HALF:] = along_low


def side_kernel(order_ref, cond_hbm, right_hbm, turns_hbm, column_hbm, *refs):
    along_out, right_out, high_ref, low_ref, cond_ref, rhs_ref, turns_ref, column_ref, semaphores = refs
    sources = (cond_hbm, right_hbm, turns_hbm.at[lax.axis_index("gx")], column_hbm)
    targets = (cond_ref, rhs_ref, turns_ref, column_ref)
    copies = [pltpu.make_async_copy(*pair, semaphores.at[i]) for i, pair in enumerate(zip(sources, targets))]
    for copy in copies:
        copy.start()
    copies[0].wait()
    for axis in range(3):
        along_out[:, COLS * axis : COLS * (axis + 1), :] = turned(cond_ref, (axis,)).reshape(GROUP, COLS, PLANE)
    copies[1].wait()
    right_out[...] = turned(rhs_ref)
    copies[2].wait()
    turns = turns_ref[...].T
    copies[3].wait()
    table = column_ref[...]
    blocks = table.reshape(GROUP, 2 * COLS, CELLS)
    other = jnp.concatenate([blocks[:, COLS:], -blocks[:, :COLS]], axis=1).reshape(2 * CELLS, CELLS)
    high_ref[...], low_ref[...] = split(table * turns[:, 0:1] + other * turns[:, 1:2])


def residual_kernel(
    rhs_ref, field_ref, along_ref, x_first_ref, x_second_ref, y_first_ref, y_second_ref, *outs
):
    out_ref, residual_ref = outs
    x_swaps, y_swaps = (x_first_ref[...], x_second_ref[...]), (y_first_ref[...], y_second_ref[...])
    left, after = from_below("gx", *x_swaps), from_below("gx", *x_swaps[::-1])
    under, over = from_below("gy", *y_swaps), from_below("gy", *y_swaps[::-1])
    field = field_ref[...]
    along = coefficients(along_ref)
    row = lax.broadcasted_iota(jnp.int32, (CELLS, PLANE), 0)
    behind_x = jnp.where(row == 0, left[0:1], pltpu.roll(field, 1, 0))
    before_x = jnp.where(row == CELLS - 1, after[0:1], pltpu.roll(field, CELLS - 1, 0))
    ahead_x = jnp.where(row == CELLS - 1, after[1:2], pltpu.roll(along[0], CELLS - 1, 0))
    y_pair, ahead_y = y_neighbours(
        field, along[1], under[:HALF], over[:HALF], over[HALF:]
    )
    image = operate(field, (behind_x, before_x), y_pair, along, ahead_x, ahead_y)
    residual = rhs_ref[...] - image
    residual_ref[...] = residual
    out_ref[:, : 3 * COLS, :] = along_ref[...]
    out_ref[:, 3 * COLS :, :] = residual.reshape(GROUP, COLS, PLANE)


def coefficients(chunk_ref):
    return [chunk_ref[:, COLS * axis : COLS * (axis + 1), :].reshape(CELLS, PLANE) for axis in range(3)]


def spread_kernel(field_ref, high_ref, low_ref, out_ref):
    field = field_ref[:, 3 * COLS :, :].reshape(CELLS, PLANE)
    table = (high_ref[...], low_ref[...])
    out_ref[...] = products(table, split(field), ((1,), (0,))).reshape(GROUP, 2 * COLS, PLANE)


def first_solve_kernel(parts_ref, inverse_ref, high_ref, low_ref, out_ref, sums_ref, wave, solved, back):
    solve(0, parts_ref, inverse_ref, high_ref, low_ref, None, out_ref, sums_ref, wave, solved, back)


def second_solve_kernel(parts_ref, inverse_ref, high_ref, low_ref, dots_ref, out_ref, wave, solved, sums_ref):
    solve(2, parts_ref, inverse_ref, high_ref, low_ref, dots_ref, out_ref, sums_ref, wave, solved, None)


def solve(which, parts_ref, inverse_ref, high_ref, low_ref, dots_ref, out_ref, sums_ref, wave, solved, back):
    table = (high_ref[...], low_ref[...])
    parts = parts_ref[...].reshape(2 * CELLS, PLANE).T
    wave[...] = products(split(parts), table, ((1,), (0,)))
    total = jnp.zeros((8, HALF), f32)
    for half in range(2):
        for pair in range(2):
            places = [(2 * pair + y, part * CELLS + half * HALF) for y in range(2) for part in range(2)]

            def step(group, sums):
                tiles = [
                    wave[pl.ds(pl.multiple_of(y * NZ + group * 8, 8), 8), lane : lane + HALF] for y, lane in places
                ]
                for z in range(8):
                    block = inverse_ref[group * 8 + z, :, half * HALF : (half + 1) * HALF]
                    sums = tuple(so_far + block * tile[z : z + 1] for so_far, tile in zip(sums, tiles))
                return sums

            sums = tuple(jnp.zeros((NZ, HALF), f32) for _ in places)
            sums = lax.fori_loop(0, NZ // 8, step, sums)
            for result, (y, lane) in zip(sums, places):
                solved[y * NZ : (y + 1) * NZ, lane : lane + HALF] = result
                product = result * wave[y * NZ : (y + 1) * NZ, lane : lane + HALF]
                total = total + jnp.sum(product.reshape(NZ // 8, 8, HALF), axis=0)
    row = lax.broadcasted_iota(jnp.int32, (8, HALF), 0)
    total = jnp.sum(total, axis=0, keepdims=True) / LENGTH
    others = 0.0 if dots_ref is None else dots_ref[...]
    sums_ref[...] = jnp.where(row == which, total, others)
    parts = products(table, split(solved[...]), ((1,), (1,))).reshape(GROUP, 2 * COLS, PLANE)
    for half in range(2):
        out_ref[:, 16 * half : 16 * (half + 1), :] = parts[:, :, half * HALF : (half + 1) * HALF]
    if which == 0:
        back[...] = parts
        for side, (column, step) in enumerate(((COLS - 1, 1), (0, GROUP - 1))):
            for part in range(2):
                rows = pltpu.roll(back[:, part * COLS + column, :], step, 0)
                for half in range(2):
                    out_ref[:, 32 + 4 * half + 2 * side + part, :] = rows[:, half * HALF : (half + 1) * HALF]
    else:
        out_ref[:, 32:40, :] = jnp.broadcast_to(sums_ref[...][None], (GROUP, 8, HALF))


def gather_field(parts_ref, high_ref, low_ref):
    parts = jnp.concatenate(
        [parts_ref[:, 16 * half : 16 * (half + 1), :].reshape(2 * CELLS, HALF) for half in range(2)], axis=1
    )
    table = (high_ref[...], low_ref[...])
    return products(table, split(parts), ((0,), (0,))) * (1.0 / LENGTH)


def gather_kernel(
    parts_ref, high_ref, low_ref, edge_high_ref, edge_low_ref, field_ref, left_ref, next_ref, row_low_ref, row_high_ref
):
    field = gather_field(parts_ref, high_ref, low_ref)
    field_ref[...] = field
    row_low_ref[...] = low_row_packed(field)
    row_high_ref[...] = high_row_packed(field)
    beside = parts_ref[:, 32:40, :].reshape(CELLS, HALF)
    edges = products((edge_high_ref[...], edge_low_ref[...]), split(beside), ((0,), (0,))) * (1.0 / LENGTH)
    left_ref[...] = jnp.concatenate([edges[0:32], edges[64:96]], axis=1)
    next_ref[...] = jnp.concatenate([edges[32:64], edges[96:128]], axis=1)


def edge_rows(edge):
    return jnp.broadcast_to(edge[:, None, :], (GROUP, COLS, PLANE)).reshape(CELLS, PLANE)


def table_kernel(order_ref, high_hbm, low_hbm, high_ref, low_ref, semaphores):
    pairs = ((high_hbm, high_ref), (low_hbm, low_ref))
    copies = [pltpu.make_async_copy(source, target, semaphores.at[i]) for i, (source, target) in enumerate(pairs)]
    for copy in copies:
        copy.start()
    for copy in copies:
        copy.wait()


def image_kernel(
    field_ref,
    chunk_ref,
    left_ref,
    next_ref,
    under_ref,
    over_ref,
    cond_next_ref,
    cond_over_ref,
    dots_ref,
    high_ref,
    low_ref,
    image_ref,
    parts_ref,
    sums_ref,
):
    field = field_ref[...]
    along = coefficients(chunk_ref)
    column = lax.broadcasted_iota(jnp.int32, (CELLS, PLANE), 0) % COLS
    cond_after = cond_next_ref[...]
    at_end = lax.axis_index("gx") == lax.axis_size("gx") - 1
    cond_after = jnp.where(at_end, pltpu.roll(cond_after, GROUP - 1, 0), cond_after)
    behind_x = jnp.where(column == 0, edge_rows(left_ref[...]), pltpu.roll(field, 1, 0))
    before_x = jnp.where(column == COLS - 1, edge_rows(next_ref[...]), pltpu.roll(field, CELLS - 1, 0))
    ahead_x = jnp.where(column == COLS - 1, edge_rows(cond_after), pltpu.roll(along[0], CELLS - 1, 0))
    y_pair, ahead_y = y_neighbours(field, along[1], under_ref[...], over_ref[...], cond_over_ref[...])
    image = operate(field, (behind_x, before_x), y_pair, along, ahead_x, ahead_y)
    image_ref[...] = image
    table = (high_ref[...], low_ref[...])
    parts_ref[...] = products(table, split(image), ((1,), (0,))).reshape(GROUP, 2 * COLS, PLANE)
    product = field * image
    total = jnp.sum((product[:, :HALF] + product[:, HALF:]), axis=0, keepdims=True)
    row = lax.broadcasted_iota(jnp.int32, (8, HALF), 0)
    sums_ref[...] = dots_ref[...] + jnp.where(row == 1, total, 0.0)


def edges_kernel(
    chunk_ref, turns_hbm, table_hbm, edge_ref, row_ref, high_ref, low_ref, turns_ref, table_ref, semaphores
):
    pairs = ((turns_hbm.at[lax.axis_index("gx")], turns_ref), (table_hbm, table_ref))
    copies = [pltpu.make_async_copy(source, target, semaphores.at[i]) for i, (source, target) in enumerate(pairs)]
    for copy in copies:
        copy.start()
    edge_ref[...] = chunk_ref[:, 0, :]
    row_ref[...] = low_row_packed(chunk_ref[:, COLS : 2 * COLS, :].reshape(CELLS, PLANE))
    for copy in copies:
        copy.wait()
    turns = turns_ref[...].T
    table = table_ref[...]
    part = lax.broadcasted_iota(jnp.int32, (CELLS, HALF), 0) % 2
    other = jnp.where(part == 0, pltpu.roll(table, CELLS - 1, 0), -pltpu.roll(table, 1, 0))
    high_ref[...], low_ref[...] = split(table * turns[:CELLS, 2:3] + other * turns[:CELLS, 3:4])


def pack_kernel(parts_ref, high_ref, low_ref, field_ref, image_ref, out_ref, sums_ref):
    out_ref[:, 0:COLS, :] = field_ref[...].reshape(GROUP, COLS, PLANE)
    out_ref[:, COLS : 2 * COLS, :] = image_ref[...].reshape(GROUP, COLS, PLANE)
    latest = gather_field(parts_ref, high_ref, low_ref)
    out_ref[:, 2 * COLS :, :] = latest.reshape(GROUP, COLS, PLANE)
    sums_ref[...] = jnp.sum(parts_ref[:, 32:40, :], axis=0)


def finish_kernel(packed_ref, start_ref, residual_ref, dots_ref, pressure_out, residual_out, direction_out):
    sums = jnp.sum(dots_ref[...], axis=1, keepdims=True)
    first, curvature, third = sums[0:1], sums[1:2], sums[2:3]
    step = first / curvature
    second = first - 2.0 * step * curvature + step * step * third
    ratio = second / first
    field = packed_ref[:, 0:COLS, :].reshape(CELLS, PLANE)
    image = packed_ref[:, COLS : 2 * COLS, :].reshape(CELLS, PLANE)
    latest = packed_ref[:, 2 * COLS :, :].reshape(CELLS, PLANE)
    change = (step * field).T
    residual = (residual_ref[...] - step * image).T
    direction = ((field - step * latest) + ratio * field).T
    for y in range(ROWS):
        rows = slice(y * NZ, (y + 1) * NZ)
        pressure_out[:, y, :] = start_ref[:, y, :] + change[rows]
        residual_out[:, y, :] = residual[rows]
        direction_out[:, y, :] = direction[rows]


def shape(*dims, dtype=f32):
    return jax.ShapeDtypeStruct(dims, dtype)


def call(kernel, outs, *args, hbm=(), scratch=(), cost=0):
    specs = [pl.BlockSpec(memory_space=pltpu.VMEM) for _ in args]
    args = list(args)
    for i in hbm:
        specs[i] = pl.BlockSpec(memory_space=pltpu.HBM)
        args[i] = pltpu.with_memory_space_constraint(args[i], pltpu.HBM)
    many = isinstance(outs, (tuple, list))
    out_spec = pl.BlockSpec(memory_space=pltpu.VMEM)
    return pl.pallas_call(
        kernel,
        out_shape=outs,
        in_specs=specs,
        out_specs=[out_spec] * len(outs) if many else out_spec,
        scratch_shapes=list(scratch),
        compiler_params=pltpu.CompilerParams(vmem_limit_bytes=16 * 1024 * 1024),
        cost_estimate=pl.CostEstimate(flops=cost, bytes_accessed=2**20, transcendentals=0),
    )(*args)


def shift(value, axis, step):
    count = lax.axis_size(axis)
    return lax.ppermute(value, axis, [(i, (i + step) % count) for i in range(count)])


def swap(first, second, axis):
    count = lax.axis_size(axis)
    first = lax.ppermute(first, axis, [(i, i ^ 1) for i in range(count)])
    second = lax.ppermute(second, axis, [(i, (i + 2 * (i % 2) - 1) % count) for i in range(count)])
    return [first, second]


def exchange(parts):
    return lax.all_to_all(parts, "gx", 0, 0, tiled=True)


def sum_rows(value):
    count = lax.axis_size("gy")
    for mask in (1, 2, 6):
        value = value + lax.ppermute(value, "gy", [(i, i ^ mask) for i in range(count)])
    return value


def shards(right_side, start_pressure, conductance, inverses):
    field_shape = shape(CELLS, PLANE)
    parts_shape = shape(GROUP, 2 * COLS, PLANE)
    wide_shape = shape(GROUP, 5 * COLS, HALF)
    edge_shape, row_shape, dots_shape = shape(GROUP, PLANE), shape(HALF, HALF), shape(8, HALF)

    cells_shape = shape(NZ, ROWS, CELLS)
    start, *swaps = call(
        entry_kernel,
        [
            field_shape,
            shape(8, PLANE),
            shape(8, PLANE),
            shape(2 * HALF, HALF),
            shape(2 * HALF, HALF),
        ],
        start_pressure,
        conductance,
        hbm=(0, 1),
        scratch=[
            pltpu.VMEM((NZ, ROWS, CELLS), f32),
            pltpu.VMEM((2, NZ, ROWS, CELLS), f32),
            pltpu.SemaphoreType.DMA((3,)),
        ],
    )
    halos = swap(swaps[0], swaps[1], "gx") + swap(swaps[2], swaps[3], "gy")
    turn_angles = jnp.asarray(turn_table())
    along, turned_right, *table = call(
        side_kernel,
        [shape(GROUP, 3 * COLS, PLANE), field_shape] + [shape(2 * CELLS, CELLS, dtype=bf16)] * 2,
        swaps[0],
        conductance,
        right_side,
        turn_angles,
        jnp.asarray(column_table()),
        hbm=(1, 2, 3, 4),
        scratch=[
            pltpu.VMEM((3, NZ, ROWS, CELLS), f32),
            pltpu.VMEM((NZ, ROWS, CELLS), f32),
            pltpu.VMEM((8, 2 * CELLS), f32),
            pltpu.VMEM((2 * CELLS, CELLS), f32),
            pltpu.SemaphoreType.DMA((4,)),
        ],
    )
    halos, along, turned_right, table = lax.optimization_barrier((halos, along, turned_right, table))
    chunk, residual = call(
        residual_kernel,
        [shape(GROUP, 4 * COLS, PLANE), field_shape],
        turned_right,
        start,
        along,
        *halos,
    )
    chunk = exchange(chunk)
    waves = [jnp.asarray(part) for part in wave_table()]
    inverse = inverses.reshape(inverses.shape[1:])

    parts = exchange(call(spread_kernel, parts_shape, chunk, *table))
    cond_edge, cond_row, *beside_table = call(
        edges_kernel,
        [edge_shape, row_shape] + [shape(CELLS, HALF, dtype=bf16)] * 2,
        chunk,
        turn_angles,
        jnp.asarray(edge_table()),
        hbm=(1, 2),
        scratch=[
            pltpu.VMEM((8, 2 * CELLS), f32),
            pltpu.VMEM((CELLS, HALF), f32),
            pltpu.SemaphoreType.DMA((2,)),
        ],
    )
    cond_after = shift(cond_edge, "gx", -1)
    cond_over = shift(cond_row, "gy", -1)
    wave_shape = pltpu.VMEM((PLANE, 2 * CELLS), f32)
    parts, dots = call(
        first_solve_kernel,
        [wide_shape, dots_shape],
        parts,
        inverse,
        *waves,
        scratch=[wave_shape, wave_shape, pltpu.VMEM((GROUP, 2 * COLS, PLANE), f32)],
        cost=2 * 10**9,
    )
    parts, cond_after, cond_over = lax.optimization_barrier((exchange(parts), cond_after, cond_over))
    field, left, after, row_low, row_high = call(
        gather_kernel,
        [field_shape, edge_shape, edge_shape, row_shape, row_shape],
        parts,
        *table,
        *beside_table,
    )
    under = shift(row_high, "gy", 1)
    over = shift(row_low, "gy", -1)
    tables = call(
        table_kernel,
        [shape(2 * CELLS, 2 * CELLS, dtype=bf16)] * 2,
        row_low,
        *waves,
        hbm=(1, 2),
        scratch=[pltpu.SemaphoreType.DMA((2,))],
    )
    under, over, tables = lax.optimization_barrier((under, over, tables))
    image, parts, dots = call(
        image_kernel,
        [field_shape, parts_shape, dots_shape],
        field,
        chunk,
        left,
        after,
        under,
        over,
        cond_after,
        cond_over,
        dots,
        *table,
    )
    parts = call(
        second_solve_kernel,
        wide_shape,
        exchange(parts),
        inverse,
        *tables,
        dots,
        scratch=[wave_shape, wave_shape, pltpu.VMEM((8, HALF), f32)],
        cost=2 * 10**9,
    )
    packed, dots = call(
        pack_kernel, [shape(GROUP, 3 * COLS, PLANE), dots_shape], exchange(parts), *table, field, image
    )
    dots = sum_rows(dots)
    return tuple(call(finish_kernel, [cells_shape] * 3, exchange(packed), start_pressure, residual, dots))


def solution(mesh):
    placed = (
        P(None, "gy", "gx"),
        P(None, "gy", "gx"),
        P(None, None, "gy", "gx"),
        P("gx", None, None, None),
    )
    return jax.shard_map(
        shards,
        mesh=mesh,
        in_specs=placed,
        out_specs=(P(None, "gy", "gx"), P(None, "gy", "gx"), P(None, "gy", "gx")),
        check_vma=False,
    )
```

```python
import functools

import jax
import jax.numpy as jnp
import numpy as np
from jax import lax
from jax.experimental import pallas as pl
from jax.experimental.pallas import tpu as pltpu
from jax.sharding import PartitionSpec as P

NZ = 64
ROWS = 4
CELLS = 256
GROUP = 32
COLS = 8
LENGTH = CELLS * GROUP
PLANE = ROWS * NZ
HALF = 128

f32 = jnp.float32
bf16 = jnp.bfloat16


def reverse_bits(number):
    return int(f"{number:05b}"[::-1], 2)


def column_table():
    residue = np.array([reverse_bits(i) for i in range(GROUP)])
    angle = 2.0 * np.pi * np.outer(residue, np.arange(GROUP)) / GROUP
    same = np.eye(COLS)

    def table(real_row, imag_row):
        pair = np.stack([real_row, imag_row], axis=1)
        full = pair[:, :, None, :, None] * same[None, None, :, None, :]
        return full.reshape(GROUP * 2 * COLS, CELLS).astype(np.float32)

    return table(np.cos(angle), -np.sin(angle))


def edge_table():
    residue = np.array([reverse_bits(i) for i in range(GROUP)])
    angle = 2.0 * np.pi * np.outer(residue, np.arange(GROUP)) / GROUP
    same = np.eye(4).reshape(2, 2, 2, 2)

    def table(real_row, imag_row):
        pair = np.stack([real_row, imag_row], axis=1)
        full = pair[:, None, None, :, None, None, :] * same[None, :, :, None, :, :, None]
        return full.reshape(GROUP * 8, 4 * GROUP).astype(np.float32)

    return table(np.cos(angle), -np.sin(angle))


def turn_table():
    residue = np.array([reverse_bits(i) for i in range(GROUP)])
    first = COLS * np.arange(GROUP)[:, None]
    own = np.tile(np.arange(COLS), 2)[None, :] + first
    beside = np.tile(np.array([-1, -1, COLS, COLS]), 2)[None, :] + first

    def angles(columns):
        turns = residue[None, :, None] * columns[:, None, :] % LENGTH
        return (2.0 * np.pi / LENGTH) * turns.reshape(GROUP, -1)

    full = np.zeros((GROUP, 8, 2 * CELLS), np.float32)
    for i, angle in enumerate((angles(own), angles(beside))):
        full[:, 2 * i, : angle.shape[1]] = np.cos(angle)
        full[:, 2 * i + 1, : angle.shape[1]] = np.sin(angle)
    return full


def wave_table():
    angle = 2.0 * np.pi * np.outer(np.arange(CELLS), np.arange(CELLS)) / CELLS
    cosine, sine = np.cos(angle), np.sin(angle)
    real_rows = np.concatenate([cosine, -sine], axis=1).reshape(GROUP, 1, COLS, 2 * CELLS)
    imag_rows = np.concatenate([sine, cosine], axis=1).reshape(GROUP, 1, COLS, 2 * CELLS)
    full = np.concatenate([real_rows, imag_rows], axis=1).reshape(2 * CELLS, 2 * CELLS)
    full = full.astype(np.float32)
    high = full.astype(jnp.bfloat16)
    low = (full - high.astype(np.float32)).astype(jnp.bfloat16)
    return high, low


def split(values):
    high = values.astype(bf16)
    return high, (values - high.astype(f32)).astype(bf16)


def products(left, right, contract):
    dims = (contract, ((), ()))
    (left_high, left_low), (right_high, right_low) = left, right

    def one(a, b):
        return lax.dot_general(a, b, dims, preferred_element_type=f32)

    return one(left_high, right_high) + (one(left_high, right_low) + one(left_low, right_high))


def lanes_of(shape):
    return lax.broadcasted_iota(jnp.int32, shape, 1)


def roll_half(tile):
    return pltpu.roll(tile, 64, 1)


def low_row_packed(field):
    tile = field[:, :HALF]
    lane = lanes_of((HALF, HALF))
    return jnp.where(lane < 64, tile[:HALF], roll_half(tile[HALF:]))


def high_row_packed(field):
    tile = field[:, HALF:]
    lane = lanes_of((HALF, HALF))
    return jnp.where(lane < 64, roll_half(tile[:HALF]), tile[HALF:])


def behind_rows(field, halo):
    first, second = field[:, :HALF], field[:, HALF:]
    turned, turned_second = roll_half(first), roll_half(second)
    lane = lanes_of(first.shape)
    return jnp.concatenate(
        [jnp.where(lane < 64, halo, turned), jnp.where(lane < 64, turned, turned_second)], axis=1
    )


def before_rows(field, halo):
    first, second = field[:, :HALF], field[:, HALF:]
    turned, turned_second = roll_half(first), roll_half(second)
    lane = lanes_of(first.shape)
    return jnp.concatenate(
        [jnp.where(lane < 64, turned, turned_second), jnp.where(lane < 64, turned_second, halo)], axis=1
    )


def operate(centre, x_pair, y_pair, along, ahead_x, ahead_y):
    along_x, along_y, along_z = along
    plane = lanes_of(centre.shape) % NZ
    first, last = plane == 0, plane == NZ - 1
    ahead_z = jnp.where(last, pltpu.roll(along_z, NZ - 1, 1), pltpu.roll(along_z, PLANE - 1, 1))
    behind_z = jnp.where(first, 0.0, pltpu.roll(centre, 1, 1))
    before_z = jnp.where(last, 0.0, pltpu.roll(centre, PLANE - 1, 1))
    result_x = along_x * (centre - x_pair[0]) + ahead_x * (centre - x_pair[1])
    result_y = along_y * (centre - y_pair[0]) + ahead_y * (centre - y_pair[1])
    result_z = along_z * (centre - behind_z) + ahead_z * (centre - before_z)
    return result_x + result_y + result_z


def turned(ref, lead=()):
    rows = [ref[lead + (slice(None), y, slice(None))] for y in range(ROWS)]
    return jnp.concatenate(rows, axis=0).T


def y_neighbours(field, along_y, under, over, cond_over):
    under = jnp.concatenate([under, roll_half(under)], axis=0)
    over = jnp.concatenate([roll_half(over), over], axis=0)
    cond_over = jnp.concatenate([roll_half(cond_over), cond_over], axis=0)
    row = lax.axis_index("gy")
    under = jnp.where(row == 0, 0.0, under)
    over = jnp.where(row == lax.axis_size("gy") - 1, 0.0, over)
    pair = (behind_rows(field, under), before_rows(field, over))
    return pair, before_rows(along_y, cond_over)


def from_below(axis, first, second):
    return jnp.where(lax.axis_index(axis) % 2 == 1, first, second)


def entry_kernel(
    start_hbm,
    cond_hbm,
    field_ref,
    x_first_ref,
    x_second_ref,
    y_first_ref,
    y_second_ref,
    start_ref,
    cond_ref,
    semaphores,
):
    copies = [pltpu.make_async_copy(start_hbm, start_ref, semaphores.at[0])]
    copies += [pltpu.make_async_copy(cond_hbm.at[i], cond_ref.at[i], semaphores.at[1 + i]) for i in range(2)]
    for copy in copies:
        copy.start()
    copies[0].wait()
    field = turned(start_ref)
    field_ref[...] = field
    high, low = high_row_packed(field), low_row_packed(field)
    copies[1].wait()
    column = jnp.concatenate([cond_ref[0, :, y, :HALF] for y in range(ROWS)], axis=0).T[0:1]
    left = jnp.concatenate([field[0:1], column], axis=0)
    right = jnp.concatenate([field[CELLS - 1 :], column], axis=0)
    x_first_ref[0:2] = from_below("gx", left, right)
    x_second_ref[0:2] = from_below("gx", right, left)
    copies[2].wait()
    along_low = jnp.concatenate([cond_ref[1, :, 0, :HALF], cond_ref[1, :, 0, HALF:]], axis=0).T
    y_first_ref[:HALF] = from_below("gy", low, high)
    y_second_ref[:HALF] = from_below("gy", high, low)
    y_first_ref[HALF:] = along_low
    y_second_ref[HALF:] = along_low


def side_kernel(order_ref, cond_hbm, right_hbm, turns_hbm, column_hbm, *refs):
    along_out, right_out, high_ref, low_ref, cond_ref, rhs_ref, turns_ref, column_ref, semaphores = refs
    sources = (cond_hbm, right_hbm, turns_hbm.at[lax.axis_index("gx")], column_hbm)
    targets = (cond_ref, rhs_ref, turns_ref, column_ref)
    copies = [pltpu.make_async_copy(*pair, semaphores.at[i]) for i, pair in enumerate(zip(sources, targets))]
    for copy in copies:
        copy.start()
    copies[0].wait()
    for axis in range(3):
        along_out[:, COLS * axis : COLS * (axis + 1), :] = turned(cond_ref, (axis,)).reshape(GROUP, COLS, PLANE)
    copies[1].wait()
    right_out[...] = turned(rhs_ref)
    copies[2].wait()
    turns = turns_ref[...].T
    copies[3].wait()
    table = column_ref[...]
    blocks = table.reshape(GROUP, 2 * COLS, CELLS)
    other = jnp.concatenate([blocks[:, COLS:], -blocks[:, :COLS]], axis=1).reshape(2 * CELLS, CELLS)
    high_ref[...], low_ref[...] = split(table * turns[:, 0:1] + other * turns[:, 1:2])


def residual_kernel(
    rhs_ref, field_ref, along_ref, x_first_ref, x_second_ref, y_first_ref, y_second_ref, *outs
):
    out_ref, residual_ref = outs
    x_swaps, y_swaps = (x_first_ref[...], x_second_ref[...]), (y_first_ref[...], y_second_ref[...])
    left, after = from_below("gx", *x_swaps), from_below("gx", *x_swaps[::-1])
    under, over = from_below("gy", *y_swaps), from_below("gy", *y_swaps[::-1])
    field = field_ref[...]
    along = coefficients(along_ref)
    row = lax.broadcasted_iota(jnp.int32, (CELLS, PLANE), 0)
    behind_x = jnp.where(row == 0, left[0:1], pltpu.roll(field, 1, 0))
    before_x = jnp.where(row == CELLS - 1, after[0:1], pltpu.roll(field, CELLS - 1, 0))
    ahead_x = jnp.where(row == CELLS - 1, after[1:2], pltpu.roll(along[0], CELLS - 1, 0))
    y_pair, ahead_y = y_neighbours(
        field, along[1], under[:HALF], over[:HALF], over[HALF:]
    )
    image = operate(field, (behind_x, before_x), y_pair, along, ahead_x, ahead_y)
    residual = rhs_ref[...] - image
    residual_ref[...] = residual
    out_ref[:, : 3 * COLS, :] = along_ref[...]
    out_ref[:, 3 * COLS :, :] = residual.reshape(GROUP, COLS, PLANE)


def coefficients(chunk_ref):
    return [chunk_ref[:, COLS * axis : COLS * (axis + 1), :].reshape(CELLS, PLANE) for axis in range(3)]


def spread_kernel(field_ref, high_ref, low_ref, out_ref):
    field = field_ref[:, 3 * COLS :, :].reshape(CELLS, PLANE)
    table = (high_ref[...], low_ref[...])
    out_ref[...] = products(table, split(field), ((1,), (0,))).reshape(GROUP, 2 * COLS, PLANE)


def first_solve_kernel(
    parts_ref, inverse_ref, high_ref, low_ref, out_hbm, sums_ref, wave, solved, back, out_ref, semaphores
):
    solve(0, (out_hbm, semaphores), parts_ref, inverse_ref, high_ref, low_ref, None, out_ref, sums_ref, wave, solved, back)


def second_solve_kernel(parts_ref, inverse_ref, high_ref, low_ref, dots_ref, out_ref, wave, solved, sums_ref):
    solve(2, None, parts_ref, inverse_ref, high_ref, low_ref, dots_ref, out_ref, sums_ref, wave, solved, None)


def solve(which, target, parts_ref, inverse_ref, high_ref, low_ref, dots_ref, out_ref, sums_ref, wave, solved, back):
    table = (high_ref[...], low_ref[...])
    parts = parts_ref[...].reshape(2 * CELLS, PLANE).T
    wave[...] = products(split(parts), table, ((1,), (0,)))
    total = jnp.zeros((8, HALF), f32)
    for half in range(2):
        for pair in range(2):
            places = [(2 * pair + y, part * CELLS + half * HALF) for y in range(2) for part in range(2)]

            def step(group, sums):
                tiles = [
                    wave[pl.ds(pl.multiple_of(y * NZ + group * 8, 8), 8), lane : lane + HALF] for y, lane in places
                ]
                for z in range(8):
                    block = inverse_ref[group * 8 + z, :, half * HALF : (half + 1) * HALF]
                    sums = tuple(so_far + block * tile[z : z + 1] for so_far, tile in zip(sums, tiles))
                return sums

            sums = tuple(jnp.zeros((NZ, HALF), f32) for _ in places)
            sums = lax.fori_loop(0, NZ // 8, step, sums)
            for result, (y, lane) in zip(sums, places):
                solved[y * NZ : (y + 1) * NZ, lane : lane + HALF] = result
                product = result * wave[y * NZ : (y + 1) * NZ, lane : lane + HALF]
                total = total + jnp.sum(product.reshape(NZ // 8, 8, HALF), axis=0)
    row = lax.broadcasted_iota(jnp.int32, (8, HALF), 0)
    total = jnp.sum(total, axis=0, keepdims=True) / LENGTH
    others = 0.0 if dots_ref is None else dots_ref[...]
    sums_ref[...] = jnp.where(row == which, total, others)
    copies = []
    for half in range(2):
        lanes = slice(half * HALF, (half + 1) * HALF)
        parts = products(table, split(solved[lanes]), ((1,), (1,))).reshape(GROUP, 2 * COLS, HALF)
        rows = pl.ds(16 * half, 16)
        out_ref[:, rows, :] = parts
        if which == 0:
            back[:, :, lanes] = parts
            copies.append(pltpu.make_async_copy(out_ref.at[:, rows], target[0].at[:, rows], target[1].at[half]))
            copies[half].start()
    if which == 0:
        for side, (column, step) in enumerate(((COLS - 1, 1), (0, GROUP - 1))):
            for part in range(2):
                rows = pltpu.roll(back[:, part * COLS + column, :], step, 0)
                for half in range(2):
                    out_ref[:, 32 + 4 * half + 2 * side + part, :] = rows[:, half * HALF : (half + 1) * HALF]
        rows = pl.ds(32, 8)
        copies.append(pltpu.make_async_copy(out_ref.at[:, rows], target[0].at[:, rows], target[1].at[2]))
        copies[2].start()
        for copy in copies:
            copy.wait()
    else:
        out_ref[:, 32:40, :] = jnp.broadcast_to(sums_ref[...][None], (GROUP, 8, HALF))


def gather_field(parts_ref, high_ref, low_ref):
    parts = jnp.concatenate(
        [parts_ref[:, 16 * half : 16 * (half + 1), :].reshape(2 * CELLS, HALF) for half in range(2)], axis=1
    )
    table = (high_ref[...], low_ref[...])
    return products(table, split(parts), ((0,), (0,))) * (1.0 / LENGTH)


def gather_kernel(
    parts_ref, high_ref, low_ref, edge_high_ref, edge_low_ref, field_ref, left_ref, next_ref, row_low_ref, row_high_ref
):
    field = gather_field(parts_ref, high_ref, low_ref)
    field_ref[...] = field
    row_low_ref[...] = low_row_packed(field)
    row_high_ref[...] = high_row_packed(field)
    beside = parts_ref[:, 32:40, :].reshape(CELLS, HALF)
    edges = products((edge_high_ref[...], edge_low_ref[...]), split(beside), ((0,), (0,))) * (1.0 / LENGTH)
    left_ref[...] = jnp.concatenate([edges[0:32], edges[64:96]], axis=1)
    next_ref[...] = jnp.concatenate([edges[32:64], edges[96:128]], axis=1)


def edge_rows(edge):
    return jnp.broadcast_to(edge[:, None, :], (GROUP, COLS, PLANE)).reshape(CELLS, PLANE)


def table_kernel(order_ref, high_hbm, low_hbm, high_ref, low_ref, semaphores):
    pairs = ((high_hbm, high_ref), (low_hbm, low_ref))
    copies = [pltpu.make_async_copy(source, target, semaphores.at[i]) for i, (source, target) in enumerate(pairs)]
    for copy in copies:
        copy.start()
    for copy in copies:
        copy.wait()


def image_kernel(
    field_ref,
    chunk_ref,
    left_ref,
    next_ref,
    under_ref,
    over_ref,
    cond_next_ref,
    cond_over_ref,
    dots_ref,
    high_ref,
    low_ref,
    image_ref,
    parts_ref,
    sums_ref,
):
    field = field_ref[...]
    along = coefficients(chunk_ref)
    column = lax.broadcasted_iota(jnp.int32, (CELLS, PLANE), 0) % COLS
    cond_after = cond_next_ref[...]
    at_end = lax.axis_index("gx") == lax.axis_size("gx") - 1
    cond_after = jnp.where(at_end, pltpu.roll(cond_after, GROUP - 1, 0), cond_after)
    behind_x = jnp.where(column == 0, edge_rows(left_ref[...]), pltpu.roll(field, 1, 0))
    before_x = jnp.where(column == COLS - 1, edge_rows(next_ref[...]), pltpu.roll(field, CELLS - 1, 0))
    ahead_x = jnp.where(column == COLS - 1, edge_rows(cond_after), pltpu.roll(along[0], CELLS - 1, 0))
    y_pair, ahead_y = y_neighbours(field, along[1], under_ref[...], over_ref[...], cond_over_ref[...])
    image = operate(field, (behind_x, before_x), y_pair, along, ahead_x, ahead_y)
    image_ref[...] = image
    table = (high_ref[...], low_ref[...])
    parts_ref[...] = products(table, split(image), ((1,), (0,))).reshape(GROUP, 2 * COLS, PLANE)
    product = field * image
    total = jnp.sum((product[:, :HALF] + product[:, HALF:]), axis=0, keepdims=True)
    row = lax.broadcasted_iota(jnp.int32, (8, HALF), 0)
    sums_ref[...] = dots_ref[...] + jnp.where(row == 1, total, 0.0)


def edges_kernel(
    chunk_ref, turns_hbm, table_hbm, edge_ref, row_ref, high_ref, low_ref, turns_ref, table_ref, semaphores
):
    pairs = ((turns_hbm.at[lax.axis_index("gx")], turns_ref), (table_hbm, table_ref))
    copies = [pltpu.make_async_copy(source, target, semaphores.at[i]) for i, (source, target) in enumerate(pairs)]
    for copy in copies:
        copy.start()
    edge_ref[...] = chunk_ref[:, 0, :]
    row_ref[...] = low_row_packed(chunk_ref[:, COLS : 2 * COLS, :].reshape(CELLS, PLANE))
    for copy in copies:
        copy.wait()
    turns = turns_ref[...].T
    table = table_ref[...]
    part = lax.broadcasted_iota(jnp.int32, (CELLS, HALF), 0) % 2
    other = jnp.where(part == 0, pltpu.roll(table, CELLS - 1, 0), -pltpu.roll(table, 1, 0))
    high_ref[...], low_ref[...] = split(table * turns[:CELLS, 2:3] + other * turns[:CELLS, 3:4])


def pack_kernel(parts_ref, high_ref, low_ref, field_ref, image_ref, out_ref, sums_ref):
    out_ref[:, 0:COLS, :] = field_ref[...].reshape(GROUP, COLS, PLANE)
    out_ref[:, COLS : 2 * COLS, :] = image_ref[...].reshape(GROUP, COLS, PLANE)
    latest = gather_field(parts_ref, high_ref, low_ref)
    out_ref[:, 2 * COLS :, :] = latest.reshape(GROUP, COLS, PLANE)
    sums_ref[...] = jnp.sum(parts_ref[:, 32:40, :], axis=0)


def finish_kernel(packed_ref, start_ref, residual_ref, dots_ref, pressure_out, residual_out, direction_out):
    sums = jnp.sum(dots_ref[...], axis=1, keepdims=True)
    first, curvature, third = sums[0:1], sums[1:2], sums[2:3]
    step = first / curvature
    second = first - 2.0 * step * curvature + step * step * third
    ratio = second / first
    field = packed_ref[:, 0:COLS, :].reshape(CELLS, PLANE)
    image = packed_ref[:, COLS : 2 * COLS, :].reshape(CELLS, PLANE)
    latest = packed_ref[:, 2 * COLS :, :].reshape(CELLS, PLANE)
    change = (step * field).T
    residual = (residual_ref[...] - step * image).T
    direction = ((field - step * latest) + ratio * field).T
    for y in range(ROWS):
        rows = slice(y * NZ, (y + 1) * NZ)
        pressure_out[:, y, :] = start_ref[:, y, :] + change[rows]
        residual_out[:, y, :] = residual[rows]
        direction_out[:, y, :] = direction[rows]


def shape(*dims, dtype=f32):
    return jax.ShapeDtypeStruct(dims, dtype)


def call(kernel, outs, *args, hbm=(), out_hbm=(), scratch=(), cost=0):
    specs = [pl.BlockSpec(memory_space=pltpu.VMEM) for _ in args]
    args = list(args)
    for i in hbm:
        specs[i] = pl.BlockSpec(memory_space=pltpu.HBM)
        args[i] = pltpu.with_memory_space_constraint(args[i], pltpu.HBM)
    many = isinstance(outs, (tuple, list))
    count = len(outs) if many else 1
    out_specs = [pl.BlockSpec(memory_space=pltpu.HBM if i in out_hbm else pltpu.VMEM) for i in range(count)]
    return pl.pallas_call(
        kernel,
        out_shape=outs,
        in_specs=specs,
        out_specs=out_specs if many else out_specs[0],
        scratch_shapes=list(scratch),
        compiler_params=pltpu.CompilerParams(vmem_limit_bytes=16 * 1024 * 1024),
        cost_estimate=pl.CostEstimate(flops=cost, bytes_accessed=2**20, transcendentals=0),
    )(*args)


def shift(value, axis, step):
    count = lax.axis_size(axis)
    return lax.ppermute(value, axis, [(i, (i + step) % count) for i in range(count)])


def swap(first, second, axis):
    count = lax.axis_size(axis)
    first = lax.ppermute(first, axis, [(i, i ^ 1) for i in range(count)])
    second = lax.ppermute(second, axis, [(i, (i + 2 * (i % 2) - 1) % count) for i in range(count)])
    return [first, second]


def exchange(parts):
    return lax.all_to_all(parts, "gx", 0, 0, tiled=True)


def sum_rows(value):
    count = lax.axis_size("gy")
    for mask in (1, 2, 6):
        value = value + lax.ppermute(value, "gy", [(i, i ^ mask) for i in range(count)])
    return value


def shards(right_side, start_pressure, conductance, inverses):
    field_shape = shape(CELLS, PLANE)
    parts_shape = shape(GROUP, 2 * COLS, PLANE)
    wide_shape = shape(GROUP, 5 * COLS, HALF)
    edge_shape, row_shape, dots_shape = shape(GROUP, PLANE), shape(HALF, HALF), shape(8, HALF)

    cells_shape = shape(NZ, ROWS, CELLS)
    start, *swaps = call(
        entry_kernel,
        [
            field_shape,
            shape(8, PLANE),
            shape(8, PLANE),
            shape(2 * HALF, HALF),
            shape(2 * HALF, HALF),
        ],
        start_pressure,
        conductance,
        hbm=(0, 1),
        scratch=[
            pltpu.VMEM((NZ, ROWS, CELLS), f32),
            pltpu.VMEM((2, NZ, ROWS, CELLS), f32),
            pltpu.SemaphoreType.DMA((3,)),
        ],
    )
    halos = swap(swaps[0], swaps[1], "gx") + swap(swaps[2], swaps[3], "gy")
    turn_angles = jnp.asarray(turn_table())
    along, turned_right, *table = call(
        side_kernel,
        [shape(GROUP, 3 * COLS, PLANE), field_shape] + [shape(2 * CELLS, CELLS, dtype=bf16)] * 2,
        swaps[0],
        conductance,
        right_side,
        turn_angles,
        jnp.asarray(column_table()),
        hbm=(1, 2, 3, 4),
        scratch=[
            pltpu.VMEM((3, NZ, ROWS, CELLS), f32),
            pltpu.VMEM((NZ, ROWS, CELLS), f32),
            pltpu.VMEM((8, 2 * CELLS), f32),
            pltpu.VMEM((2 * CELLS, CELLS), f32),
            pltpu.SemaphoreType.DMA((4,)),
        ],
    )
    halos, along, turned_right, table = lax.optimization_barrier((halos, along, turned_right, table))
    chunk, residual = call(
        residual_kernel,
        [shape(GROUP, 4 * COLS, PLANE), field_shape],
        turned_right,
        start,
        along,
        *halos,
    )
    chunk = exchange(chunk)
    waves = [jnp.asarray(part) for part in wave_table()]
    inverse = inverses.reshape(inverses.shape[1:])

    parts = exchange(call(spread_kernel, parts_shape, chunk, *table))
    cond_edge, cond_row, *beside_table = call(
        edges_kernel,
        [edge_shape, row_shape] + [shape(CELLS, HALF, dtype=bf16)] * 2,
        chunk,
        turn_angles,
        jnp.asarray(edge_table()),
        hbm=(1, 2),
        scratch=[
            pltpu.VMEM((8, 2 * CELLS), f32),
            pltpu.VMEM((CELLS, HALF), f32),
            pltpu.SemaphoreType.DMA((2,)),
        ],
    )
    cond_after = shift(cond_edge, "gx", -1)
    cond_over = shift(cond_row, "gy", -1)
    wave_shape = pltpu.VMEM((PLANE, 2 * CELLS), f32)
    parts, dots = call(
        first_solve_kernel,
        [wide_shape, dots_shape],
        parts,
        inverse,
        *waves,
        out_hbm=(0,),
        scratch=[
            wave_shape,
            wave_shape,
            pltpu.VMEM((GROUP, 2 * COLS, PLANE), f32),
            pltpu.VMEM((GROUP, 5 * COLS, HALF), f32),
            pltpu.SemaphoreType.DMA((3,)),
        ],
        cost=2 * 10**9,
    )
    parts, cond_after, cond_over = lax.optimization_barrier((exchange(parts), cond_after, cond_over))
    field, left, after, row_low, row_high = call(
        gather_kernel,
        [field_shape, edge_shape, edge_shape, row_shape, row_shape],
        parts,
        *table,
        *beside_table,
    )
    under = shift(row_high, "gy", 1)
    over = shift(row_low, "gy", -1)
    tables = call(
        table_kernel,
        [shape(2 * CELLS, 2 * CELLS, dtype=bf16)] * 2,
        row_low,
        *waves,
        hbm=(1, 2),
        scratch=[pltpu.SemaphoreType.DMA((2,))],
    )
    under, over, tables = lax.optimization_barrier((under, over, tables))
    image, parts, dots = call(
        image_kernel,
        [field_shape, parts_shape, dots_shape],
        field,
        chunk,
        left,
        after,
        under,
        over,
        cond_after,
        cond_over,
        dots,
        *table,
    )
    parts = call(
        second_solve_kernel,
        wide_shape,
        exchange(parts),
        inverse,
        *tables,
        dots,
        scratch=[wave_shape, wave_shape, pltpu.VMEM((8, HALF), f32)],
        cost=2 * 10**9,
    )
    packed, dots = call(
        pack_kernel, [shape(GROUP, 3 * COLS, PLANE), dots_shape], exchange(parts), *table, field, image
    )
    dots = sum_rows(dots)
    return tuple(call(finish_kernel, [cells_shape] * 3, exchange(packed), start_pressure, residual, dots))


def solution(mesh):
    placed = (
        P(None, "gy", "gx"),
        P(None, "gy", "gx"),
        P(None, None, "gy", "gx"),
        P("gx", None, None, None),
    )
    return jax.shard_map(
        shards,
        mesh=mesh,
        in_specs=placed,
        out_specs=(P(None, "gy", "gx"), P(None, "gy", "gx"), P(None, "gy", "gx")),
        check_vma=False,
    )
```
